32 devices in a mesh: seq: 4 (over y, x), tp: 8 (over z, core).
Axes of the slice: x: 2, y: 2, z: 4, core: 2. Of those that a mesh axis runs over, the one named last changes fastest.
Arguments:
- hidden_in: bfloat16 [1024, 5120], P('seq', 'tp'), may hold values from -16 to 16
- seg_ids: int32 [1024], P('seq'), may hold values from 0 to 3, never falling along the last dimension, each value on 1 to 640 neighbouring positions
- positions: int32 [3, 1024], P(None, 'seq'), may hold values from 0 to 63
- mod_table: float32 [4, 3, 5120], P(None, None, 'tp'), may hold values from -4 to 4
- w_qkv: bfloat16 [5120, 3, 4096], P('seq', None, 'tp')
- q_gain: float32 [4096], P('tp'), may hold values from 0.5 to 3.5
- k_gain: float32 [4096], P('tp'), may hold values from 0.5 to 3.5
- w_out: bfloat16 [4096, 5120], P('tp', 'seq'), may hold values from -0.125 to 0.125
Outputs:
- hidden_out: bfloat16 [1024, 5120], P('seq', 'tp')
- k_cache: bfloat16 [1024, 4096], P('seq', 'tp')
- v_cache: bfloat16 [1024, 4096], P('seq', 'tp')
The draws below stay inside these ranges and needn't reach their ends.
Inputs may be any that keep to these rules, and one draw needn't show every extreme that they name: `seg_ids`: segment ids never fall along the stream; each segment holds 1 to 640 tokens, and one holds exactly 640.
All inputs are finite; a program needn't handle non-finite values.
Results may differ from the reference program's by a relative error of at most 0.018.
Values may be sent and summed in bfloat16 or wider, within the bound.
A program may use at most 64 MiB of HBM per device.

```python
import math
import jax
import jax.numpy as jnp
import numpy as np
from jax import lax

D = 5120
HEADS = 32
HEAD_DIM = 128
SEGS = 4
TOKENS = 1024
HD = 4096
SEG_MAX = 640
N_TP = 8


def draw_hidden_in(key, part):
    first_key = jax.random.fold_in(key, 0)
    third_key = jax.random.fold_in(key, 2)
    column = jnp.arange(D, dtype=jnp.float32) / D
    token_place = jnp.arange(TOKENS, dtype=jnp.float32) / TOKENS
    wave = jnp.cos(2.0 * math.pi * token_place)
    direction = jax.random.normal(third_key, (D,), jnp.float32)
    common = 2.0 * wave[:, None] * direction[None, :]
    base = jax.random.normal(first_key, (TOKENS, D), jnp.float32)
    values = base * jnp.exp(math.log(3.0) * column)[None, :] + common
    return jnp.clip(values, -16.0, 16.0).astype(jnp.bfloat16)


def draw_w_qkv(key, part):
    first_key = jax.random.fold_in(key, 0)
    head_place = (jnp.arange(HEADS * HEAD_DIM) // HEAD_DIM).astype(jnp.float32) / HEADS
    head_scale = jnp.exp(math.log(3.0) * head_place)
    base = jax.random.normal(first_key, (D, 3, HEADS * HEAD_DIM), jnp.float32) / math.sqrt(D)
    return (base * head_scale[None, None, :]).astype(jnp.bfloat16)


def gain_values(key):
    return jnp.exp(jax.random.uniform(key, (HEADS * HEAD_DIM,), jnp.float32, math.log(0.5), math.log(1.5)))


def draw_q_gain(key, part):
    return gain_values(jax.random.fold_in(key, 11))


def draw_k_gain(key, part):
    return gain_values(jax.random.fold_in(key, 23))


def set_ends(result, own_key, least, high):
    dims = result.shape
    place = [jax.random.randint(jax.random.fold_in(own_key, axis), (), 0, dims[axis]) for axis in range(len(dims))]
    result = result.at[tuple(place)].set(least)
    longest = dims.index(max(dims))
    place[longest] = (place[longest] + 1) % dims[longest]
    return result.at[tuple(place)].set(high)


def with_spikes(result, key, source, target, shards_of, factor):
    owner, partner = [(jnp.arange(result.shape[position]) // (result.shape[position] // shards_of)).reshape([-1 if axis == position else 1 for axis in range(result.ndim)]) for position in (source, target)]
    chosen = jax.random.permutation(key, shards_of)[partner]
    strong = (owner == chosen) | (owner == (partner + shards_of // 2) % shards_of)
    return jnp.where(strong, factor * result, result)


def block_scale(stream_key, dims, cuts, low, top_value):
    def one(axis_at, shards_of):
        steps = jax.random.uniform(jax.random.fold_in(jax.random.fold_in(stream_key, 6), axis_at), (shards_of,), jnp.float32, low / len(cuts), top_value / len(cuts))
        return jnp.repeat(jnp.exp(steps), dims[axis_at] // shards_of).reshape((-1,) + (1,) * (len(dims) - axis_at - 1))

    loudness = one(*cuts[0])
    for cut in cuts[1:]:
        loudness = loudness * one(*cut)
    return loudness


def split_up(count, total, bound, slope):
    weights = [(1 << 20) // math.isqrt(rank ** slope) + 1 for rank in range(2, count + 1)]
    spare, holding = total - bound - (count - 1), [1] * (count - 1)
    while spare > 0:
        movable = [i for i in range(count - 1) if holding[i] < bound]
        whole, left = sum([weights[i] for i in movable]), spare
        for i in movable:
            addition = min(bound - holding[i], max(1, left * weights[i] // whole), spare)
            holding[i] = holding[i] + addition
            spare = spare - addition
    return np.array([bound] + holding)


def uneven_parts(stream_key, count, total, most, lean):
    if count == 2:
        one = jax.random.randint(stream_key, (), max(1, total - most), min(most, total - 1) + 1)
        return jnp.stack([one, total - one])
    sizes = jnp.asarray(split_up(count, total, most, lean), jnp.int32)
    pairs = (count - 1) // 2
    source_of, sink = sizes[1:1 + 2 * pairs:2], sizes[2:2 + 2 * pairs:2]
    room = jnp.minimum(source_of - 1, most - sink)
    passed = jax.random.randint(jax.random.fold_in(stream_key, 1), (pairs,), 0, 1 << 20) % (room + 1)
    sizes = sizes.at[1:1 + 2 * pairs:2].set(source_of - passed).at[2:2 + 2 * pairs:2].set(sink + passed)
    return sizes[jax.random.permutation(jax.random.fold_in(stream_key, 2), count)]


def gaussian(stream_key, shape, deviation, most, cuts=(), kind=jnp.bfloat16):
    factor_of = block_scale(stream_key, shape, cuts, -0.22, 0.18) if cuts else 1.0
    values = jax.random.normal(stream_key, shape, jnp.float32) * deviation * factor_of
    return jnp.minimum(jnp.maximum(values, -most), most).astype(kind)


def noise_with(stream_key, dims, width, limit, cuts, heavy, held_as=jnp.bfloat16):
    values = width * jax.random.normal(stream_key, dims, jnp.float32)
    if cuts:
        values = values * block_scale(stream_key, dims, cuts, -0.22, 0.18)
    return jnp.clip(with_spikes(values, jax.random.fold_in(stream_key, 3), *heavy), -limit, limit).astype(held_as)


def setup_inputs(seed: int = 0) -> dict:
    key_of = jax.random.split(jax.random.key(seed), 9)
    return {
        "hidden_in": draw_hidden_in(jax.random.fold_in(key_of[8], 71), 0),
        "seg_ids": jnp.searchsorted(jnp.cumsum(uneven_parts(key_of[1], SEGS, TOKENS, SEG_MAX, 2)), jnp.arange(TOKENS), side="right").astype(jnp.int32),
        "positions": set_ends(jax.random.randint(key_of[2], (3, TOKENS), 0, 64), jax.random.fold_in(key_of[2], 1), 0, 63).astype(jnp.int32),
        "mod_table": gaussian(key_of[3], (SEGS, 3, D), 0.8, 4.0, ((2, 8),), jnp.float32),
        "w_qkv": draw_w_qkv(jax.random.fold_in(key_of[8], 71), 0),
        "q_gain": draw_q_gain(jax.random.fold_in(key_of[8], 71), 0),
        "k_gain": draw_k_gain(jax.random.fold_in(key_of[8], 71), 0),
        "w_out": noise_with(key_of[7], (HD, D), HD ** -0.5, 0.125, ((0, 8), (1, 4)), (0, 1, 8, 2.0)),
    }


EPSILON = 1e-06
NEG_FILL = -1e+30

def rope_tables(positions):
    part_width = HEAD_DIM // 6
    widths = (HEAD_DIM - 4 * part_width, 2 * part_width, 2 * part_width)
    angle_list = []
    for axis_number in range(3):
        exponent = jnp.arange(0, widths[axis_number], 2, dtype=jnp.float32) / widths[axis_number]
        frequency = 1.0 / 10000.0 ** exponent
        angle_list.append(positions[axis_number].astype(jnp.float32)[:, None] * frequency[None, :])
    angle_all = jnp.concatenate(angle_list, axis=1)
    return (jnp.cos(angle_all), jnp.sin(angle_all))

def rotate_pairs(field, cosine, sine):
    even_part = field[..., 0::2]
    odd_part = field[..., 1::2]
    cos_wide = cosine[:, None, :]
    sin_wide = sine[:, None, :]
    new_even = even_part * cos_wide - odd_part * sin_wide
    new_odd = even_part * sin_wide + odd_part * cos_wide
    return jnp.stack([new_even, new_odd], axis=-1).reshape(field.shape)

def reference(hidden_in, seg_ids, positions, mod_table, w_qkv, q_gain, k_gain, w_out):
    token_count = hidden_in.shape[0]
    heads_width = HEADS * HEAD_DIM
    score_scale = 1.0 / math.sqrt(HEAD_DIM)
    x_float = hidden_in.astype(jnp.float32)
    row_sums = lax.optimization_barrier(jnp.sum(x_float, axis=1))
    row_squares = lax.optimization_barrier(jnp.sum(x_float * x_float, axis=1))
    mean_value = row_sums / D
    variance = row_squares / D - mean_value * mean_value
    normed = (x_float - mean_value[:, None]) * lax.rsqrt(variance[:, None] + EPSILON)
    modulation = mod_table[seg_ids]
    shift_mod = modulation[:, 0]
    scale_mod = modulation[:, 1]
    gate_mod = modulation[:, 2]
    modded = (normed * (1.0 + scale_mod) + shift_mod).astype(jnp.bfloat16)
    projected = jnp.dot(modded, w_qkv.reshape(D, 3 * heads_width), preferred_element_type=jnp.float32)
    query_f = projected[:, :heads_width]
    key_f = projected[:, heads_width:2 * heads_width]
    value_f = projected[:, 2 * heads_width:]
    query_n = query_f * lax.rsqrt(lax.optimization_barrier(jnp.mean(query_f * query_f, axis=1, keepdims=True)) + EPSILON) * q_gain[None, :]
    key_n = key_f * lax.rsqrt(lax.optimization_barrier(jnp.mean(key_f * key_f, axis=1, keepdims=True)) + EPSILON) * k_gain[None, :]
    cosine, sine = rope_tables(positions)
    q_rot = rotate_pairs(query_n.reshape(token_count, HEADS, HEAD_DIM), cosine, sine).astype(jnp.bfloat16)
    k_rot = rotate_pairs(key_n.reshape(token_count, HEADS, HEAD_DIM), cosine, sine).astype(jnp.bfloat16)
    v_cache = value_f.astype(jnp.bfloat16)
    v_heads = v_cache.reshape(token_count, HEADS, HEAD_DIM)
    same_seg = seg_ids[:, None] == seg_ids[None, :]

    def one_head(operands):
        q_head, k_head, v_head = operands
        scores = jnp.dot(q_head, k_head.T, preferred_element_type=jnp.float32) * score_scale
        masked = jnp.where(same_seg, scores, NEG_FILL)
        row_max = lax.optimization_barrier(jnp.max(masked, axis=1, keepdims=True))
        weights = jnp.where(same_seg, jnp.exp(masked - row_max), 0.0)
        denominator = lax.optimization_barrier(jnp.sum(weights, axis=1, keepdims=True))
        numerator = jnp.dot(weights.astype(jnp.bfloat16), v_head, preferred_element_type=jnp.float32)
        return numerator / denominator
    attended = lax.map(one_head, (q_rot.transpose(1, 0, 2), k_rot.transpose(1, 0, 2), v_heads.transpose(1, 0, 2)))
    attn_out = attended.transpose(1, 0, 2).reshape(token_count, heads_width).astype(jnp.bfloat16)
    per_device = heads_width // N_TP
    attn_blocks = attn_out.reshape(token_count, N_TP, per_device).transpose(1, 0, 2)
    out_blocks = w_out.reshape(N_TP, per_device, D)

    def add_partial(carry, operands):
        attn_part, weight_part = operands
        term = jnp.dot(attn_part, weight_part, preferred_element_type=jnp.float32).astype(jnp.bfloat16)
        term = lax.optimization_barrier(term)
        return (carry + term.astype(jnp.float32), None)
    mixed = lax.scan(add_partial, jnp.zeros((token_count, D), jnp.float32), (attn_blocks, out_blocks))[0]
    hidden_out = (x_float + gate_mod * mixed).astype(jnp.bfloat16)
    return (hidden_out, k_rot.reshape(token_count, heads_width), v_cache)
```

```python
import functools
import math

import jax
import jax.numpy as jnp
import numpy as np
from jax import lax
from jax.experimental import pallas as pl
from jax.experimental.pallas import tpu as pltpu
from jax.sharding import PartitionSpec as P

HEAD_DIM = 128


EPSILON = 1e-06
NEG_FILL = -1e30


def rope_tables(positions):
    part_width = HEAD_DIM // 6
    widths = (HEAD_DIM - 4 * part_width, 2 * part_width, 2 * part_width)
    angle_list = []
    for axis_number in range(3):
        exponent = jnp.arange(0, widths[axis_number], 2, dtype=jnp.float32) / widths[axis_number]
        frequency = 1.0 / 10000.0**exponent
        angle_list.append(positions[axis_number].astype(jnp.float32)[:, None] * frequency[None, :])
    angle_all = jnp.concatenate(angle_list, axis=1)
    return (jnp.cos(angle_all), jnp.sin(angle_all))


def rotate_pairs(field, cosine, sine):
    even_part = field[..., 0::2]
    odd_part = field[..., 1::2]
    cos_wide = cosine[:, None, :]
    sin_wide = sine[:, None, :]
    new_even = even_part * cos_wide - odd_part * sin_wide
    new_odd = even_part * sin_wide + odd_part * cos_wide
    return jnp.stack([new_even, new_odd], axis=-1).reshape(field.shape)


def empty_state(query_rows, heads_here):
    maxima = jnp.full((heads_here, query_rows), NEG_FILL, jnp.float32)
    totals = jnp.zeros((heads_here, query_rows), jnp.float32)
    weighted = jnp.zeros((heads_here, query_rows, HEAD_DIM), jnp.float32)
    return (maxima, totals, weighted)


def merge_states(first, second):
    largest = jnp.maximum(first[0], second[0])
    first_factor = jnp.exp(first[0] - largest)
    second_factor = jnp.exp(second[0] - largest)
    totals = first[1] * first_factor + second[1] * second_factor
    weighted = first[2] * first_factor[..., None] + second[2] * second_factor[..., None]
    return (largest, totals, weighted)


def block_state(q_heads, seg_q, key_heads, value_heads, seg_k):
    score_scale = 1.0 / math.sqrt(HEAD_DIM)
    scores = (
        jnp.einsum("qhd,khd->hqk", q_heads, key_heads, preferred_element_type=jnp.float32)
        * score_scale
    )
    same_seg = seg_q[:, None] == seg_k[None, :]
    masked = jnp.where(same_seg[None], scores, NEG_FILL)
    maxima = jnp.max(masked, axis=2)
    weights = jnp.where(same_seg[None], jnp.exp(masked - maxima[..., None]), 0.0)
    totals = jnp.sum(weights, axis=2)
    weighted = jnp.einsum(
        "hqk,khd->hqd",
        weights.astype(jnp.bfloat16),
        value_heads,
        preferred_element_type=jnp.float32,
    )
    return (maxima, totals, weighted)


def absorb_keys(carry_state, q_heads, seg_q, key_rows, value_rows, seg_k):
    row_count = key_rows.shape[0]
    heads_here = q_heads.shape[1]
    block_rows = 512
    block_count = row_count // block_rows
    key_blocks = key_rows.reshape(block_count, block_rows, heads_here, HEAD_DIM)
    value_blocks = value_rows.reshape(block_count, block_rows, heads_here, HEAD_DIM)
    seg_blocks = seg_k.reshape(block_count, block_rows)

    def step_block(state_now, operands):
        key_block, value_block, seg_block = operands
        return (
            merge_states(state_now, block_state(q_heads, seg_q, key_block, value_block, seg_block)),
            None,
        )

    return lax.scan(step_block, carry_state, (key_blocks, value_blocks, seg_blocks))[0]


def body(hidden_in, seg_ids, positions, mod_table, w_qkv, q_gain, k_gain, w_out):
    tok_rows, feat_local = hidden_in.shape
    model_width = feat_local * lax.axis_size("tp")
    heads_width = w_qkv.shape[2]
    heads_here = heads_width // HEAD_DIM
    all_heads_width = heads_width * lax.axis_size("tp")
    x_float = hidden_in.astype(jnp.float32)
    row_sums, row_squares = lax.psum(
        (jnp.sum(x_float, axis=1), jnp.sum(x_float * x_float, axis=1)), "tp"
    )
    mean_value = row_sums / model_width
    variance = row_squares / model_width - mean_value * mean_value
    normed = (x_float - mean_value[:, None]) * lax.rsqrt(variance[:, None] + EPSILON)
    segment_count = mod_table.shape[0]
    table = mod_table.reshape(segment_count, 3 * feat_local)
    onehot = (seg_ids[:, None] == jnp.arange(segment_count, dtype=jnp.int32)[None, :]).astype(
        jnp.float32
    )
    modulation = jnp.dot(onehot, table, precision=lax.Precision.HIGHEST).reshape(
        tok_rows, 3, feat_local
    )
    modded = (normed * (1.0 + modulation[:, 1]) + modulation[:, 0]).astype(jnp.bfloat16)
    full_rows = lax.all_gather(modded, "tp", axis=1, tiled=True)
    portion = lax.all_gather(w_qkv, "seq", axis=0, tiled=True)
    flat = portion.reshape(portion.shape[0], 3 * heads_width)
    projected = jnp.dot(full_rows, flat, preferred_element_type=jnp.float32)
    query_f = projected[:, :heads_width]
    key_f = projected[:, heads_width : 2 * heads_width]
    value_f = projected[:, 2 * heads_width :]
    query_sq, key_sq = lax.psum(
        (jnp.sum(query_f * query_f, axis=1), jnp.sum(key_f * key_f, axis=1)), "tp"
    )
    query_n = query_f * lax.rsqrt(query_sq / all_heads_width + EPSILON)[:, None] * q_gain[None, :]
    key_n = key_f * lax.rsqrt(key_sq / all_heads_width + EPSILON)[:, None] * k_gain[None, :]
    cosine, sine = rope_tables(positions)
    q_heads = rotate_pairs(query_n.reshape(tok_rows, heads_here, HEAD_DIM), cosine, sine).astype(
        jnp.bfloat16
    )
    k_heads = rotate_pairs(key_n.reshape(tok_rows, heads_here, HEAD_DIM), cosine, sine).astype(
        jnp.bfloat16
    )
    k_cache = k_heads.reshape(tok_rows, heads_width)
    v_cache = value_f.astype(jnp.bfloat16)
    key_rows = lax.all_gather(k_cache, "seq", axis=0, tiled=True)
    value_rows = lax.all_gather(v_cache, "seq", axis=0, tiled=True)
    seg_k = lax.all_gather(seg_ids, "seq", axis=0, tiled=True)
    state_end = absorb_keys(
        empty_state(tok_rows, heads_here), q_heads, seg_ids, key_rows, value_rows, seg_k
    )
    attention = (state_end[2] / state_end[1][..., None]).transpose(1, 0, 2)
    attn_out = attention.reshape(tok_rows, heads_width).astype(jnp.bfloat16)
    terms = jnp.dot(
        attn_out,
        lax.all_gather(w_out, "seq", axis=1, tiled=True),
        preferred_element_type=jnp.float32,
    )
    mixed = lax.psum_scatter(
        terms.astype(jnp.bfloat16), "tp", scatter_dimension=1, tiled=True
    ).astype(jnp.float32)
    hidden_out = (x_float + modulation[:, 2] * mixed).astype(jnp.bfloat16)
    return (hidden_out, k_cache, v_cache)


MESH = pl.DeviceIdType.MESH
EXACT = lax.Precision.HIGHEST
FAR = -1e30


def dot00(a, b):
    return lax.dot_general(
        a, b, (((0,), (0,)), ((), ())), precision=EXACT, preferred_element_type=jnp.float32
    )


def dot11(a, b, precision=None):
    return lax.dot_general(
        a, b, (((1,), (1,)), ((), ())), precision=precision, preferred_element_type=jnp.float32
    )


def fused(
    n_seq, n_tp, width, all_heads,
    hid, meta, modt, freq, w, q_gain, k_gain, w_out,
    out, k_out, v_out,
    meta_all, st1, gathered, full, part, parts_in, st2, st3, qkv, cosine, sine,
    q_ext, k_ext, v_all, attn, terms, pair_in, summed, moved, arrived, gate,
    meta_s, meta_r, st1_s, st1_r, z_s, z_r, f_s, f_r, swap_s, swap_r, p_s, p_r,
    st2_s, st2_r, st3_s, st3_r, k_s, k_r, v_s, v_r, a_s, a_r, pair_s, pair_r,
    mv_s, mv_r, ar_s, ar_r,
):
    s = lax.axis_index("seq")
    t = lax.axis_index("tp")
    z = t // 2
    c = t % 2
    rows, feats = hid.shape
    n_z = n_tp // 2
    sibling = z * 2 + 1 - c

    def copy(src, dst, send, recv, to_s, to_t):
        return pltpu.make_async_remote_copy(
            src_ref=src, dst_ref=dst, send_sem=send, recv_sem=recv,
            device_id=(to_s, to_t), device_id_type=MESH,
        )

    plane = [(s + d) % n_seq for d in range(1, n_seq)]
    column = [(t + d) % n_tp for d in range(1, n_tp)]
    line = [(z + d) % n_z for d in range(1, n_z)]

    barrier = pltpu.get_barrier_semaphore()
    for p in plane:
        pl.semaphore_signal(barrier, inc=1, device_id=(p, t), device_id_type=MESH)
    for p in column:
        pl.semaphore_signal(barrier, inc=1, device_id=(s, p), device_id_type=MESH)

    x = hid[...].astype(jnp.float32)
    row8 = lax.broadcasted_iota(jnp.int32, (8, rows), 0)
    ones_b = jnp.ones((8, feats), jnp.bfloat16)
    ones_f = jnp.ones((8, feats), jnp.float32)
    st1[t] = jnp.where(row8 == 0, dot11(ones_b, hid[...]), dot11(ones_f, x * x, EXACT))
    meta_all[s] = meta[...]
    pl.semaphore_wait(barrier, n_seq - 1 + n_tp - 1)
    for p in column:
        copy(st1.at[t], st1.at[t], st1_s.at[p], st1_r.at[t], s, p).start()
    for p in plane:
        copy(meta_all.at[s], meta_all.at[s], meta_s.at[p], meta_r.at[s], p, t).start()

    onehot = (meta[3:4, :] == row8.astype(jnp.float32)).astype(jnp.float32)
    modulation = dot00(onehot, modt[...])
    gate[...] = modulation[:, 2 * feats :]

    for p in column:
        copy(st1.at[p], st1.at[p], st1_s.at[p], st1_r.at[p], s, p).wait_recv()
    totals = jnp.sum(st1[...], axis=0)
    mean_row = totals[0:1] / width
    scale_row = lax.rsqrt(totals[1:2] / width - mean_row * mean_row + EPSILON)
    both = jnp.where(row8 == 0, mean_row, jnp.where(row8 == 1, scale_row, 0.0))
    pick = lax.broadcasted_iota(jnp.int32, (8, 128), 0)
    mean_col = dot00(both, (pick == 0).astype(jnp.float32))[:, 0:1]
    scale_col = dot00(both, (pick == 1).astype(jnp.float32))[:, 0:1]
    normed = (x - mean_col) * scale_col
    modded = normed * (1.0 + modulation[:, feats : 2 * feats]) + modulation[:, :feats]
    gathered[z] = modded.astype(jnp.bfloat16)

    for p in line:
        copy(gathered.at[z], gathered.at[z], z_s.at[p], z_r.at[z], s, p * 2 + c).start()

    def pass_on(p):
        @pl.when(p == s)
        def _():
            full[c, s] = gathered[p]

        @pl.when(p != s)
        def _():
            copy(gathered.at[p], full.at[c, s], f_s.at[p], f_r.at[s], p, t).start()

    pass_on(z)

    for p in plane:
        copy(meta_all.at[p], meta_all.at[p], meta_s.at[p], meta_r.at[p], p, t).wait_recv()
    lane = lax.broadcasted_iota(jnp.int32, (rows, 128), 1)
    even = lane % 2 == 0

    def tables(j, carry):
        block = meta_all[j]
        angle = dot00(block, freq[...])
        cosine[j] = jnp.cos(angle)
        sine[j] = jnp.where(even, -1.0, 1.0) * jnp.sin(angle)
        seg = dot00(block, (pick == 3).astype(jnp.float32))
        same = seg == lane.astype(jnp.float32)
        q_ext[j, :, 128:] = same.astype(jnp.float32).astype(jnp.bfloat16)
        k_ext[j, :, 128:] = jnp.where(same | (lane >= 8), 0.0, FAR).astype(jnp.bfloat16)
        return carry

    lax.fori_loop(0, n_seq, tables, 0)

    for p in line:
        copy(gathered.at[p], gathered.at[p], z_s.at[p], z_r.at[p], s, p * 2 + c).wait_recv()
        pass_on(p)

    def project(d, carry):
        j = (s + d) % n_seq

        @pl.when(d > 0)
        def _():
            copy(full.at[c, j], full.at[c, j], f_s.at[j], f_r.at[j], j, t).wait_recv()

        copy(full.at[c, j], full.at[c, j], swap_s.at[j], swap_r.at[j], s, sibling).start()
        copy(full.at[1 - c, j], full.at[1 - c, j], swap_s.at[j], swap_r.at[j], s, sibling).wait_recv()
        for h in range(n_seq):
            cols = slice(h * 384, (h + 1) * 384)
            acc = jnp.dot(full[0, j], w[:feats, cols], preferred_element_type=jnp.float32)
            acc += jnp.dot(full[1, j], w[feats:, cols], preferred_element_type=jnp.float32)
            part[j, h] = acc.astype(jnp.bfloat16)
        for p in plane:
            copy(part.at[j, p], parts_in.at[s, j], p_s.at[j, p], p_r.at[s, j], p, t).start()
        return carry

    lax.fori_loop(0, n_seq, project, 0)

    ones_h = jnp.ones((8, 128), jnp.float32)
    st2[s] = jnp.zeros((8, rows), jnp.float32)

    def collect(d, carry):
        j = (s + d) % n_seq
        total = part[j, s].astype(jnp.float32)
        for p in plane:
            copy(part.at[j, p], parts_in.at[p, j], p_s.at[j, p], p_r.at[p, j], p, t).wait_recv()
            total += parts_in[p, j].astype(jnp.float32)
        qkv[j] = total
        v_all[j] = total[:, 256:].astype(jnp.bfloat16)
        q_sq = dot11(ones_h, total[:, :128] * total[:, :128], EXACT)
        k_sq = dot11(ones_h, total[:, 128:256] * total[:, 128:256], EXACT)
        st2[s] = jnp.where(row8 == 2 * j, q_sq, jnp.where(row8 == 2 * j + 1, k_sq, st2[s]))
        return carry

    lax.fori_loop(0, n_seq, collect, 0)

    for p in plane:
        copy(st2.at[s], st2.at[s], st2_s.at[p], st2_r.at[s], p, t).start()

    def lanes_of(h):
        return pl.ds(pl.multiple_of(h * 128, 128), 128)

    gains = (q_gain[pl.ds(s, 1), :], k_gain[pl.ds(s, 1), :])

    def rotate(j, carry):
        for i in range(2):
            cols = slice(i * 128, (i + 1) * 128)
            field = qkv[j, :, cols] * gains[i]
            swapped = jnp.where(even, pltpu.roll(field, 127, 1), pltpu.roll(field, 1, 1))
            qkv[j, :, cols] = field * cosine[j] + swapped * sine[j]
        return carry

    for p in plane:
        copy(st2.at[p], st2.at[p], st2_s.at[p], st2_r.at[p], p, t).wait_recv()
    st3[t] = jnp.sum(st2[...], axis=0)
    for p in column:
        copy(st3.at[t], st3.at[t], st3_s.at[p], st3_r.at[t], s, p).start()
    for p in plane:
        copy(v_all.at[p], v_out.at[:, lanes_of(s)], v_s.at[p], v_r.at[s], p, t).start()
    v_out[:, lanes_of(s)] = v_all[s]
    lax.fori_loop(0, n_seq, rotate, 0)
    for p in column:
        copy(st3.at[p], st3.at[p], st3_s.at[p], st3_r.at[p], s, p).wait_recv()
    norm_rows = lax.rsqrt(jnp.sum(st3[...], axis=0) / all_heads + EPSILON)

    def scale_rows(j, carry):
        q_col = dot00(norm_rows, (pick == 2 * j).astype(jnp.float32))
        k_col = dot00(norm_rows, (pick == 2 * j + 1).astype(jnp.float32))
        q_ext[j, :, :128] = (qkv[j, :, :128] * q_col).astype(jnp.bfloat16)
        k_ext[j, :, :128] = (qkv[j, :, 128:256] * k_col).astype(jnp.bfloat16)
        return carry

    lax.fori_loop(0, n_seq, scale_rows, 0)
    for p in plane:
        copy(
            k_ext.at[p, :, pl.ds(0, 128)], k_out.at[:, lanes_of(s)], k_s.at[p], k_r.at[s], p, t
        ).start()
    k_out[:, lanes_of(s)] = k_ext[s, :, :128]

    score_scale = 1.0 / math.sqrt(HEAD_DIM)

    def attend(j, carry):
        keys = k_ext[...].reshape(n_seq * rows, 256)
        values = v_all[...].reshape(n_seq * rows, 128)
        scores = dot11(q_ext[j], keys)
        top = jnp.max(scores, axis=1, keepdims=True)
        weights = jnp.exp((scores - top) * score_scale)
        denominator = jnp.sum(weights, axis=1, keepdims=True)
        mixed = jnp.dot(weights.astype(jnp.bfloat16), values, preferred_element_type=jnp.float32)
        attn[j, :, lanes_of(s)] = (mixed / denominator).astype(jnp.bfloat16)
        for p in plane:
            mine = attn.at[j, :, lanes_of(s)]
            copy(mine, mine, a_s.at[j, p], a_r.at[j, s], p, t).start()
        return carry

    lax.fori_loop(0, n_seq, attend, 0)

    def out_project(j, carry):
        for p in plane:
            theirs = attn.at[j, :, lanes_of(p)]
            copy(theirs, theirs, a_s.at[j, p], a_r.at[j, p], p, t).wait_recv()
        for i in range(2):
            cols = slice(i * feats, (i + 1) * feats)
            terms[j, i] = jnp.dot(
                attn[j], w_out[:, cols], preferred_element_type=jnp.float32
            ).astype(jnp.bfloat16)
        copy(terms.at[j, 1 - c], pair_in.at[j], pair_s.at[j], pair_r.at[j], s, sibling).start()
        return carry

    lax.fori_loop(0, n_seq, out_project, 0)

    def pair_sum(d, carry):
        j = (s + d) % n_seq
        copy(terms.at[j, 1 - c], pair_in.at[j], pair_s.at[j], pair_r.at[j], s, sibling).wait_recv()
        total = (terms[j, c].astype(jnp.float32) + pair_in[j].astype(jnp.float32)).astype(jnp.bfloat16)
        summed[j] = total

        @pl.when(d == 0)
        def _():
            moved[s] = total

        @pl.when(d > 0)
        def _():
            copy(summed.at[j], moved.at[s], mv_s.at[j], mv_r.at[s], j, t).start()

        return carry

    lax.fori_loop(0, n_seq, pair_sum, 0)

    def deliver(p):
        @pl.when(p == z)
        def _():
            arrived[z] = moved[p]

        @pl.when(p != z)
        def _():
            copy(moved.at[p], arrived.at[z], ar_s.at[p], ar_r.at[z], s, p * 2 + c).start()

    deliver(s)
    for p in plane:
        copy(moved.at[p], moved.at[p], mv_s.at[p], mv_r.at[p], p, t).wait_recv()
        deliver(p)
    for p in line:
        copy(arrived.at[p], arrived.at[p], ar_s.at[p], ar_r.at[p], s, p * 2 + c).wait_recv()
    mixed = arrived[0].astype(jnp.float32)
    for p in range(1, n_z):
        mixed += arrived[p].astype(jnp.float32)
    out[...] = (hid[...].astype(jnp.float32) + gate[...] * mixed).astype(jnp.bfloat16)

    for p in plane:
        mine = k_ext.at[p, :, pl.ds(0, 128)]
        copy(mine, k_out.at[:, lanes_of(p)], k_s.at[p], k_r.at[p], p, t).wait()
        copy(v_all.at[p], v_out.at[:, lanes_of(p)], v_s.at[p], v_r.at[p], p, t).wait()
        copy(meta_all.at[s], meta_all.at[s], meta_s.at[p], meta_r.at[s], p, t).wait_send()
        copy(st2.at[s], st2.at[s], st2_s.at[p], st2_r.at[s], p, t).wait_send()
        copy(gathered.at[p], full.at[c, s], f_s.at[p], f_r.at[s], p, t).wait_send()
        copy(summed.at[p], moved.at[s], mv_s.at[p], mv_r.at[s], p, t).wait_send()
    for p in column:
        copy(st1.at[t], st1.at[t], st1_s.at[p], st1_r.at[t], s, p).wait_send()
        copy(st3.at[t], st3.at[t], st3_s.at[p], st3_r.at[t], s, p).wait_send()
    for p in line:
        copy(gathered.at[z], gathered.at[z], z_s.at[p], z_r.at[z], s, p * 2 + c).wait_send()
        copy(moved.at[p], arrived.at[z], ar_s.at[p], ar_r.at[z], s, p * 2 + c).wait_send()

    def drain(j, carry):
        copy(full.at[c, j], full.at[c, j], swap_s.at[j], swap_r.at[j], s, sibling).wait_send()
        copy(terms.at[j, 1 - c], pair_in.at[j], pair_s.at[j], pair_r.at[j], s, sibling).wait_send()
        for p in plane:
            copy(part.at[j, p], parts_in.at[s, j], p_s.at[j, p], p_r.at[s, j], p, t).wait_send()
            mine = attn.at[j, :, lanes_of(s)]
            copy(mine, mine, a_s.at[j, p], a_r.at[j, s], p, t).wait_send()
        return carry

    lax.fori_loop(0, n_seq, drain, 0)


def frequencies():
    part_width = HEAD_DIM // 6
    widths = (HEAD_DIM - 4 * part_width, 2 * part_width, 2 * part_width)
    table = np.zeros((8, HEAD_DIM), np.float32)
    at = 0
    for axis_number, wide in enumerate(widths):
        exponent = np.arange(0, wide, 2, dtype=np.float32) / np.float32(wide)
        frequency = (1.0 / np.float32(10000.0) ** exponent).astype(np.float32)
        table[axis_number, at : at + wide] = np.repeat(frequency, 2)
        at += wide
    return table


def fused_body(hidden_in, seg_ids, positions, mod_table, w_qkv, q_gain, k_gain, w_out):
    n_seq = lax.axis_size("seq")
    n_tp = lax.axis_size("tp")
    rows, feats = hidden_in.shape
    depth, _, heads_width = w_qkv.shape
    segs = mod_table.shape[0]
    meta = jnp.concatenate(
        [positions, seg_ids[None], jnp.zeros((4, rows), jnp.int32)], axis=0
    ).astype(jnp.float32)
    modt = jnp.pad(mod_table.reshape(segs, 3 * feats), ((0, 8 - segs), (0, 0)))
    w = (
        w_qkv.reshape(depth, 3, n_seq, HEAD_DIM)
        .transpose(0, 2, 1, 3)
        .reshape(depth, 3 * heads_width)
    )
    bf16, f32 = jnp.bfloat16, jnp.float32
    n_z = n_tp // 2
    dma = pltpu.SemaphoreType.DMA
    scratch = [
        pltpu.VMEM((n_seq, 8, rows), f32),
        pltpu.VMEM((n_tp, 8, rows), f32),
        pltpu.VMEM((n_z, rows, feats), bf16),
        pltpu.VMEM((2, n_seq, rows, feats), bf16),
        pltpu.VMEM((n_seq, n_seq, rows, 384), bf16),
        pltpu.VMEM((n_seq, n_seq, rows, 384), bf16),
        pltpu.VMEM((n_seq, 8, rows), f32),
        pltpu.VMEM((n_tp, 8, rows), f32),
        pltpu.VMEM((n_seq, rows, 384), f32),
        pltpu.VMEM((n_seq, rows, 128), f32),
        pltpu.VMEM((n_seq, rows, 128), f32),
        pltpu.VMEM((n_seq, rows, 256), bf16),
        pltpu.VMEM((n_seq, rows, 256), bf16),
        pltpu.VMEM((n_seq, rows, 128), bf16),
        pltpu.VMEM((n_seq, rows, heads_width), bf16),
        pltpu.VMEM((n_seq, 2, rows, feats), bf16),
        pltpu.VMEM((n_seq, rows, feats), bf16),
        pltpu.VMEM((n_seq, rows, feats), bf16),
        pltpu.VMEM((n_seq, rows, feats), bf16),
        pltpu.VMEM((n_z, rows, feats), bf16),
        pltpu.VMEM((rows, feats), f32),
    ]
    square = (n_seq, n_seq)
    shapes = [
        (n_seq,), (n_tp,), (n_z,), (n_seq,), (n_seq,), square,
        (n_seq,), (n_tp,), (n_seq,), (n_seq,), square, (n_seq,), (n_seq,), (n_z,),
    ]
    for shape in shapes:
        scratch += [dma(shape), dma(shape)]
    vmem = pl.BlockSpec(memory_space=pltpu.VMEM)
    return pl.pallas_call(
        functools.partial(fused, n_seq, n_tp, feats * n_tp, heads_width * n_tp),
        out_shape=(
            jax.ShapeDtypeStruct((rows, feats), bf16),
            jax.ShapeDtypeStruct((rows, heads_width), bf16),
            jax.ShapeDtypeStruct((rows, heads_width), bf16),
        ),
        in_specs=[vmem] * 8,
        out_specs=(vmem, vmem, vmem),
        scratch_shapes=scratch,
        compiler_params=pltpu.CompilerParams(
            collective_id=0, has_side_effects=True, vmem_limit_bytes=58 * 1024 * 1024
        ),
        cost_estimate=pl.CostEstimate(
            flops=6_000_000_000, bytes_accessed=8_000_000, transcendentals=1_200_000
        ),
    )(
        hidden_in, meta, modt, jnp.asarray(frequencies()), w,
        q_gain.reshape(n_seq, HEAD_DIM), k_gain.reshape(n_seq, HEAD_DIM), w_out,
    )


def pick_body(*operands):
    hidden_in, seg_ids, positions, mod_table, w_qkv = operands[:5]
    n_seq, n_tp = lax.axis_size("seq"), lax.axis_size("tp")
    fits = (
        n_tp == 2 * n_seq
        and n_seq == 4
        and w_qkv.shape[2] == n_seq * HEAD_DIM
        and w_qkv.shape[0] == 2 * hidden_in.shape[1]
        and hidden_in.shape[0] == 256
        and mod_table.shape[0] <= 8
    )
    return (fused_body if fits else body)(*operands)


def solution(mesh):
    in_specs = (
        P("seq", "tp"),
        P("seq"),
        P(None, "seq"),
        P(None, None, "tp"),
        P("seq", None, "tp"),
        P("tp"),
        P("tp"),
        P("tp", "seq"),
    )
    out_specs = (P("seq", "tp"), P("seq", "tp"), P("seq", "tp"))
    return jax.shard_map(pick_body, mesh=mesh, in_specs=in_specs, out_specs=out_specs, check_vma=False)
```

```python
import functools
import math

import jax
import jax.numpy as jnp
import numpy as np
from jax import lax
from jax.experimental import pallas as pl
from jax.experimental.pallas import tpu as pltpu
from jax.sharding import PartitionSpec as P

HEAD_DIM = 128


EPSILON = 1e-06
NEG_FILL = -1e30


def rope_tables(positions):
    part_width = HEAD_DIM // 6
    widths = (HEAD_DIM - 4 * part_width, 2 * part_width, 2 * part_width)
    angle_list = []
    for axis_number in range(3):
        exponent = jnp.arange(0, widths[axis_number], 2, dtype=jnp.float32) / widths[axis_number]
        frequency = 1.0 / 10000.0**exponent
        angle_list.append(positions[axis_number].astype(jnp.float32)[:, None] * frequency[None, :])
    angle_all = jnp.concatenate(angle_list, axis=1)
    return (jnp.cos(angle_all), jnp.sin(angle_all))


def rotate_pairs(field, cosine, sine):
    even_part = field[..., 0::2]
    odd_part = field[..., 1::2]
    cos_wide = cosine[:, None, :]
    sin_wide = sine[:, None, :]
    new_even = even_part * cos_wide - odd_part * sin_wide
    new_odd = even_part * sin_wide + odd_part * cos_wide
    return jnp.stack([new_even, new_odd], axis=-1).reshape(field.shape)


def empty_state(query_rows, heads_here):
    maxima = jnp.full((heads_here, query_rows), NEG_FILL, jnp.float32)
    totals = jnp.zeros((heads_here, query_rows), jnp.float32)
    weighted = jnp.zeros((heads_here, query_rows, HEAD_DIM), jnp.float32)
    return (maxima, totals, weighted)


def merge_states(first, second):
    largest = jnp.maximum(first[0], second[0])
    first_factor = jnp.exp(first[0] - largest)
    second_factor = jnp.exp(second[0] - largest)
    totals = first[1] * first_factor + second[1] * second_factor
    weighted = first[2] * first_factor[..., None] + second[2] * second_factor[..., None]
    return (largest, totals, weighted)


def block_state(q_heads, seg_q, key_heads, value_heads, seg_k):
    score_scale = 1.0 / math.sqrt(HEAD_DIM)
    scores = (
        jnp.einsum("qhd,khd->hqk", q_heads, key_heads, preferred_element_type=jnp.float32)
        * score_scale
    )
    same_seg = seg_q[:, None] == seg_k[None, :]
    masked = jnp.where(same_seg[None], scores, NEG_FILL)
    maxima = jnp.max(masked, axis=2)
    weights = jnp.where(same_seg[None], jnp.exp(masked - maxima[..., None]), 0.0)
    totals = jnp.sum(weights, axis=2)
    weighted = jnp.einsum(
        "hqk,khd->hqd",
        weights.astype(jnp.bfloat16),
        value_heads,
        preferred_element_type=jnp.float32,
    )
    return (maxima, totals, weighted)


def absorb_keys(carry_state, q_heads, seg_q, key_rows, value_rows, seg_k):
    row_count = key_rows.shape[0]
    heads_here = q_heads.shape[1]
    block_rows = 512
    block_count = row_count // block_rows
    key_blocks = key_rows.reshape(block_count, block_rows, heads_here, HEAD_DIM)
    value_blocks = value_rows.reshape(block_count, block_rows, heads_here, HEAD_DIM)
    seg_blocks = seg_k.reshape(block_count, block_rows)

    def step_block(state_now, operands):
        key_block, value_block, seg_block = operands
        return (
            merge_states(state_now, block_state(q_heads, seg_q, key_block, value_block, seg_block)),
            None,
        )

    return lax.scan(step_block, carry_state, (key_blocks, value_blocks, seg_blocks))[0]


def body(hidden_in, seg_ids, positions, mod_table, w_qkv, q_gain, k_gain, w_out):
    tok_rows, feat_local = hidden_in.shape
    model_width = feat_local * lax.axis_size("tp")
    heads_width = w_qkv.shape[2]
    heads_here = heads_width // HEAD_DIM
    all_heads_width = heads_width * lax.axis_size("tp")
    x_float = hidden_in.astype(jnp.float32)
    row_sums, row_squares = lax.psum(
        (jnp.sum(x_float, axis=1), jnp.sum(x_float * x_float, axis=1)), "tp"
    )
    mean_value = row_sums / model_width
    variance = row_squares / model_width - mean_value * mean_value
    normed = (x_float - mean_value[:, None]) * lax.rsqrt(variance[:, None] + EPSILON)
    segment_count = mod_table.shape[0]
    table = mod_table.reshape(segment_count, 3 * feat_local)
    onehot = (seg_ids[:, None] == jnp.arange(segment_count, dtype=jnp.int32)[None, :]).astype(
        jnp.float32
    )
    modulation = jnp.dot(onehot, table, precision=lax.Precision.HIGHEST).reshape(
        tok_rows, 3, feat_local
    )
    modded = (normed * (1.0 + modulation[:, 1]) + modulation[:, 0]).astype(jnp.bfloat16)
    full_rows = lax.all_gather(modded, "tp", axis=1, tiled=True)
    portion = lax.all_gather(w_qkv, "seq", axis=0, tiled=True)
    flat = portion.reshape(portion.shape[0], 3 * heads_width)
    projected = jnp.dot(full_rows, flat, preferred_element_type=jnp.float32)
    query_f = projected[:, :heads_width]
    key_f = projected[:, heads_width : 2 * heads_width]
    value_f = projected[:, 2 * heads_width :]
    query_sq, key_sq = lax.psum(
        (jnp.sum(query_f * query_f, axis=1), jnp.sum(key_f * key_f, axis=1)), "tp"
    )
    query_n = query_f * lax.rsqrt(query_sq / all_heads_width + EPSILON)[:, None] * q_gain[None, :]
    key_n = key_f * lax.rsqrt(key_sq / all_heads_width + EPSILON)[:, None] * k_gain[None, :]
    cosine, sine = rope_tables(positions)
    q_heads = rotate_pairs(query_n.reshape(tok_rows, heads_here, HEAD_DIM), cosine, sine).astype(
        jnp.bfloat16
    )
    k_heads = rotate_pairs(key_n.reshape(tok_rows, heads_here, HEAD_DIM), cosine, sine).astype(
        jnp.bfloat16
    )
    k_cache = k_heads.reshape(tok_rows, heads_width)
    v_cache = value_f.astype(jnp.bfloat16)
    key_rows = lax.all_gather(k_cache, "seq", axis=0, tiled=True)
    value_rows = lax.all_gather(v_cache, "seq", axis=0, tiled=True)
    seg_k = lax.all_gather(seg_ids, "seq", axis=0, tiled=True)
    state_end = absorb_keys(
        empty_state(tok_rows, heads_here), q_heads, seg_ids, key_rows, value_rows, seg_k
    )
    attention = (state_end[2] / state_end[1][..., None]).transpose(1, 0, 2)
    attn_out = attention.reshape(tok_rows, heads_width).astype(jnp.bfloat16)
    terms = jnp.dot(
        attn_out,
        lax.all_gather(w_out, "seq", axis=1, tiled=True),
        preferred_element_type=jnp.float32,
    )
    mixed = lax.psum_scatter(
        terms.astype(jnp.bfloat16), "tp", scatter_dimension=1, tiled=True
    ).astype(jnp.float32)
    hidden_out = (x_float + modulation[:, 2] * mixed).astype(jnp.bfloat16)
    return (hidden_out, k_cache, v_cache)


MESH = pl.DeviceIdType.MESH
EXACT = lax.Precision.HIGHEST
FAR = -1e30
CHUNKS = 4


def dot00(a, b):
    return lax.dot_general(
        a, b, (((0,), (0,)), ((), ())), precision=EXACT, preferred_element_type=jnp.float32
    )


def dot11(a, b, precision=None):
    return lax.dot_general(
        a, b, (((1,), (1,)), ((), ())), precision=precision, preferred_element_type=jnp.float32
    )


def fused(
    n_seq, n_tp, width, all_heads,
    hid, segs, positions, modt, freq, w_any, q_gain, k_gain, w_out_any,
    out, k_out, v_out,
    w, w_out, mod8, meta_all, st1, gathered, full, part, relay, parts_in, parts_last,
    st2, st3, qkv, cosine, sine, q_ext, k_ext, v_all, attn, terms, pair_in, summed, moved,
    arrived, gate,
    w_sem, meta_s, meta_r, st1_s, st1_r, z_s, z_r, f_s, f_r, swap_s, swap_r, p_s, p_r,
    last_s, last_r, st2_s, st2_r, st3_s, st3_r, k_s, k_r, v_s, v_r, a_s, a_r, pair_s, pair_r,
    mv_s, mv_r, ar_s, ar_r,
):
    s = lax.axis_index("seq")
    t = lax.axis_index("tp")
    z = t // 2
    c = t % 2
    rows, feats = hid.shape
    n_z = n_tp // 2
    chunks = CHUNKS
    cr = rows // chunks
    many = n_seq * cr
    sibling = z * 2 + 1 - c
    x_next = (s // 2) * 2 + 1 - s % 2
    y_next = (1 - s // 2) * 2 + s % 2
    corner = (1 - s // 2) * 2 + 1 - s % 2

    def copy(src, dst, send, recv, to_s, to_t):
        return pltpu.make_async_remote_copy(
            src_ref=src, dst_ref=dst, send_sem=send, recv_sem=recv,
            device_id=(to_s, to_t), device_id_type=MESH,
        )

    def chunk(i):
        return pl.ds(pl.multiple_of(i * cr, cr), cr)

    def lanes_of(h):
        return pl.ds(pl.multiple_of(h * 128, 128), 128)

    plane = [(s + d) % n_seq for d in range(1, n_seq)]
    column = [(t + d) % n_tp for d in range(1, n_tp)]
    line = [(z + d) % n_z for d in range(1, n_z)]

    barrier = pltpu.get_barrier_semaphore()
    for p in plane:
        pl.semaphore_signal(barrier, inc=1, device_id=(p, t), device_id_type=MESH)
    for p in column:
        pl.semaphore_signal(barrier, inc=1, device_id=(s, p), device_id_type=MESH)
    load_w = pltpu.make_async_copy(w_any, w, w_sem.at[0])
    load_w_out = pltpu.make_async_copy(w_out_any, w_out, w_sem.at[1])
    load_w.start()
    load_w_out.start()

    x = hid[...].astype(jnp.float32)
    row8 = lax.broadcasted_iota(jnp.int32, (8, rows), 0)
    ones_b = jnp.ones((8, feats), jnp.bfloat16)
    ones_f = jnp.ones((8, feats), jnp.float32)
    st1[t] = jnp.where(row8 == 0, dot11(ones_b, hid[...]), dot11(ones_f, x * x, EXACT))
    meta_all[s] = jnp.zeros((8, rows), jnp.float32)
    meta_all[s, 0:3] = positions[...].astype(jnp.float32)
    meta_all[s, 3:4] = segs[...].astype(jnp.float32)
    pl.semaphore_wait(barrier, n_seq - 1 + n_tp - 1)
    for p in column:
        copy(st1.at[t], st1.at[t], st1_s.at[p], st1_r.at[t], s, p).start()
    for p in plane:
        copy(meta_all.at[s], meta_all.at[s], meta_s.at[p], meta_r.at[s], p, t).start()

    onehot = (segs[...] == row8).astype(jnp.float32)
    mod8[...] = jnp.zeros(mod8.shape, jnp.float32)
    mod8[:, : modt.shape[1]] = modt[...]
    shift = dot00(onehot, mod8[0])
    scale = dot00(onehot, mod8[1])
    gate[...] = dot00(onehot, mod8[2])

    for p in column:
        copy(st1.at[p], st1.at[p], st1_s.at[p], st1_r.at[p], s, p).wait_recv()
    totals = jnp.sum(st1[...], axis=0)
    mean_row = totals[0:1] / width
    scale_row = lax.rsqrt(totals[1:2] / width - mean_row * mean_row + EPSILON)
    both = jnp.where(row8 == 0, mean_row, jnp.where(row8 == 1, scale_row, 0.0))
    pick = lax.broadcasted_iota(jnp.int32, (8, 128), 0)
    mean_col = dot00(both, (pick == 0).astype(jnp.float32))[:, 0:1]
    scale_col = dot00(both, (pick == 1).astype(jnp.float32))[:, 0:1]
    normed = (x - mean_col) * scale_col
    gathered[z] = (normed * (1.0 + scale) + shift).astype(jnp.bfloat16)

    for i in range(chunks):
        for p in line:
            mine = gathered.at[z, chunk(i)]
            copy(mine, mine, z_s.at[i, p], z_r.at[i, z], s, p * 2 + c).start()
    for p in plane:
        copy(meta_all.at[p], meta_all.at[p], meta_s.at[p], meta_r.at[p], p, t).wait_recv()
    lane = lax.broadcasted_iota(jnp.int32, (rows, 128), 1)
    even = lane % 2 == 0

    def pass_on(i, p):
        @pl.when(p == s)
        def _():
            full[c, s, chunk(i)] = gathered[p, chunk(i)]

        @pl.when(p != s)
        def _():
            copy(
                gathered.at[p, chunk(i)], full.at[c, s, chunk(i)], f_s.at[i, p], f_r.at[i, s], p, t
            ).start()

    def from_line(i):
        pass_on(i, z)
        for p in line:
            theirs = gathered.at[p, chunk(i)]
            copy(theirs, theirs, z_s.at[i, p], z_r.at[i, p], s, p * 2 + c).wait_recv()
            pass_on(i, p)

    def swap(i, half):
        block = full.at[half, :, chunk(i)]
        return copy(block, block, swap_s.at[i], swap_r.at[i], s, sibling)

    def from_plane(i):
        for p in plane:
            theirs = full.at[c, p, chunk(i)]
            copy(theirs, theirs, f_s.at[i, p], f_r.at[i, p], p, t).wait_recv()
        swap(i, c).start()

    def tables(j):
        block = meta_all[j]
        angle = dot00(block, freq[...])
        cosine[:, j] = jnp.cos(angle).reshape(chunks, cr, 128)
        sine[:, j] = (jnp.where(even, -1.0, 1.0) * jnp.sin(angle)).reshape(chunks, cr, 128)
        seg = dot00(block, (pick == 3).astype(jnp.float32))
        same = seg == lane.astype(jnp.float32)
        q_mask = same.astype(jnp.float32).astype(jnp.bfloat16)
        k_mask = jnp.where(same | (lane >= 8), 0.0, FAR).astype(jnp.bfloat16)
        q_ext[:, j, :, 128:] = q_mask.reshape(chunks, cr, 128)
        k_ext[:, j, :, 128:] = k_mask.reshape(chunks, cr, 128)

    def first_of(i):
        return jnp.where(i % 2 == 0, x_next, y_next)

    def second_of(i):
        return jnp.where(i % 2 == 0, y_next, x_next)

    def to_first(i, n, h):
        return copy(part.at[i, h], parts_in.at[i, n], p_s.at[i, n], p_r.at[i, n], first_of(i), t)

    def to_second(i):
        return copy(relay.at[i], parts_last.at[i], last_s.at[i], last_r.at[i], second_of(i), t)

    def project(i):
        swap(i, 1 - c).wait_recv()
        left = full[0, :, chunk(i)].reshape(many, feats)
        right = full[1, :, chunk(i)].reshape(many, feats)
        for n in range(3):
            acc = jnp.dot(left, w[n, :feats], preferred_element_type=jnp.float32)
            acc += jnp.dot(right, w[n, feats:], preferred_element_type=jnp.float32)
            for h in range(n_seq):
                part[i, h, :, n * 128 : (n + 1) * 128] = acc[:, h * 128 : (h + 1) * 128].astype(
                    jnp.bfloat16
                )
        to_first(i, 1, corner).start()
        to_first(i, 0, first_of(i)).start()

    def relay_on(i):
        to_first(i, 1, corner).wait_recv()
        relay[i] = (
            part[i, second_of(i)].astype(jnp.float32) + parts_in[i, 1].astype(jnp.float32)
        ).astype(jnp.bfloat16)
        to_second(i).start()

    ones_h = jnp.ones((8, 128), jnp.float32)
    st2[s] = jnp.zeros((8, rows), jnp.float32)

    def collect(i):
        to_first(i, 0, corner).wait_recv()
        to_second(i).wait_recv()
        total = part[i, s].astype(jnp.float32) + parts_in[i, 0].astype(jnp.float32)
        total += parts_last[i].astype(jnp.float32)
        qkv[i] = total
        v_all[i] = total[:, 256:].astype(jnp.bfloat16).reshape(n_seq, cr, 128)
        q_sq = dot11(ones_h, total[:, :128] * total[:, :128], EXACT)
        k_sq = dot11(ones_h, total[:, 128:256] * total[:, 128:256], EXACT)
        st2[s] = jnp.where(row8 == 2 * i, q_sq, jnp.where(row8 == 2 * i + 1, k_sq, st2[s]))

    load_w.wait()
    load_w_out.wait()

    def during(step, at, work):
        @pl.when((step >= at) & (step < at + chunks))
        def _():
            work(step - at)

    def project_step(step, carry):
        during(step, 0, from_line)
        during(step, 1, project)
        during(step, 2, relay_on)
        during(step, 0, from_plane)
        during(step, 0, tables)
        during(step, 3, collect)
        return carry

    lax.fori_loop(0, chunks + 3, project_step, 0)

    for p in plane:
        copy(st2.at[s], st2.at[s], st2_s.at[p], st2_r.at[s], p, t).start()

    gains = (q_gain[pl.ds(s, 1), :], k_gain[pl.ds(s, 1), :])

    def rotate(i, carry):
        cos_i = cosine[i].reshape(many, 128)
        sin_i = sine[i].reshape(many, 128)
        for n in range(2):
            cols = slice(n * 128, (n + 1) * 128)
            field = qkv[i, :, cols] * gains[n]
            swapped = jnp.where(even, pltpu.roll(field, 127, 1), pltpu.roll(field, 1, 1))
            qkv[i, :, cols] = field * cos_i + swapped * sin_i
        return carry

    for p in plane:
        copy(st2.at[p], st2.at[p], st2_s.at[p], st2_r.at[p], p, t).wait_recv()
    st3[t] = jnp.sum(st2[...], axis=0)
    for p in column:
        copy(st3.at[t], st3.at[t], st3_s.at[p], st3_r.at[t], s, p).start()

    def send_v(p):
        return copy(v_all.at[:, p], v_out.at[:, :, lanes_of(s)], v_s.at[p], v_r.at[s], p, t)

    def send_k(p):
        mine = k_ext.at[:, p, :, pl.ds(0, 128)]
        return copy(mine, k_out.at[:, :, lanes_of(s)], k_s.at[p], k_r.at[s], p, t)

    for p in plane:
        send_v(p).start()
    v_out[:, :, lanes_of(s)] = v_all[:, s]
    lax.fori_loop(0, chunks, rotate, 0)
    for p in column:
        copy(st3.at[p], st3.at[p], st3_s.at[p], st3_r.at[p], s, p).wait_recv()
    norm_rows = lax.rsqrt(jnp.sum(st3[...], axis=0) / all_heads + EPSILON)

    def scale_rows(i, carry):
        q_col = dot00(norm_rows, (pick == 2 * i).astype(jnp.float32))
        k_col = dot00(norm_rows, (pick == 2 * i + 1).astype(jnp.float32))
        q_i = (qkv[i, :, :128] * q_col).astype(jnp.bfloat16)
        k_i = (qkv[i, :, 128:256] * k_col).astype(jnp.bfloat16)
        q_ext[i, :, :, :128] = q_i.reshape(n_seq, cr, 128)
        k_ext[i, :, :, :128] = k_i.reshape(n_seq, cr, 128)
        return carry

    lax.fori_loop(0, chunks, scale_rows, 0)

    score_scale = 1.0 / math.sqrt(HEAD_DIM)

    def attend(i):
        keys = k_ext[...].reshape(n_seq * rows, 256)
        values = v_all[...].reshape(n_seq * rows, 128)
        scores = dot11(q_ext[i].reshape(many, 256), keys)
        top = jnp.max(scores, axis=1, keepdims=True)
        weights = jnp.exp((scores - top) * score_scale)
        denominator = jnp.sum(weights, axis=1, keepdims=True)
        mixed = jnp.dot(weights.astype(jnp.bfloat16), values, preferred_element_type=jnp.float32)
        done = (mixed / denominator).astype(jnp.bfloat16)
        attn[i, :, :, lanes_of(s)] = done.reshape(n_seq, cr, 128)
        for p in plane:
            mine = attn.at[i, :, :, lanes_of(s)]
            copy(mine, mine, a_s.at[i, p], a_r.at[i, s], p, t).start()

    def pair(i):
        return copy(
            terms.at[i, 1 - c], pair_in.at[i], pair_s.at[i], pair_r.at[i], s, sibling
        )

    def out_project(i):
        for p in plane:
            theirs = attn.at[i, :, :, lanes_of(p)]
            copy(theirs, theirs, a_s.at[i, p], a_r.at[i, p], p, t).wait_recv()
        for n in range(2):
            cols = slice(n * feats, (n + 1) * feats)
            product = jnp.dot(
                attn[i].reshape(many, n_seq * 128), w_out[:, cols],
                preferred_element_type=jnp.float32,
            )
            terms[i, n] = product.astype(jnp.bfloat16).reshape(n_seq, cr, feats)
        pair(i).start()

    def pair_sum(i):
        pair(i).wait_recv()
        summed[i] = (terms[i, c].astype(jnp.float32) + pair_in[i].astype(jnp.float32)).astype(
            jnp.bfloat16
        )
        moved[s, i] = summed[i, s]
        for p in plane:
            copy(summed.at[i, p], moved.at[s, i], mv_s.at[i, p], mv_r.at[i, s], p, t).start()

    def deliver(i, p):
        @pl.when(p == z)
        def _():
            arrived[z, i] = moved[p, i]

        @pl.when(p != z)
        def _():
            copy(
                moved.at[p, i], arrived.at[z, i], ar_s.at[i, p], ar_r.at[i, z], s, p * 2 + c
            ).start()

    def deliver_all(i):
        deliver(i, s)
        for p in plane:
            theirs = moved.at[p, i]
            copy(theirs, theirs, mv_s.at[i, p], mv_r.at[i, p], p, t).wait_recv()
            deliver(i, p)

    def attend_step(step, carry):
        during(step, 0, attend)
        during(step, 1, out_project)
        during(step, 2, deliver_all)
        during(step, 1, pair_sum)
        return carry

    lax.fori_loop(0, chunks + 2, attend_step, 0)
    for p in plane:
        send_k(p).start()
    k_out[:, :, lanes_of(s)] = k_ext[:, s, :, :128]

    def finish(i, carry):
        for p in line:
            theirs = arrived.at[p, i]
            copy(theirs, theirs, ar_s.at[i, p], ar_r.at[i, p], s, p * 2 + c).wait_recv()
        mixed = arrived[0, i].astype(jnp.float32)
        for p in range(1, n_z):
            mixed += arrived[p, i].astype(jnp.float32)
        base = hid[chunk(i), :].astype(jnp.float32)
        out[chunk(i), :] = (base + gate[chunk(i), :] * mixed).astype(jnp.bfloat16)
        return carry

    lax.fori_loop(0, chunks, finish, 0)

    for p in plane:
        copy(
            k_ext.at[:, p, :, pl.ds(0, 128)], k_out.at[:, :, lanes_of(p)], k_s.at[p], k_r.at[p], p, t
        ).wait()
        copy(v_all.at[:, p], v_out.at[:, :, lanes_of(p)], v_s.at[p], v_r.at[p], p, t).wait()
        copy(meta_all.at[s], meta_all.at[s], meta_s.at[p], meta_r.at[s], p, t).wait_send()
        copy(st2.at[s], st2.at[s], st2_s.at[p], st2_r.at[s], p, t).wait_send()
    for p in column:
        copy(st1.at[t], st1.at[t], st1_s.at[p], st1_r.at[t], s, p).wait_send()
        copy(st3.at[t], st3.at[t], st3_s.at[p], st3_r.at[t], s, p).wait_send()

    def drain(i, carry):
        swap(i, c).wait_send()
        pair(i).wait_send()
        to_first(i, 0, first_of(i)).wait_send()
        to_first(i, 1, corner).wait_send()
        to_second(i).wait_send()
        for p in line:
            mine = gathered.at[z, chunk(i)]
            copy(mine, mine, z_s.at[i, p], z_r.at[i, z], s, p * 2 + c).wait_send()
            copy(
                moved.at[p, i], arrived.at[z, i], ar_s.at[i, p], ar_r.at[i, z], s, p * 2 + c
            ).wait_send()
        for p in plane:
            copy(
                gathered.at[p, chunk(i)], full.at[c, s, chunk(i)], f_s.at[i, p], f_r.at[i, s], p, t
            ).wait_send()
            mine = attn.at[i, :, :, lanes_of(s)]
            copy(mine, mine, a_s.at[i, p], a_r.at[i, s], p, t).wait_send()
            copy(summed.at[i, p], moved.at[s, i], mv_s.at[i, p], mv_r.at[i, s], p, t).wait_send()
        return carry

    lax.fori_loop(0, chunks, drain, 0)


def hand_over(*refs):
    n = 3
    sems = refs[2 * n]
    moves = [pltpu.make_async_copy(refs[i], refs[n + i], sems.at[i]) for i in range(n)]
    for move in moves:
        move.start()
    for move in moves:
        move.wait()


def frequencies():
    part_width = HEAD_DIM // 6
    widths = (HEAD_DIM - 4 * part_width, 2 * part_width, 2 * part_width)
    table = np.zeros((8, HEAD_DIM), np.float32)
    at = 0
    for axis_number, wide in enumerate(widths):
        exponent = np.arange(0, wide, 2, dtype=np.float32) / np.float32(wide)
        frequency = (1.0 / np.float32(10000.0) ** exponent).astype(np.float32)
        table[axis_number, at : at + wide] = np.repeat(frequency, 2)
        at += wide
    return table


def fused_body(hidden_in, seg_ids, positions, mod_table, w_qkv, q_gain, k_gain, w_out):
    n_seq = lax.axis_size("seq")
    n_tp = lax.axis_size("tp")
    rows, feats = hidden_in.shape
    depth, _, heads_width = w_qkv.shape
    bf16, f32 = jnp.bfloat16, jnp.float32
    n_z = n_tp // 2
    chunks = CHUNKS
    cr = rows // chunks
    many = n_seq * cr
    dma = pltpu.SemaphoreType.DMA
    scratch = [
        pltpu.VMEM((3, depth, heads_width), bf16),
        pltpu.VMEM(w_out.shape, bf16),
        pltpu.VMEM((3, 8, feats), f32),
        pltpu.VMEM((n_seq, 8, rows), f32),
        pltpu.VMEM((n_tp, 8, rows), f32),
        pltpu.VMEM((n_z, rows, feats), bf16),
        pltpu.VMEM((2, n_seq, rows, feats), bf16),
        pltpu.VMEM((chunks, n_seq, many, 384), bf16),
        pltpu.VMEM((chunks, many, 384), bf16),
        pltpu.VMEM((chunks, 2, many, 384), bf16),
        pltpu.VMEM((chunks, many, 384), bf16),
        pltpu.VMEM((n_seq, 8, rows), f32),
        pltpu.VMEM((n_tp, 8, rows), f32),
        pltpu.VMEM((chunks, many, 384), f32),
        pltpu.VMEM((chunks, n_seq, cr, 128), f32),
        pltpu.VMEM((chunks, n_seq, cr, 128), f32),
        pltpu.VMEM((chunks, n_seq, cr, 256), bf16),
        pltpu.VMEM((chunks, n_seq, cr, 256), bf16),
        pltpu.VMEM((chunks, n_seq, cr, 128), bf16),
        pltpu.VMEM((chunks, n_seq, cr, heads_width), bf16),
        pltpu.VMEM((chunks, 2, n_seq, cr, feats), bf16),
        pltpu.VMEM((chunks, n_seq, cr, feats), bf16),
        pltpu.VMEM((chunks, n_seq, cr, feats), bf16),
        pltpu.VMEM((n_seq, chunks, cr, feats), bf16),
        pltpu.VMEM((n_z, chunks, cr, feats), bf16),
        pltpu.VMEM((rows, feats), f32),
        dma((2,)),
    ]
    wide = (chunks, n_seq)
    shapes = [
        (n_seq,), (n_tp,), (chunks, n_z), wide, (chunks,), (chunks, 2), (chunks,),
        (n_seq,), (n_tp,), (n_seq,), (n_seq,), wide, (chunks,), wide, (chunks, n_z),
    ]
    for shape in shapes:
        scratch += [dma(shape), dma(shape)]
    vmem = pl.BlockSpec(memory_space=pltpu.VMEM)
    whole = pl.BlockSpec(memory_space=pl.ANY)
    results = pl.pallas_call(
        functools.partial(fused, n_seq, n_tp, feats * n_tp, heads_width * n_tp),
        out_shape=(
            jax.ShapeDtypeStruct((rows, feats), bf16),
            jax.ShapeDtypeStruct((chunks, cr, heads_width), bf16),
            jax.ShapeDtypeStruct((chunks, cr, heads_width), bf16),
        ),
        in_specs=[vmem, vmem, vmem, vmem, vmem, whole, vmem, vmem, whole],
        out_specs=(vmem, vmem, vmem),
        scratch_shapes=scratch,
        compiler_params=pltpu.CompilerParams(
            collective_id=0, has_side_effects=True, vmem_limit_bytes=58 * 1024 * 1024
        ),
        cost_estimate=pl.CostEstimate(
            flops=6_000_000_000, bytes_accessed=8_000_000, transcendentals=1_200_000
        ),
    )(
        hidden_in, seg_ids.reshape(1, rows), positions, mod_table.transpose(1, 0, 2),
        jnp.asarray(frequencies()), w_qkv.transpose(1, 0, 2),
        q_gain.reshape(n_seq, HEAD_DIM), k_gain.reshape(n_seq, HEAD_DIM), w_out,
    )
    hidden, k_cache, v_cache = pl.pallas_call(
        hand_over,
        out_shape=tuple(jax.ShapeDtypeStruct(r.shape, r.dtype) for r in results),
        in_specs=[whole] * 3,
        out_specs=(whole,) * 3,
        scratch_shapes=[dma((3,))],
        cost_estimate=pl.CostEstimate(flops=0, bytes_accessed=1_700_000, transcendentals=0),
    )(*results)
    return (
        hidden,
        k_cache.reshape(rows, heads_width),
        v_cache.reshape(rows, heads_width),
    )


def pick_body(*operands):
    hidden_in, seg_ids, positions, mod_table, w_qkv = operands[:5]
    n_seq, n_tp = lax.axis_size("seq"), lax.axis_size("tp")
    fits = (
        n_tp == 2 * n_seq
        and n_seq == 4
        and w_qkv.shape[2] == n_seq * HEAD_DIM
        and w_qkv.shape[0] == 2 * hidden_in.shape[1]
        and hidden_in.shape[0] == 256
        and mod_table.shape[0] <= 8
    )
    return (fused_body if fits else body)(*operands)


def solution(mesh):
    in_specs = (
        P("seq", "tp"),
        P("seq"),
        P(None, "seq"),
        P(None, None, "tp"),
        P("seq", None, "tp"),
        P("tp"),
        P("tp"),
        P("tp", "seq"),
    )
    out_specs = (P("seq", "tp"), P("seq", "tp"), P("seq", "tp"))
    return jax.shard_map(pick_body, mesh=mesh, in_specs=in_specs, out_specs=out_specs, check_vma=False)
```

```python
import functools
import math

import jax
import jax.numpy as jnp
import numpy as np
from jax import lax
from jax.experimental import pallas as pl
from jax.experimental.pallas import tpu as pltpu
from jax.sharding import PartitionSpec as P

HEAD_DIM = 128


EPSILON = 1e-06
NEG_FILL = -1e30


def rope_tables(positions):
    part_width = HEAD_DIM // 6
    widths = (HEAD_DIM - 4 * part_width, 2 * part_width, 2 * part_width)
    angle_list = []
    for axis_number in range(3):
        exponent = jnp.arange(0, widths[axis_number], 2, dtype=jnp.float32) / widths[axis_number]
        frequency = 1.0 / 10000.0**exponent
        angle_list.append(positions[axis_number].astype(jnp.float32)[:, None] * frequency[None, :])
    angle_all = jnp.concatenate(angle_list, axis=1)
    return (jnp.cos(angle_all), jnp.sin(angle_all))


def rotate_pairs(field, cosine, sine):
    even_part = field[..., 0::2]
    odd_part = field[..., 1::2]
    cos_wide = cosine[:, None, :]
    sin_wide = sine[:, None, :]
    new_even = even_part * cos_wide - odd_part * sin_wide
    new_odd = even_part * sin_wide + odd_part * cos_wide
    return jnp.stack([new_even, new_odd], axis=-1).reshape(field.shape)


def empty_state(query_rows, heads_here):
    maxima = jnp.full((heads_here, query_rows), NEG_FILL, jnp.float32)
    totals = jnp.zeros((heads_here, query_rows), jnp.float32)
    weighted = jnp.zeros((heads_here, query_rows, HEAD_DIM), jnp.float32)
    return (maxima, totals, weighted)


def merge_states(first, second):
    largest = jnp.maximum(first[0], second[0])
    first_factor = jnp.exp(first[0] - largest)
    second_factor = jnp.exp(second[0] - largest)
    totals = first[1] * first_factor + second[1] * second_factor
    weighted = first[2] * first_factor[..., None] + second[2] * second_factor[..., None]
    return (largest, totals, weighted)


def block_state(q_heads, seg_q, key_heads, value_heads, seg_k):
    score_scale = 1.0 / math.sqrt(HEAD_DIM)
    scores = (
        jnp.einsum("qhd,khd->hqk", q_heads, key_heads, preferred_element_type=jnp.float32)
        * score_scale
    )
    same_seg = seg_q[:, None] == seg_k[None, :]
    masked = jnp.where(same_seg[None], scores, NEG_FILL)
    maxima = jnp.max(masked, axis=2)
    weights = jnp.where(same_seg[None], jnp.exp(masked - maxima[..., None]), 0.0)
    totals = jnp.sum(weights, axis=2)
    weighted = jnp.einsum(
        "hqk,khd->hqd",
        weights.astype(jnp.bfloat16),
        value_heads,
        preferred_element_type=jnp.float32,
    )
    return (maxima, totals, weighted)


def absorb_keys(carry_state, q_heads, seg_q, key_rows, value_rows, seg_k):
    row_count = key_rows.shape[0]
    heads_here = q_heads.shape[1]
    block_rows = 512
    block_count = row_count // block_rows
    key_blocks = key_rows.reshape(block_count, block_rows, heads_here, HEAD_DIM)
    value_blocks = value_rows.reshape(block_count, block_rows, heads_here, HEAD_DIM)
    seg_blocks = seg_k.reshape(block_count, block_rows)

    def step_block(state_now, operands):
        key_block, value_block, seg_block = operands
        return (
            merge_states(state_now, block_state(q_heads, seg_q, key_block, value_block, seg_block)),
            None,
        )

    return lax.scan(step_block, carry_state, (key_blocks, value_blocks, seg_blocks))[0]


def body(hidden_in, seg_ids, positions, mod_table, w_qkv, q_gain, k_gain, w_out):
    tok_rows, feat_local = hidden_in.shape
    model_width = feat_local * lax.axis_size("tp")
    heads_width = w_qkv.shape[2]
    heads_here = heads_width // HEAD_DIM
    all_heads_width = heads_width * lax.axis_size("tp")
    x_float = hidden_in.astype(jnp.float32)
    row_sums, row_squares = lax.psum(
        (jnp.sum(x_float, axis=1), jnp.sum(x_float * x_float, axis=1)), "tp"
    )
    mean_value = row_sums / model_width
    variance = row_squares / model_width - mean_value * mean_value
    normed = (x_float - mean_value[:, None]) * lax.rsqrt(variance[:, None] + EPSILON)
    segment_count = mod_table.shape[0]
    table = mod_table.reshape(segment_count, 3 * feat_local)
    onehot = (seg_ids[:, None] == jnp.arange(segment_count, dtype=jnp.int32)[None, :]).astype(
        jnp.float32
    )
    modulation = jnp.dot(onehot, table, precision=lax.Precision.HIGHEST).reshape(
        tok_rows, 3, feat_local
    )
    modded = (normed * (1.0 + modulation[:, 1]) + modulation[:, 0]).astype(jnp.bfloat16)
    full_rows = lax.all_gather(modded, "tp", axis=1, tiled=True)
    portion = lax.all_gather(w_qkv, "seq", axis=0, tiled=True)
    flat = portion.reshape(portion.shape[0], 3 * heads_width)
    projected = jnp.dot(full_rows, flat, preferred_element_type=jnp.float32)
    query_f = projected[:, :heads_width]
    key_f = projected[:, heads_width : 2 * heads_width]
    value_f = projected[:, 2 * heads_width :]
    query_sq, key_sq = lax.psum(
        (jnp.sum(query_f * query_f, axis=1), jnp.sum(key_f * key_f, axis=1)), "tp"
    )
    query_n = query_f * lax.rsqrt(query_sq / all_heads_width + EPSILON)[:, None] * q_gain[None, :]
    key_n = key_f * lax.rsqrt(key_sq / all_heads_width + EPSILON)[:, None] * k_gain[None, :]
    cosine, sine = rope_tables(positions)
    q_heads = rotate_pairs(query_n.reshape(tok_rows, heads_here, HEAD_DIM), cosine, sine).astype(
        jnp.bfloat16
    )
    k_heads = rotate_pairs(key_n.reshape(tok_rows, heads_here, HEAD_DIM), cosine, sine).astype(
        jnp.bfloat16
    )
    k_cache = k_heads.reshape(tok_rows, heads_width)
    v_cache = value_f.astype(jnp.bfloat16)
    key_rows = lax.all_gather(k_cache, "seq", axis=0, tiled=True)
    value_rows = lax.all_gather(v_cache, "seq", axis=0, tiled=True)
    seg_k = lax.all_gather(seg_ids, "seq", axis=0, tiled=True)
    state_end = absorb_keys(
        empty_state(tok_rows, heads_here), q_heads, seg_ids, key_rows, value_rows, seg_k
    )
    attention = (state_end[2] / state_end[1][..., None]).transpose(1, 0, 2)
    attn_out = attention.reshape(tok_rows, heads_width).astype(jnp.bfloat16)
    terms = jnp.dot(
        attn_out,
        lax.all_gather(w_out, "seq", axis=1, tiled=True),
        preferred_element_type=jnp.float32,
    )
    mixed = lax.psum_scatter(
        terms.astype(jnp.bfloat16), "tp", scatter_dimension=1, tiled=True
    ).astype(jnp.float32)
    hidden_out = (x_float + modulation[:, 2] * mixed).astype(jnp.bfloat16)
    return (hidden_out, k_cache, v_cache)


MESH = pl.DeviceIdType.MESH
EXACT = lax.Precision.HIGHEST
FAR = -1e30
CHUNKS = 4


def dot00(a, b):
    return lax.dot_general(
        a, b, (((0,), (0,)), ((), ())), precision=EXACT, preferred_element_type=jnp.float32
    )


def dot11(a, b, precision=None):
    return lax.dot_general(
        a, b, (((1,), (1,)), ((), ())), precision=precision, preferred_element_type=jnp.float32
    )


def fused(
    n_seq, n_tp, width, all_heads,
    hid, segs, positions, modt, freq, w_any, q_gain, k_gain, w_out_any,
    out, k_out, v_out,
    w, w_out, mod8, meta_all, st1, gathered, full, part, relay, parts_in, parts_last,
    st2, st3, qkv, cosine, sine, q_ext, k_ext, v_all, attn, terms, pair_in, summed, moved,
    arrived, joint, joined, part_v, relay_v, v_in, v_last, gate,
    w_sem, j_r, pv_s, pv_r, lv_s, lv_r, meta_s, meta_r, st1_s, st1_r, z_s, z_r, f_s, f_r, swap_s, swap_r, p_s, p_r,
    last_s, last_r, st2_s, st2_r, st3_s, st3_r, k_s, k_r, v_s, v_r, a_s, a_r, pair_s, pair_r,
    mv_s, mv_r, ar_s, ar_r,
):
    s = lax.axis_index("seq")
    t = lax.axis_index("tp")
    z = t // 2
    c = t % 2
    rows, feats = hid.shape
    n_z = n_tp // 2
    chunks = CHUNKS
    cr = rows // chunks
    many = n_seq * cr
    sibling = z * 2 + 1 - c
    x_next = (s // 2) * 2 + 1 - s % 2
    y_next = (1 - s // 2) * 2 + s % 2
    corner = (1 - s // 2) * 2 + 1 - s % 2

    def copy(src, dst, send, recv, to_s, to_t):
        return pltpu.make_async_remote_copy(
            src_ref=src, dst_ref=dst, send_sem=send, recv_sem=recv,
            device_id=(to_s, to_t), device_id_type=MESH,
        )

    def chunk(i):
        return pl.ds(pl.multiple_of(i * cr, cr), cr)

    def lanes_of(h):
        return pl.ds(pl.multiple_of(h * 128, 128), 128)

    plane = [(s + d) % n_seq for d in range(1, n_seq)]
    column = [(t + d) % n_tp for d in range(1, n_tp)]
    line = [(z + jnp.where(z < n_z // 2, d, n_z - d)) % n_z for d in range(1, n_z)]

    def apart(p):
        return (p + z == n_z - 1) & (p * z == 0)

    def between(p):
        return ((z == n_z - 2) & (p == 0)) | ((z == 1) & (p == n_z - 1))

    barrier = pltpu.get_barrier_semaphore()
    for p in plane:
        pl.semaphore_signal(barrier, inc=1, device_id=(p, t), device_id_type=MESH)
    for p in column:
        pl.semaphore_signal(barrier, inc=1, device_id=(s, p), device_id_type=MESH)
    load_w = pltpu.make_async_copy(w_any, w, w_sem.at[0])
    load_w_out = pltpu.make_async_copy(w_out_any, w_out, w_sem.at[1])
    load_w.start()
    load_w_out.start()

    x = hid[...].astype(jnp.float32)
    row8 = lax.broadcasted_iota(jnp.int32, (8, rows), 0)
    ones_b = jnp.ones((8, feats), jnp.bfloat16)
    ones_f = jnp.ones((8, feats), jnp.float32)
    st1[t] = jnp.where(row8 == 0, dot11(ones_b, hid[...]), dot11(ones_f, x * x, EXACT))
    meta_all[s] = jnp.zeros((8, rows), jnp.float32)
    meta_all[s, 0:3] = positions[...].astype(jnp.float32)
    meta_all[s, 3:4] = segs[...].astype(jnp.float32)
    pl.semaphore_wait(barrier, n_seq - 1 + n_tp - 1)
    for p in column:
        copy(st1.at[t], st1.at[t], st1_s.at[p], st1_r.at[t], s, p).start()
    for p in plane:
        copy(meta_all.at[s], meta_all.at[s], meta_s.at[p], meta_r.at[s], p, t).start()

    onehot = (segs[...] == row8).astype(jnp.float32)
    mod8[...] = jnp.zeros(mod8.shape, jnp.float32)
    mod8[:, : modt.shape[1]] = modt[...]
    shift = dot00(onehot, mod8[0])
    scale = dot00(onehot, mod8[1])
    gate[...] = dot00(onehot, mod8[2])

    for p in column:
        copy(st1.at[p], st1.at[p], st1_s.at[p], st1_r.at[p], s, p).wait_recv()
    totals = jnp.sum(st1[...], axis=0)
    mean_row = totals[0:1] / width
    scale_row = lax.rsqrt(totals[1:2] / width - mean_row * mean_row + EPSILON)
    both = jnp.where(row8 == 0, mean_row, jnp.where(row8 == 1, scale_row, 0.0))
    pick = lax.broadcasted_iota(jnp.int32, (8, 128), 0)
    mean_col = dot00(both, (pick == 0).astype(jnp.float32))[:, 0:1]
    scale_col = dot00(both, (pick == 1).astype(jnp.float32))[:, 0:1]
    normed = (x - mean_col) * scale_col
    gathered[z] = (normed * (1.0 + scale) + shift).astype(jnp.bfloat16)

    def own_block(i, p):
        mine = gathered.at[z, chunk(i)]
        return copy(mine, mine, z_s.at[i, p], z_r.at[i, z], s, p * 2 + c)

    def block_on(i, p):
        theirs = gathered.at[p, chunk(i)]
        return copy(theirs, theirs, z_s.at[i, z], z_r.at[i, p], s, (n_z - 1 - p) * 2 + c)

    for i in range(chunks):
        for p in line:
            @pl.when(jnp.logical_not(apart(p)))
            def _():
                own_block(i, p).start()

    for p in plane:
        copy(meta_all.at[p], meta_all.at[p], meta_s.at[p], meta_r.at[p], p, t).wait_recv()
    lane = lax.broadcasted_iota(jnp.int32, (rows, 128), 1)
    even = lane % 2 == 0

    def pass_on(i, p):
        @pl.when(p == s)
        def _():
            full[c, s, chunk(i)] = gathered[p, chunk(i)]

        @pl.when(p != s)
        def _():
            copy(
                gathered.at[p, chunk(i)], full.at[c, s, chunk(i)], f_s.at[i, p], f_r.at[i, s], p, t
            ).start()

    def from_line(i):
        pass_on(i, z)
        for p in line:
            theirs = gathered.at[p, chunk(i)]
            copy(theirs, theirs, z_s.at[i, p], z_r.at[i, p], s, p * 2 + c).wait_recv()

            @pl.when(between(p))
            def _():
                block_on(i, p).start()

            pass_on(i, p)

    def swap(i, half):
        block = full.at[half, :, chunk(i)]
        return copy(block, block, swap_s.at[i], swap_r.at[i], s, sibling)

    def from_plane(i):
        for p in plane:
            theirs = full.at[c, p, chunk(i)]
            copy(theirs, theirs, f_s.at[i, p], f_r.at[i, p], p, t).wait_recv()
        swap(i, c).start()

    def tables(j):
        block = meta_all[j]
        angle = dot00(block, freq[...])
        cosine[:, j] = jnp.cos(angle).reshape(chunks, cr, 128)
        sine[:, j] = (jnp.where(even, -1.0, 1.0) * jnp.sin(angle)).reshape(chunks, cr, 128)
        seg = dot00(block, (pick == 3).astype(jnp.float32))
        same = seg == lane.astype(jnp.float32)
        q_mask = same.astype(jnp.float32).astype(jnp.bfloat16)
        k_mask = jnp.where(same | (lane >= 8), 0.0, FAR).astype(jnp.bfloat16)
        q_ext[:, j, :, 128:] = q_mask.reshape(chunks, cr, 128)
        k_ext[:, j, :, 128:] = k_mask.reshape(chunks, cr, 128)

    def first_of(i):
        return jnp.where(i % 2 == 0, x_next, y_next)

    def second_of(i):
        return jnp.where(i % 2 == 0, y_next, x_next)

    qk_bufs = (part, parts_in, relay, parts_last, p_s, p_r, last_s, last_r)
    v_bufs = (part_v, v_in, relay_v, v_last, pv_s, pv_r, lv_s, lv_r)

    def to_first(bufs, i, n, h):
        own, got, _, _, send, recv, _, _ = bufs
        return copy(own.at[i, h], got.at[i, n], send.at[i, n], recv.at[i, n], first_of(i), t)

    def to_second(bufs, i):
        _, _, passed, got, _, _, send, recv = bufs
        return copy(passed.at[i], got.at[i], send.at[i], recv.at[i], second_of(i), t)

    def project(bufs, fields, i):
        left = full[0, :, chunk(i)].reshape(many, feats)
        right = full[1, :, chunk(i)].reshape(many, feats)
        for at, n in enumerate(fields):
            acc = jnp.dot(left, w[n, :feats], preferred_element_type=jnp.float32)
            acc += jnp.dot(right, w[n, feats:], preferred_element_type=jnp.float32)
            for h in range(n_seq):
                bufs[0][i, h, :, at * 128 : (at + 1) * 128] = acc[
                    :, h * 128 : (h + 1) * 128
                ].astype(jnp.bfloat16)
        to_first(bufs, i, 1, corner).start()
        to_first(bufs, i, 0, first_of(i)).start()

    def project_qk(i):
        swap(i, 1 - c).wait_recv()
        project(qk_bufs, (0, 1), i)

    def project_v(i):
        project(v_bufs, (2,), i)

    def relay_on(bufs, i):
        own, got, passed = bufs[:3]
        to_first(bufs, i, 1, corner).wait_recv()
        passed[i] = (
            own[i, second_of(i)].astype(jnp.float32) + got[i, 1].astype(jnp.float32)
        ).astype(jnp.bfloat16)
        to_second(bufs, i).start()

    def summed_head(bufs, i):
        own, got, _, last = bufs[:4]
        to_first(bufs, i, 0, corner).wait_recv()
        to_second(bufs, i).wait_recv()
        total = own[i, s].astype(jnp.float32) + got[i, 0].astype(jnp.float32)
        return total + last[i].astype(jnp.float32)

    ones_h = jnp.ones((8, 128), jnp.float32)
    st2[s] = jnp.zeros((8, rows), jnp.float32)

    def collect(i):
        total = summed_head(qk_bufs, i)
        qkv[i] = total
        q_sq = dot11(ones_h, total[:, :128] * total[:, :128], EXACT)
        k_sq = dot11(ones_h, total[:, 128:256] * total[:, 128:256], EXACT)
        st2[s] = jnp.where(row8 == 2 * i, q_sq, jnp.where(row8 == 2 * i + 1, k_sq, st2[s]))

    def collect_v(i, carry):
        v_all[i] = summed_head(v_bufs, i).astype(jnp.bfloat16).reshape(n_seq, cr, 128)
        return carry

    load_w.wait()
    load_w_out.wait()

    def during(step, at, work):
        @pl.when((step >= at) & (step < at + chunks))
        def _():
            work(step - at)

    def project_step(step, carry):
        during(step, 0, from_line)
        during(step, 1, project_qk)
        during(step, 2, functools.partial(relay_on, qk_bufs))
        during(step, 0, from_plane)
        during(step, 0, tables)
        during(step, 3, project_v)
        during(step, 3, collect)
        return carry

    lax.fori_loop(0, chunks + 3, project_step, 0)

    for p in plane:
        copy(st2.at[s], st2.at[s], st2_s.at[p], st2_r.at[s], p, t).start()

    def relay_v_on(i, carry):
        relay_on(v_bufs, i)
        return carry

    lax.fori_loop(0, chunks, relay_v_on, 0)

    gains = (q_gain[pl.ds(s, 1), :], k_gain[pl.ds(s, 1), :])

    def rotate(i, carry):
        cos_i = cosine[i].reshape(many, 128)
        sin_i = sine[i].reshape(many, 128)
        for n in range(2):
            cols = slice(n * 128, (n + 1) * 128)
            field = qkv[i, :, cols] * gains[n]
            swapped = jnp.where(even, pltpu.roll(field, 127, 1), pltpu.roll(field, 1, 1))
            qkv[i, :, cols] = field * cos_i + swapped * sin_i
        return carry

    for p in plane:
        copy(st2.at[p], st2.at[p], st2_s.at[p], st2_r.at[p], p, t).wait_recv()
    st3[t] = jnp.sum(st2[...], axis=0)
    for p in column:
        copy(st3.at[t], st3.at[t], st3_s.at[p], st3_r.at[t], s, p).start()

    def send_v(p):
        return copy(v_all.at[:, p], v_out.at[:, :, lanes_of(s)], v_s.at[p], v_r.at[s], p, t)

    def send_k(p):
        mine = k_ext.at[:, p, :, pl.ds(0, 128)]
        return copy(mine, k_out.at[:, :, lanes_of(s)], k_s.at[p], k_r.at[s], p, t)

    lax.fori_loop(0, chunks, rotate, 0)
    lax.fori_loop(0, chunks, collect_v, 0)
    for p in column:
        copy(st3.at[p], st3.at[p], st3_s.at[p], st3_r.at[p], s, p).wait_recv()
    norm_rows = lax.rsqrt(jnp.sum(st3[...], axis=0) / all_heads + EPSILON)

    def scale_rows(i, carry):
        q_col = dot00(norm_rows, (pick == 2 * i).astype(jnp.float32))
        k_col = dot00(norm_rows, (pick == 2 * i + 1).astype(jnp.float32))
        q_i = (qkv[i, :, :128] * q_col).astype(jnp.bfloat16)
        k_i = (qkv[i, :, 128:256] * k_col).astype(jnp.bfloat16)
        q_ext[i, :, :, :128] = q_i.reshape(n_seq, cr, 128)
        k_ext[i, :, :, :128] = k_i.reshape(n_seq, cr, 128)
        return carry

    lax.fori_loop(0, chunks, scale_rows, 0)

    score_scale = 1.0 / math.sqrt(HEAD_DIM)

    def attend(i):
        keys = k_ext[...].reshape(n_seq * rows, 256)
        values = v_all[...].reshape(n_seq * rows, 128)
        scores = dot11(q_ext[i].reshape(many, 256), keys)
        top = jnp.max(scores, axis=1, keepdims=True)
        weights = jnp.exp((scores - top) * score_scale)
        denominator = jnp.sum(weights, axis=1, keepdims=True)
        mixed = jnp.dot(weights.astype(jnp.bfloat16), values, preferred_element_type=jnp.float32)
        done = (mixed / denominator).astype(jnp.bfloat16)
        attn[i, :, :, lanes_of(s)] = done.reshape(n_seq, cr, 128)
        for p in plane:
            mine = attn.at[i, :, :, lanes_of(s)]
            copy(mine, mine, a_s.at[i, p], a_r.at[i, s], p, t).start()

    def pair(i):
        return copy(
            terms.at[i, 1 - c], pair_in.at[i], pair_s.at[i], pair_r.at[i], s, sibling
        )

    def out_project(i):
        for p in plane:
            theirs = attn.at[i, :, :, lanes_of(p)]
            copy(theirs, theirs, a_s.at[i, p], a_r.at[i, p], p, t).wait_recv()
        for n in range(2):
            cols = slice(n * feats, (n + 1) * feats)
            product = jnp.dot(
                attn[i].reshape(many, n_seq * 128), w_out[:, cols],
                preferred_element_type=jnp.float32,
            )
            terms[i, n] = product.astype(jnp.bfloat16).reshape(n_seq, cr, feats)
        pair(i).start()

    def pair_sum(i):
        pair(i).wait_recv()
        summed[i] = (terms[i, c].astype(jnp.float32) + pair_in[i].astype(jnp.float32)).astype(
            jnp.bfloat16
        )
        moved[s, i] = summed[i, s]
        for p in plane:
            copy(summed.at[i, p], moved.at[s, i], mv_s.at[i, p], mv_r.at[i, s], p, t).start()

    def to_line(i, p):
        return copy(
            moved.at[p, i], arrived.at[z, i], ar_s.at[i, p], ar_r.at[i, z], s, p * 2 + c
        )

    def to_joint(i, p):
        via = jnp.where(z == 0, 1, n_z - 2)
        return copy(moved.at[p, i], joint.at[i], ar_s.at[i, p], j_r.at[i], s, via * 2 + c)

    def deliver(i, p):
        @pl.when(p == z)
        def _():
            arrived[z, i] = moved[p, i]

        @pl.when(apart(p))
        def _():
            to_joint(i, p).start()
            arrived[p, i] = jnp.zeros((cr, feats), jnp.bfloat16)

        @pl.when((p != z) & jnp.logical_not(apart(p)) & jnp.logical_not(between(p)))
        def _():
            to_line(i, p).start()

    def join(i):
        @pl.when((z > 0) & (z < n_z - 1))
        def _():
            p = jnp.where(z == 1, n_z - 1, 0)
            to_joint(i, p).wait_recv()
            joined[i] = (
                moved[p, i].astype(jnp.float32) + joint[i].astype(jnp.float32)
            ).astype(jnp.bfloat16)
            copy(
                joined.at[i], arrived.at[z, i], ar_s.at[i, p], ar_r.at[i, z], s, p * 2 + c
            ).start()

    def deliver_all(i):
        deliver(i, s)
        for p in plane:
            theirs = moved.at[p, i]
            copy(theirs, theirs, mv_s.at[i, p], mv_r.at[i, p], p, t).wait_recv()
            deliver(i, p)

    def attend_step(step, carry):
        during(step, 0, attend)
        during(step, 1, out_project)
        during(step, 3, join)
        during(step, 2, deliver_all)
        during(step, 1, pair_sum)
        return carry

    lax.fori_loop(0, chunks + 3, attend_step, 0)
    for p in plane:
        send_k(p).start()
        send_v(p).start()
    k_out[:, :, lanes_of(s)] = k_ext[:, s, :, :128]
    v_out[:, :, lanes_of(s)] = v_all[:, s]

    def finish(i, carry):
        for p in line:
            theirs = arrived.at[p, i]

            @pl.when(jnp.logical_not(apart(p)))
            def _():
                copy(theirs, theirs, ar_s.at[i, p], ar_r.at[i, p], s, p * 2 + c).wait_recv()

        mixed = arrived[0, i].astype(jnp.float32)
        for p in range(1, n_z):
            mixed += arrived[p, i].astype(jnp.float32)
        base = hid[chunk(i), :].astype(jnp.float32)
        out[chunk(i), :] = (base + gate[chunk(i), :] * mixed).astype(jnp.bfloat16)
        return carry

    lax.fori_loop(0, chunks, finish, 0)

    for p in plane:
        copy(
            k_ext.at[:, p, :, pl.ds(0, 128)], k_out.at[:, :, lanes_of(p)], k_s.at[p], k_r.at[p], p, t
        ).wait()
        copy(v_all.at[:, p], v_out.at[:, :, lanes_of(p)], v_s.at[p], v_r.at[p], p, t).wait()
        copy(meta_all.at[s], meta_all.at[s], meta_s.at[p], meta_r.at[s], p, t).wait_send()
        copy(st2.at[s], st2.at[s], st2_s.at[p], st2_r.at[s], p, t).wait_send()
    for p in column:
        copy(st1.at[t], st1.at[t], st1_s.at[p], st1_r.at[t], s, p).wait_send()
        copy(st3.at[t], st3.at[t], st3_s.at[p], st3_r.at[t], s, p).wait_send()

    def drain(i, carry):
        swap(i, c).wait_send()
        pair(i).wait_send()
        for bufs in (qk_bufs, v_bufs):
            to_first(bufs, i, 0, first_of(i)).wait_send()
            to_first(bufs, i, 1, corner).wait_send()
            to_second(bufs, i).wait_send()
        for p in line:
            @pl.when(jnp.logical_not(apart(p)))
            def _():
                own_block(i, p).wait_send()

            @pl.when(between(p))
            def _():
                block_on(i, p).wait_send()

            to_line(i, p).wait_send()
        for p in plane:
            copy(
                gathered.at[p, chunk(i)], full.at[c, s, chunk(i)], f_s.at[i, p], f_r.at[i, s], p, t
            ).wait_send()
            mine = attn.at[i, :, :, lanes_of(s)]
            copy(mine, mine, a_s.at[i, p], a_r.at[i, s], p, t).wait_send()
            copy(summed.at[i, p], moved.at[s, i], mv_s.at[i, p], mv_r.at[i, s], p, t).wait_send()
        return carry

    lax.fori_loop(0, chunks, drain, 0)


def hand_over(*refs):
    for i in range(3):
        refs[3 + i][...] = refs[i][...]


def frequencies():
    part_width = HEAD_DIM // 6
    widths = (HEAD_DIM - 4 * part_width, 2 * part_width, 2 * part_width)
    table = np.zeros((8, HEAD_DIM), np.float32)
    at = 0
    for axis_number, wide in enumerate(widths):
        exponent = np.arange(0, wide, 2, dtype=np.float32) / np.float32(wide)
        frequency = (1.0 / np.float32(10000.0) ** exponent).astype(np.float32)
        table[axis_number, at : at + wide] = np.repeat(frequency, 2)
        at += wide
    return table


def fused_body(hidden_in, seg_ids, positions, mod_table, w_qkv, q_gain, k_gain, w_out):
    n_seq = lax.axis_size("seq")
    n_tp = lax.axis_size("tp")
    rows, feats = hidden_in.shape
    depth, _, heads_width = w_qkv.shape
    bf16, f32 = jnp.bfloat16, jnp.float32
    n_z = n_tp // 2
    chunks = CHUNKS
    cr = rows // chunks
    many = n_seq * cr
    dma = pltpu.SemaphoreType.DMA
    scratch = [
        pltpu.VMEM((3, depth, heads_width), bf16),
        pltpu.VMEM(w_out.shape, bf16),
        pltpu.VMEM((3, 8, feats), f32),
        pltpu.VMEM((n_seq, 8, rows), f32),
        pltpu.VMEM((n_tp, 8, rows), f32),
        pltpu.VMEM((n_z, rows, feats), bf16),
        pltpu.VMEM((2, n_seq, rows, feats), bf16),
        pltpu.VMEM((chunks, n_seq, many, 256), bf16),
        pltpu.VMEM((chunks, many, 256), bf16),
        pltpu.VMEM((chunks, 2, many, 256), bf16),
        pltpu.VMEM((chunks, many, 256), bf16),
        pltpu.VMEM((n_seq, 8, rows), f32),
        pltpu.VMEM((n_tp, 8, rows), f32),
        pltpu.VMEM((chunks, many, 256), f32),
        pltpu.VMEM((chunks, n_seq, cr, 128), f32),
        pltpu.VMEM((chunks, n_seq, cr, 128), f32),
        pltpu.VMEM((chunks, n_seq, cr, 256), bf16),
        pltpu.VMEM((chunks, n_seq, cr, 256), bf16),
        pltpu.VMEM((chunks, n_seq, cr, 128), bf16),
        pltpu.VMEM((chunks, n_seq, cr, heads_width), bf16),
        pltpu.VMEM((chunks, 2, n_seq, cr, feats), bf16),
        pltpu.VMEM((chunks, n_seq, cr, feats), bf16),
        pltpu.VMEM((chunks, n_seq, cr, feats), bf16),
        pltpu.VMEM((n_seq, chunks, cr, feats), bf16),
        pltpu.VMEM((n_z, chunks, cr, feats), bf16),
        pltpu.VMEM((chunks, cr, feats), bf16),
        pltpu.VMEM((chunks, cr, feats), bf16),
        pltpu.VMEM((chunks, n_seq, many, 128), bf16),
        pltpu.VMEM((chunks, many, 128), bf16),
        pltpu.VMEM((chunks, 2, many, 128), bf16),
        pltpu.VMEM((chunks, many, 128), bf16),
        pltpu.VMEM((rows, feats), f32),
        dma((2,)),
        dma((chunks,)),
        dma((chunks, 2)),
        dma((chunks, 2)),
        dma((chunks,)),
        dma((chunks,)),
    ]
    wide = (chunks, n_seq)
    shapes = [
        (n_seq,), (n_tp,), (chunks, n_z), wide, (chunks,), (chunks, 2), (chunks,),
        (n_seq,), (n_tp,), (n_seq,), (n_seq,), wide, (chunks,), wide, (chunks, n_z),
    ]
    for shape in shapes:
        scratch += [dma(shape), dma(shape)]
    vmem = pl.BlockSpec(memory_space=pltpu.VMEM)
    whole = pl.BlockSpec(memory_space=pl.ANY)
    results = pl.pallas_call(
        functools.partial(fused, n_seq, n_tp, feats * n_tp, heads_width * n_tp),
        out_shape=(
            jax.ShapeDtypeStruct((rows, feats), bf16),
            jax.ShapeDtypeStruct((chunks, cr, heads_width), bf16),
            jax.ShapeDtypeStruct((chunks, cr, heads_width), bf16),
        ),
        in_specs=[vmem, vmem, vmem, vmem, vmem, whole, vmem, vmem, whole],
        out_specs=(vmem, vmem, vmem),
        scratch_shapes=scratch,
        compiler_params=pltpu.CompilerParams(
            collective_id=0, has_side_effects=True, vmem_limit_bytes=58 * 1024 * 1024
        ),
        cost_estimate=pl.CostEstimate(
            flops=6_000_000_000, bytes_accessed=8_000_000, transcendentals=1_200_000
        ),
    )(
        hidden_in, seg_ids.reshape(1, rows), positions, mod_table.transpose(1, 0, 2),
        jnp.asarray(frequencies()), w_qkv.transpose(1, 0, 2),
        q_gain.reshape(n_seq, HEAD_DIM), k_gain.reshape(n_seq, HEAD_DIM), w_out,
    )
    hidden, k_cache, v_cache = pl.pallas_call(
        hand_over,
        out_shape=tuple(jax.ShapeDtypeStruct(r.shape, r.dtype) for r in results),
        in_specs=[vmem] * 3,
        out_specs=(vmem,) * 3,
        cost_estimate=pl.CostEstimate(flops=0, bytes_accessed=1_700_000, transcendentals=0),
    )(*results)
    return (
        hidden,
        k_cache.reshape(rows, heads_width),
        v_cache.reshape(rows, heads_width),
    )


def pick_body(*operands):
    hidden_in, seg_ids, positions, mod_table, w_qkv = operands[:5]
    n_seq, n_tp = lax.axis_size("seq"), lax.axis_size("tp")
    fits = (
        n_tp == 2 * n_seq
        and n_seq == 4
        and w_qkv.shape[2] == n_seq * HEAD_DIM
        and w_qkv.shape[0] == 2 * hidden_in.shape[1]
        and hidden_in.shape[0] == 256
        and mod_table.shape[0] <= 8
    )
    return (fused_body if fits else body)(*operands)


def solution(mesh):
    in_specs = (
        P("seq", "tp"),
        P("seq"),
        P(None, "seq"),
        P(None, None, "tp"),
        P("seq", None, "tp"),
        P("tp"),
        P("tp"),
        P("tp", "seq"),
    )
    out_specs = (P("seq", "tp"), P("seq", "tp"), P("seq", "tp"))
    return jax.shard_map(pick_body, mesh=mesh, in_specs=in_specs, out_specs=out_specs, check_vma=False)
```

```python
import functools
import math

import jax
import jax.numpy as jnp
import numpy as np
from jax import lax
from jax.experimental import pallas as pl
from jax.experimental.pallas import tpu as pltpu
from jax.sharding import PartitionSpec as P

HEAD_DIM = 128


EPSILON = 1e-06
NEG_FILL = -1e30


def rope_tables(positions):
    part_width = HEAD_DIM // 6
    widths = (HEAD_DIM - 4 * part_width, 2 * part_width, 2 * part_width)
    angle_list = []
    for axis_number in range(3):
        exponent = jnp.arange(0, widths[axis_number], 2, dtype=jnp.float32) / widths[axis_number]
        frequency = 1.0 / 10000.0**exponent
        angle_list.append(positions[axis_number].astype(jnp.float32)[:, None] * frequency[None, :])
    angle_all = jnp.concatenate(angle_list, axis=1)
    return (jnp.cos(angle_all), jnp.sin(angle_all))


def rotate_pairs(field, cosine, sine):
    even_part = field[..., 0::2]
    odd_part = field[..., 1::2]
    cos_wide = cosine[:, None, :]
    sin_wide = sine[:, None, :]
    new_even = even_part * cos_wide - odd_part * sin_wide
    new_odd = even_part * sin_wide + odd_part * cos_wide
    return jnp.stack([new_even, new_odd], axis=-1).reshape(field.shape)


def empty_state(query_rows, heads_here):
    maxima = jnp.full((heads_here, query_rows), NEG_FILL, jnp.float32)
    totals = jnp.zeros((heads_here, query_rows), jnp.float32)
    weighted = jnp.zeros((heads_here, query_rows, HEAD_DIM), jnp.float32)
    return (maxima, totals, weighted)


def merge_states(first, second):
    largest = jnp.maximum(first[0], second[0])
    first_factor = jnp.exp(first[0] - largest)
    second_factor = jnp.exp(second[0] - largest)
    totals = first[1] * first_factor + second[1] * second_factor
    weighted = first[2] * first_factor[..., None] + second[2] * second_factor[..., None]
    return (largest, totals, weighted)


def block_state(q_heads, seg_q, key_heads, value_heads, seg_k):
    score_scale = 1.0 / math.sqrt(HEAD_DIM)
    scores = (
        jnp.einsum("qhd,khd->hqk", q_heads, key_heads, preferred_element_type=jnp.float32)
        * score_scale
    )
    same_seg = seg_q[:, None] == seg_k[None, :]
    masked = jnp.where(same_seg[None], scores, NEG_FILL)
    maxima = jnp.max(masked, axis=2)
    weights = jnp.where(same_seg[None], jnp.exp(masked - maxima[..., None]), 0.0)
    totals = jnp.sum(weights, axis=2)
    weighted = jnp.einsum(
        "hqk,khd->hqd",
        weights.astype(jnp.bfloat16),
        value_heads,
        preferred_element_type=jnp.float32,
    )
    return (maxima, totals, weighted)


def absorb_keys(carry_state, q_heads, seg_q, key_rows, value_rows, seg_k):
    row_count = key_rows.shape[0]
    heads_here = q_heads.shape[1]
    block_rows = 512
    block_count = row_count // block_rows
    key_blocks = key_rows.reshape(block_count, block_rows, heads_here, HEAD_DIM)
    value_blocks = value_rows.reshape(block_count, block_rows, heads_here, HEAD_DIM)
    seg_blocks = seg_k.reshape(block_count, block_rows)

    def step_block(state_now, operands):
        key_block, value_block, seg_block = operands
        return (
            merge_states(state_now, block_state(q_heads, seg_q, key_block, value_block, seg_block)),
            None,
        )

    return lax.scan(step_block, carry_state, (key_blocks, value_blocks, seg_blocks))[0]


def body(hidden_in, seg_ids, positions, mod_table, w_qkv, q_gain, k_gain, w_out):
    tok_rows, feat_local = hidden_in.shape
    model_width = feat_local * lax.axis_size("tp")
    heads_width = w_qkv.shape[2]
    heads_here = heads_width // HEAD_DIM
    all_heads_width = heads_width * lax.axis_size("tp")
    x_float = hidden_in.astype(jnp.float32)
    row_sums, row_squares = lax.psum(
        (jnp.sum(x_float, axis=1), jnp.sum(x_float * x_float, axis=1)), "tp"
    )
    mean_value = row_sums / model_width
    variance = row_squares / model_width - mean_value * mean_value
    normed = (x_float - mean_value[:, None]) * lax.rsqrt(variance[:, None] + EPSILON)
    segment_count = mod_table.shape[0]
    table = mod_table.reshape(segment_count, 3 * feat_local)
    onehot = (seg_ids[:, None] == jnp.arange(segment_count, dtype=jnp.int32)[None, :]).astype(
        jnp.float32
    )
    modulation = jnp.dot(onehot, table, precision=lax.Precision.HIGHEST).reshape(
        tok_rows, 3, feat_local
    )
    modded = (normed * (1.0 + modulation[:, 1]) + modulation[:, 0]).astype(jnp.bfloat16)
    full_rows = lax.all_gather(modded, "tp", axis=1, tiled=True)
    portion = lax.all_gather(w_qkv, "seq", axis=0, tiled=True)
    flat = portion.reshape(portion.shape[0], 3 * heads_width)
    projected = jnp.dot(full_rows, flat, preferred_element_type=jnp.float32)
    query_f = projected[:, :heads_width]
    key_f = projected[:, heads_width : 2 * heads_width]
    value_f = projected[:, 2 * heads_width :]
    query_sq, key_sq = lax.psum(
        (jnp.sum(query_f * query_f, axis=1), jnp.sum(key_f * key_f, axis=1)), "tp"
    )
    query_n = query_f * lax.rsqrt(query_sq / all_heads_width + EPSILON)[:, None] * q_gain[None, :]
    key_n = key_f * lax.rsqrt(key_sq / all_heads_width + EPSILON)[:, None] * k_gain[None, :]
    cosine, sine = rope_tables(positions)
    q_heads = rotate_pairs(query_n.reshape(tok_rows, heads_here, HEAD_DIM), cosine, sine).astype(
        jnp.bfloat16
    )
    k_heads = rotate_pairs(key_n.reshape(tok_rows, heads_here, HEAD_DIM), cosine, sine).astype(
        jnp.bfloat16
    )
    k_cache = k_heads.reshape(tok_rows, heads_width)
    v_cache = value_f.astype(jnp.bfloat16)
    key_rows = lax.all_gather(k_cache, "seq", axis=0, tiled=True)
    value_rows = lax.all_gather(v_cache, "seq", axis=0, tiled=True)
    seg_k = lax.all_gather(seg_ids, "seq", axis=0, tiled=True)
    state_end = absorb_keys(
        empty_state(tok_rows, heads_here), q_heads, seg_ids, key_rows, value_rows, seg_k
    )
    attention = (state_end[2] / state_end[1][..., None]).transpose(1, 0, 2)
    attn_out = attention.reshape(tok_rows, heads_width).astype(jnp.bfloat16)
    terms = jnp.dot(
        attn_out,
        lax.all_gather(w_out, "seq", axis=1, tiled=True),
        preferred_element_type=jnp.float32,
    )
    mixed = lax.psum_scatter(
        terms.astype(jnp.bfloat16), "tp", scatter_dimension=1, tiled=True
    ).astype(jnp.float32)
    hidden_out = (x_float + modulation[:, 2] * mixed).astype(jnp.bfloat16)
    return (hidden_out, k_cache, v_cache)


MESH = pl.DeviceIdType.MESH
EXACT = lax.Precision.HIGHEST
FAR = -1e30
CHUNKS = 4
PLACES = 64


def dot00(a, b):
    return lax.dot_general(
        a, b, (((0,), (0,)), ((), ())), precision=EXACT, preferred_element_type=jnp.float32
    )


def dot11(a, b, precision=None):
    return lax.dot_general(
        a, b, (((1,), (1,)), ((), ())), precision=precision, preferred_element_type=jnp.float32
    )


def fused(
    n_seq, n_tp, width, all_heads,
    hid, segs, positions, modt, freq, w_any, q_gain, k_gain, w_out_any,
    out, k_out, v_out,
    w, w_out, mod8, meta_all, st1, gathered, full, part, relay, parts_in, parts_last,
    st2, st3, qkv, cosine, sine, q_ext, k_ext, v_all, attn, terms, pair_in, summed, moved,
    arrived, joint, joined, part_v, relay_v, v_in, v_last, lookup, gate,
    w_sem, j_r, pv_s, pv_r, lv_s, lv_r, meta_s, meta_r, st1_s, st1_r, z_s, z_r, f_s, f_r, swap_s, swap_r, p_s, p_r,
    last_s, last_r, st2_s, st2_r, st3_s, st3_r, k_s, k_r, v_s, v_r, a_s, a_r, pair_s, pair_r,
    mv_s, mv_r, ar_s, ar_r,
):
    s = lax.axis_index("seq")
    t = lax.axis_index("tp")
    z = t // 2
    c = t % 2
    rows, feats = hid.shape
    n_z = n_tp // 2
    chunks = CHUNKS
    cr = rows // chunks
    many = n_seq * cr
    sibling = z * 2 + 1 - c
    x_next = (s // 2) * 2 + 1 - s % 2
    y_next = (1 - s // 2) * 2 + s % 2
    corner = (1 - s // 2) * 2 + 1 - s % 2

    def copy(src, dst, send, recv, to_s, to_t):
        return pltpu.make_async_remote_copy(
            src_ref=src, dst_ref=dst, send_sem=send, recv_sem=recv,
            device_id=(to_s, to_t), device_id_type=MESH,
        )

    def chunk(i):
        return pl.ds(pl.multiple_of(i * cr, cr), cr)

    def lanes_of(h):
        return pl.ds(pl.multiple_of(h * 128, 128), 128)

    plane = [(s + d) % n_seq for d in range(1, n_seq)]
    column = [(t + d) % n_tp for d in range(1, n_tp)]
    line = [(z + jnp.where(z < n_z // 2, d, n_z - d)) % n_z for d in range(1, n_z)]

    def apart(p):
        return (p + z == n_z - 1) & (p * z == 0)

    def between(p):
        return ((z == n_z - 2) & (p == 0)) | ((z == 1) & (p == n_z - 1))

    barrier = pltpu.get_barrier_semaphore()
    for p in plane:
        pl.semaphore_signal(barrier, inc=1, device_id=(p, t), device_id_type=MESH)
    for p in column:
        pl.semaphore_signal(barrier, inc=1, device_id=(s, p), device_id_type=MESH)
    load_w = pltpu.make_async_copy(w_any, w, w_sem.at[0])
    load_w_out = pltpu.make_async_copy(w_out_any, w_out, w_sem.at[1])
    load_w.start()
    load_w_out.start()

    x = hid[...].astype(jnp.float32)
    row8 = lax.broadcasted_iota(jnp.int32, (8, rows), 0)
    ones_b = jnp.ones((8, feats), jnp.bfloat16)
    ones_f = jnp.ones((8, feats), jnp.float32)
    st1[t] = jnp.where(row8 == 0, dot11(ones_b, hid[...]), dot11(ones_f, x * x, EXACT))
    meta_all[s] = jnp.zeros((8, rows), jnp.float32)
    meta_all[s, 0:3] = positions[...].astype(jnp.float32)
    meta_all[s, 3:4] = segs[...].astype(jnp.float32)
    pl.semaphore_wait(barrier, n_seq - 1 + n_tp - 1)
    for p in column:
        copy(st1.at[t], st1.at[t], st1_s.at[p], st1_r.at[t], s, p).start()
    for p in plane:
        copy(meta_all.at[s], meta_all.at[s], meta_s.at[p], meta_r.at[s], p, t).start()

    onehot = (segs[...] == row8).astype(jnp.float32)
    mod8[...] = jnp.zeros(mod8.shape, jnp.float32)
    mod8[:, : modt.shape[1]] = modt[...]
    shift = dot00(onehot, mod8[0])
    scale = dot00(onehot, mod8[1])
    gate[...] = dot00(onehot, mod8[2])

    for p in column:
        copy(st1.at[p], st1.at[p], st1_s.at[p], st1_r.at[p], s, p).wait_recv()
    totals = jnp.sum(st1[...], axis=0)
    mean_row = totals[0:1] / width
    scale_row = lax.rsqrt(totals[1:2] / width - mean_row * mean_row + EPSILON)
    both = jnp.where(row8 == 0, mean_row, jnp.where(row8 == 1, scale_row, 0.0))
    pick = lax.broadcasted_iota(jnp.int32, (8, 128), 0)
    mean_col = dot00(both, (pick == 0).astype(jnp.float32))[:, 0:1]
    scale_col = dot00(both, (pick == 1).astype(jnp.float32))[:, 0:1]
    normed = (x - mean_col) * scale_col
    gathered[z] = (normed * (1.0 + scale) + shift).astype(jnp.bfloat16)

    def own_block(i, p):
        mine = gathered.at[z, chunk(i)]
        return copy(mine, mine, z_s.at[i, p], z_r.at[i, z], s, p * 2 + c)

    def block_on(i, p):
        theirs = gathered.at[p, chunk(i)]
        return copy(theirs, theirs, z_s.at[i, z], z_r.at[i, p], s, (n_z - 1 - p) * 2 + c)

    for i in range(chunks):
        for p in line:
            @pl.when(jnp.logical_not(apart(p)))
            def _():
                own_block(i, p).start()

    for p in plane:
        copy(meta_all.at[p], meta_all.at[p], meta_s.at[p], meta_r.at[p], p, t).wait_recv()
    lane = lax.broadcasted_iota(jnp.int32, (rows, 128), 1)
    even = lane % 2 == 0

    def pass_on(i, p):
        @pl.when(p == s)
        def _():
            full[c, s, chunk(i)] = gathered[p, chunk(i)]

        @pl.when(p != s)
        def _():
            copy(
                gathered.at[p, chunk(i)], full.at[c, s, chunk(i)], f_s.at[i, p], f_r.at[i, s], p, t
            ).start()

    def from_line(i):
        pass_on(i, z)
        for p in line:
            theirs = gathered.at[p, chunk(i)]
            copy(theirs, theirs, z_s.at[i, p], z_r.at[i, p], s, p * 2 + c).wait_recv()

            @pl.when(between(p))
            def _():
                block_on(i, p).start()

            pass_on(i, p)

    def swap(i, half):
        block = full.at[half, :, chunk(i)]
        return copy(block, block, swap_s.at[i], swap_r.at[i], s, sibling)

    def from_plane(i):
        for p in plane:
            theirs = full.at[c, p, chunk(i)]
            copy(theirs, theirs, f_s.at[i, p], f_r.at[i, p], p, t).wait_recv()
        swap(i, c).start()

    place_col = lax.broadcasted_iota(jnp.int32, (PLACES, 128), 0).astype(jnp.float32)
    angle = place_col * (freq[0:1, :] + freq[1:2, :] + freq[2:3, :])
    even_col = lax.broadcasted_iota(jnp.int32, (PLACES, 128), 1) % 2 == 0
    cos_all = jnp.cos(angle)
    sin_all = jnp.where(even_col, -1.0, 1.0) * jnp.sin(angle)
    for a in range(3):
        on_axis = freq[a : a + 1, :] > 0.0
        lookup[a * PLACES : (a + 1) * PLACES, :128] = jnp.where(on_axis, cos_all, 0.0)
        lookup[a * PLACES : (a + 1) * PLACES, 128:] = jnp.where(on_axis, sin_all, 0.0)

    def tables(j):
        block = meta_all[j]
        place = lax.broadcasted_iota(jnp.int32, (PLACES, rows), 0).astype(jnp.float32)
        where = [(block[a : a + 1] == place).astype(jnp.float32) for a in range(3)]
        found = dot00(jnp.concatenate(where, axis=0), lookup[...])
        cosine[:, j] = found[:, :128].reshape(chunks, cr, 128)
        sine[:, j] = found[:, 128:].reshape(chunks, cr, 128)
        seg = dot00(block, (pick == 3).astype(jnp.float32))
        same = seg == lane.astype(jnp.float32)
        q_mask = same.astype(jnp.float32).astype(jnp.bfloat16)
        k_mask = jnp.where(same | (lane >= 8), 0.0, FAR).astype(jnp.bfloat16)
        q_ext[:, j, :, 128:] = q_mask.reshape(chunks, cr, 128)
        k_ext[:, j, :, 128:] = k_mask.reshape(chunks, cr, 128)

    def first_of(i):
        return jnp.where(i % 2 == 0, x_next, y_next)

    def second_of(i):
        return jnp.where(i % 2 == 0, y_next, x_next)

    qk_bufs = (part, parts_in, relay, parts_last, p_s, p_r, last_s, last_r)
    v_bufs = (part_v, v_in, relay_v, v_last, pv_s, pv_r, lv_s, lv_r)

    def to_first(bufs, i, n, h):
        own, got, _, _, send, recv, _, _ = bufs
        return copy(own.at[i, h], got.at[i, n], send.at[i, n], recv.at[i, n], first_of(i), t)

    def to_second(bufs, i):
        _, _, passed, got, _, _, send, recv = bufs
        return copy(passed.at[i], got.at[i], send.at[i], recv.at[i], second_of(i), t)

    def project(bufs, fields, i):
        left = full[0, :, chunk(i)].reshape(many, feats)
        right = full[1, :, chunk(i)].reshape(many, feats)
        for at, n in enumerate(fields):
            acc = jnp.dot(left, w[n, :feats], preferred_element_type=jnp.float32)
            acc += jnp.dot(right, w[n, feats:], preferred_element_type=jnp.float32)
            for h in range(n_seq):
                bufs[0][i, h, :, at * 128 : (at + 1) * 128] = acc[
                    :, h * 128 : (h + 1) * 128
                ].astype(jnp.bfloat16)
        to_first(bufs, i, 1, corner).start()
        to_first(bufs, i, 0, first_of(i)).start()

    def project_qk(i):
        swap(i, 1 - c).wait_recv()
        project(qk_bufs, (0, 1), i)

    def project_v(i):
        project(v_bufs, (2,), i)

    def relay_on(bufs, i):
        own, got, passed = bufs[:3]
        to_first(bufs, i, 1, corner).wait_recv()
        passed[i] = (
            own[i, second_of(i)].astype(jnp.float32) + got[i, 1].astype(jnp.float32)
        ).astype(jnp.bfloat16)
        to_second(bufs, i).start()

    def summed_head(bufs, i):
        own, got, _, last = bufs[:4]
        to_first(bufs, i, 0, corner).wait_recv()
        to_second(bufs, i).wait_recv()
        total = own[i, s].astype(jnp.float32) + got[i, 0].astype(jnp.float32)
        return total + last[i].astype(jnp.float32)

    ones_h = jnp.ones((8, 128), jnp.float32)
    st2[s] = jnp.zeros((8, rows), jnp.float32)

    def collect(i):
        total = summed_head(qk_bufs, i)
        qkv[i] = total
        q_sq = dot11(ones_h, total[:, :128] * total[:, :128], EXACT)
        k_sq = dot11(ones_h, total[:, 128:256] * total[:, 128:256], EXACT)
        st2[s] = jnp.where(row8 == 2 * i, q_sq, jnp.where(row8 == 2 * i + 1, k_sq, st2[s]))

    def collect_v(i, carry):
        v_all[i] = summed_head(v_bufs, i).astype(jnp.bfloat16).reshape(n_seq, cr, 128)
        return carry

    load_w.wait()
    load_w_out.wait()

    def during(step, at, work):
        @pl.when((step >= at) & (step < at + chunks))
        def _():
            work(step - at)

    def project_step(step, carry):
        during(step, 2, project_qk)
        during(step, 3, functools.partial(relay_on, qk_bufs))
        during(step, 1, from_plane)
        during(step, 4, project_v)
        during(step, 4, collect)
        during(step, 0, tables)
        during(step, 0, from_line)
        return carry

    lax.fori_loop(0, chunks + 4, project_step, 0)

    for p in plane:
        copy(st2.at[s], st2.at[s], st2_s.at[p], st2_r.at[s], p, t).start()

    def relay_v_on(i, carry):
        relay_on(v_bufs, i)
        return carry

    lax.fori_loop(0, chunks, relay_v_on, 0)

    gains = (q_gain[pl.ds(s, 1), :], k_gain[pl.ds(s, 1), :])

    def rotate(i, carry):
        cos_i = cosine[i].reshape(many, 128)
        sin_i = sine[i].reshape(many, 128)
        for n in range(2):
            cols = slice(n * 128, (n + 1) * 128)
            field = qkv[i, :, cols] * gains[n]
            swapped = jnp.where(even, pltpu.roll(field, 127, 1), pltpu.roll(field, 1, 1))
            qkv[i, :, cols] = field * cos_i + swapped * sin_i
        return carry

    for p in plane:
        copy(st2.at[p], st2.at[p], st2_s.at[p], st2_r.at[p], p, t).wait_recv()
    st3[t] = jnp.sum(st2[...], axis=0)
    for p in column:
        copy(st3.at[t], st3.at[t], st3_s.at[p], st3_r.at[t], s, p).start()

    def send_v(p):
        return copy(v_all.at[:, p], v_out.at[:, :, lanes_of(s)], v_s.at[p], v_r.at[s], p, t)

    def send_k(p):
        mine = k_ext.at[:, p, :, pl.ds(0, 128)]
        return copy(mine, k_out.at[:, :, lanes_of(s)], k_s.at[p], k_r.at[s], p, t)

    lax.fori_loop(0, chunks, rotate, 0)
    lax.fori_loop(0, chunks, collect_v, 0)
    for p in column:
        copy(st3.at[p], st3.at[p], st3_s.at[p], st3_r.at[p], s, p).wait_recv()
    norm_rows = lax.rsqrt(jnp.sum(st3[...], axis=0) / all_heads + EPSILON)

    def scale_rows(i, carry):
        q_col = dot00(norm_rows, (pick == 2 * i).astype(jnp.float32))
        k_col = dot00(norm_rows, (pick == 2 * i + 1).astype(jnp.float32))
        q_i = (qkv[i, :, :128] * q_col).astype(jnp.bfloat16)
        k_i = (qkv[i, :, 128:256] * k_col).astype(jnp.bfloat16)
        q_ext[i, :, :, :128] = q_i.reshape(n_seq, cr, 128)
        k_ext[i, :, :, :128] = k_i.reshape(n_seq, cr, 128)
        return carry

    lax.fori_loop(0, chunks, scale_rows, 0)

    score_scale = 1.0 / math.sqrt(HEAD_DIM)

    def attend(i):
        keys = k_ext[...].reshape(n_seq * rows, 256)
        values = v_all[...].reshape(n_seq * rows, 128)
        scores = dot11(q_ext[i].reshape(many, 256), keys)
        top = jnp.max(scores, axis=1, keepdims=True)
        weights = jnp.exp((scores - top) * score_scale)
        denominator = jnp.sum(weights, axis=1, keepdims=True)
        mixed = jnp.dot(weights.astype(jnp.bfloat16), values, preferred_element_type=jnp.float32)
        done = (mixed / denominator).astype(jnp.bfloat16)
        attn[i, :, :, lanes_of(s)] = done.reshape(n_seq, cr, 128)
        for p in plane:
            mine = attn.at[i, :, :, lanes_of(s)]
            copy(mine, mine, a_s.at[i, p], a_r.at[i, s], p, t).start()

    def pair(i):
        return copy(
            terms.at[i, 1 - c], pair_in.at[i], pair_s.at[i], pair_r.at[i], s, sibling
        )

    def out_project(i):
        for p in plane:
            theirs = attn.at[i, :, :, lanes_of(p)]
            copy(theirs, theirs, a_s.at[i, p], a_r.at[i, p], p, t).wait_recv()
        for n in range(2):
            cols = slice(n * feats, (n + 1) * feats)
            product = jnp.dot(
                attn[i].reshape(many, n_seq * 128), w_out[:, cols],
                preferred_element_type=jnp.float32,
            )
            terms[i, n] = product.astype(jnp.bfloat16).reshape(n_seq, cr, feats)
        pair(i).start()

    def pair_sum(i):
        pair(i).wait_recv()
        summed[i] = (terms[i, c].astype(jnp.float32) + pair_in[i].astype(jnp.float32)).astype(
            jnp.bfloat16
        )
        moved[s, i] = summed[i, s]
        for p in plane:
            copy(summed.at[i, p], moved.at[s, i], mv_s.at[i, p], mv_r.at[i, s], p, t).start()

    def to_line(i, p):
        return copy(
            moved.at[p, i], arrived.at[z, i], ar_s.at[i, p], ar_r.at[i, z], s, p * 2 + c
        )

    def to_joint(i, p):
        via = jnp.where(z == 0, 1, n_z - 2)
        return copy(moved.at[p, i], joint.at[i], ar_s.at[i, p], j_r.at[i], s, via * 2 + c)

    def deliver(i, p):
        @pl.when(p == z)
        def _():
            arrived[z, i] = moved[p, i]

        @pl.when(apart(p))
        def _():
            to_joint(i, p).start()
            arrived[p, i] = jnp.zeros((cr, feats), jnp.bfloat16)

        @pl.when((p != z) & jnp.logical_not(apart(p)) & jnp.logical_not(between(p)))
        def _():
            to_line(i, p).start()

    def join(i):
        @pl.when((z > 0) & (z < n_z - 1))
        def _():
            p = jnp.where(z == 1, n_z - 1, 0)
            to_joint(i, p).wait_recv()
            joined[i] = (
                moved[p, i].astype(jnp.float32) + joint[i].astype(jnp.float32)
            ).astype(jnp.bfloat16)
            copy(
                joined.at[i], arrived.at[z, i], ar_s.at[i, p], ar_r.at[i, z], s, p * 2 + c
            ).start()

    def deliver_all(i):
        deliver(i, s)
        for p in plane:
            theirs = moved.at[p, i]
            copy(theirs, theirs, mv_s.at[i, p], mv_r.at[i, p], p, t).wait_recv()
            deliver(i, p)

    def attend_step(step, carry):
        during(step, 4, join)
        during(step, 3, deliver_all)
        during(step, 2, pair_sum)
        during(step, 0, attend)
        during(step, 1, out_project)
        return carry

    lax.fori_loop(0, chunks + 4, attend_step, 0)
    for p in plane:
        send_k(p).start()
        send_v(p).start()
    k_out[:, :, lanes_of(s)] = k_ext[:, s, :, :128]
    v_out[:, :, lanes_of(s)] = v_all[:, s]

    def finish(i, carry):
        for p in line:
            theirs = arrived.at[p, i]

            @pl.when(jnp.logical_not(apart(p)))
            def _():
                copy(theirs, theirs, ar_s.at[i, p], ar_r.at[i, p], s, p * 2 + c).wait_recv()

        mixed = arrived[0, i].astype(jnp.float32)
        for p in range(1, n_z):
            mixed += arrived[p, i].astype(jnp.float32)
        base = hid[chunk(i), :].astype(jnp.float32)
        out[chunk(i), :] = (base + gate[chunk(i), :] * mixed).astype(jnp.bfloat16)
        return carry

    lax.fori_loop(0, chunks, finish, 0)

    for p in plane:
        copy(
            k_ext.at[:, p, :, pl.ds(0, 128)], k_out.at[:, :, lanes_of(p)], k_s.at[p], k_r.at[p], p, t
        ).wait()
        copy(v_all.at[:, p], v_out.at[:, :, lanes_of(p)], v_s.at[p], v_r.at[p], p, t).wait()
        copy(meta_all.at[s], meta_all.at[s], meta_s.at[p], meta_r.at[s], p, t).wait_send()
        copy(st2.at[s], st2.at[s], st2_s.at[p], st2_r.at[s], p, t).wait_send()
    for p in column:
        copy(st1.at[t], st1.at[t], st1_s.at[p], st1_r.at[t], s, p).wait_send()
        copy(st3.at[t], st3.at[t], st3_s.at[p], st3_r.at[t], s, p).wait_send()

    def drain(i, carry):
        swap(i, c).wait_send()
        pair(i).wait_send()
        for bufs in (qk_bufs, v_bufs):
            to_first(bufs, i, 0, first_of(i)).wait_send()
            to_first(bufs, i, 1, corner).wait_send()
            to_second(bufs, i).wait_send()
        for p in line:
            @pl.when(jnp.logical_not(apart(p)))
            def _():
                own_block(i, p).wait_send()

            @pl.when(between(p))
            def _():
                block_on(i, p).wait_send()

            to_line(i, p).wait_send()
        for p in plane:
            copy(
                gathered.at[p, chunk(i)], full.at[c, s, chunk(i)], f_s.at[i, p], f_r.at[i, s], p, t
            ).wait_send()
            mine = attn.at[i, :, :, lanes_of(s)]
            copy(mine, mine, a_s.at[i, p], a_r.at[i, s], p, t).wait_send()
            copy(summed.at[i, p], moved.at[s, i], mv_s.at[i, p], mv_r.at[i, s], p, t).wait_send()
        return carry

    lax.fori_loop(0, chunks, drain, 0)


def hand_over(*refs):
    for i in range(3):
        refs[3 + i][...] = refs[i][...]


def frequencies():
    part_width = HEAD_DIM // 6
    widths = (HEAD_DIM - 4 * part_width, 2 * part_width, 2 * part_width)
    table = np.zeros((8, HEAD_DIM), np.float32)
    at = 0
    for axis_number, wide in enumerate(widths):
        exponent = np.arange(0, wide, 2, dtype=np.float32) / np.float32(wide)
        frequency = (1.0 / np.float32(10000.0) ** exponent).astype(np.float32)
        table[axis_number, at : at + wide] = np.repeat(frequency, 2)
        at += wide
    return table


def fused_body(hidden_in, seg_ids, positions, mod_table, w_qkv, q_gain, k_gain, w_out):
    n_seq = lax.axis_size("seq")
    n_tp = lax.axis_size("tp")
    rows, feats = hidden_in.shape
    depth, _, heads_width = w_qkv.shape
    bf16, f32 = jnp.bfloat16, jnp.float32
    n_z = n_tp // 2
    chunks = CHUNKS
    cr = rows // chunks
    many = n_seq * cr
    dma = pltpu.SemaphoreType.DMA
    scratch = [
        pltpu.VMEM((3, depth, heads_width), bf16),
        pltpu.VMEM(w_out.shape, bf16),
        pltpu.VMEM((3, 8, feats), f32),
        pltpu.VMEM((n_seq, 8, rows), f32),
        pltpu.VMEM((n_tp, 8, rows), f32),
        pltpu.VMEM((n_z, rows, feats), bf16),
        pltpu.VMEM((2, n_seq, rows, feats), bf16),
        pltpu.VMEM((chunks, n_seq, many, 256), bf16),
        pltpu.VMEM((chunks, many, 256), bf16),
        pltpu.VMEM((chunks, 2, many, 256), bf16),
        pltpu.VMEM((chunks, many, 256), bf16),
        pltpu.VMEM((n_seq, 8, rows), f32),
        pltpu.VMEM((n_tp, 8, rows), f32),
        pltpu.VMEM((chunks, many, 256), f32),
        pltpu.VMEM((chunks, n_seq, cr, 128), f32),
        pltpu.VMEM((chunks, n_seq, cr, 128), f32),
        pltpu.VMEM((chunks, n_seq, cr, 256), bf16),
        pltpu.VMEM((chunks, n_seq, cr, 256), bf16),
        pltpu.VMEM((chunks, n_seq, cr, 128), bf16),
        pltpu.VMEM((chunks, n_seq, cr, heads_width), bf16),
        pltpu.VMEM((chunks, 2, n_seq, cr, feats), bf16),
        pltpu.VMEM((chunks, n_seq, cr, feats), bf16),
        pltpu.VMEM((chunks, n_seq, cr, feats), bf16),
        pltpu.VMEM((n_seq, chunks, cr, feats), bf16),
        pltpu.VMEM((n_z, chunks, cr, feats), bf16),
        pltpu.VMEM((chunks, cr, feats), bf16),
        pltpu.VMEM((chunks, cr, feats), bf16),
        pltpu.VMEM((chunks, n_seq, many, 128), bf16),
        pltpu.VMEM((chunks, many, 128), bf16),
        pltpu.VMEM((chunks, 2, many, 128), bf16),
        pltpu.VMEM((chunks, many, 128), bf16),
        pltpu.VMEM((3 * PLACES, 256), f32),
        pltpu.VMEM((rows, feats), f32),
        dma((2,)),
        dma((chunks,)),
        dma((chunks, 2)),
        dma((chunks, 2)),
        dma((chunks,)),
        dma((chunks,)),
    ]
    wide = (chunks, n_seq)
    shapes = [
        (n_seq,), (n_tp,), (chunks, n_z), wide, (chunks,), (chunks, 2), (chunks,),
        (n_seq,), (n_tp,), (n_seq,), (n_seq,), wide, (chunks,), wide, (chunks, n_z),
    ]
    for shape in shapes:
        scratch += [dma(shape), dma(shape)]
    vmem = pl.BlockSpec(memory_space=pltpu.VMEM)
    whole = pl.BlockSpec(memory_space=pl.ANY)
    results = pl.pallas_call(
        functools.partial(fused, n_seq, n_tp, feats * n_tp, heads_width * n_tp),
        out_shape=(
            jax.ShapeDtypeStruct((rows, feats), bf16),
            jax.ShapeDtypeStruct((chunks, cr, heads_width), bf16),
            jax.ShapeDtypeStruct((chunks, cr, heads_width), bf16),
        ),
        in_specs=[vmem, vmem, vmem, vmem, vmem, whole, vmem, vmem, whole],
        out_specs=(vmem, vmem, vmem),
        scratch_shapes=scratch,
        compiler_params=pltpu.CompilerParams(
            collective_id=0, has_side_effects=True, vmem_limit_bytes=58 * 1024 * 1024
        ),
        cost_estimate=pl.CostEstimate(
            flops=6_000_000_000, bytes_accessed=8_000_000, transcendentals=1_200_000
        ),
    )(
        hidden_in, seg_ids.reshape(1, rows), positions, mod_table.transpose(1, 0, 2),
        jnp.asarray(frequencies()), w_qkv.transpose(1, 0, 2),
        q_gain.reshape(n_seq, HEAD_DIM), k_gain.reshape(n_seq, HEAD_DIM), w_out,
    )
    hidden, k_cache, v_cache = pl.pallas_call(
        hand_over,
        out_shape=tuple(jax.ShapeDtypeStruct(r.shape, r.dtype) for r in results),
        in_specs=[vmem] * 3,
        out_specs=(vmem,) * 3,
        cost_estimate=pl.CostEstimate(flops=0, bytes_accessed=1_700_000, transcendentals=0),
    )(*results)
    return (
        hidden,
        k_cache.reshape(rows, heads_width),
        v_cache.reshape(rows, heads_width),
    )


def pick_body(*operands):
    hidden_in, seg_ids, positions, mod_table, w_qkv = operands[:5]
    n_seq, n_tp = lax.axis_size("seq"), lax.axis_size("tp")
    fits = (
        n_tp == 2 * n_seq
        and n_seq == 4
        and w_qkv.shape[2] == n_seq * HEAD_DIM
        and w_qkv.shape[0] == 2 * hidden_in.shape[1]
        and hidden_in.shape[0] == 256
        and mod_table.shape[0] <= 8
    )
    return (fused_body if fits else body)(*operands)


def solution(mesh):
    in_specs = (
        P("seq", "tp"),
        P("seq"),
        P(None, "seq"),
        P(None, None, "tp"),
        P("seq", None, "tp"),
        P("tp"),
        P("tp"),
        P("tp", "seq"),
    )
    out_specs = (P("seq", "tp"), P("seq", "tp"), P("seq", "tp"))
    return jax.shard_map(pick_body, mesh=mesh, in_specs=in_specs, out_specs=out_specs, check_vma=False)
```

```python
import functools
import math

import jax
import jax.numpy as jnp
import numpy as np
from jax import lax
from jax.experimental import pallas as pl
from jax.experimental.pallas import tpu as pltpu
from jax.sharding import PartitionSpec as P

HEAD_DIM = 128


EPSILON = 1e-06
NEG_FILL = -1e30


def rope_tables(positions):
    part_width = HEAD_DIM // 6
    widths = (HEAD_DIM - 4 * part_width, 2 * part_width, 2 * part_width)
    angle_list = []
    for axis_number in range(3):
        exponent = jnp.arange(0, widths[axis_number], 2, dtype=jnp.float32) / widths[axis_number]
        frequency = 1.0 / 10000.0**exponent
        angle_list.append(positions[axis_number].astype(jnp.float32)[:, None] * frequency[None, :])
    angle_all = jnp.concatenate(angle_list, axis=1)
    return (jnp.cos(angle_all), jnp.sin(angle_all))


def rotate_pairs(field, cosine, sine):
    even_part = field[..., 0::2]
    odd_part = field[..., 1::2]
    cos_wide = cosine[:, None, :]
    sin_wide = sine[:, None, :]
    new_even = even_part * cos_wide - odd_part * sin_wide
    new_odd = even_part * sin_wide + odd_part * cos_wide
    return jnp.stack([new_even, new_odd], axis=-1).reshape(field.shape)


def empty_state(query_rows, heads_here):
    maxima = jnp.full((heads_here, query_rows), NEG_FILL, jnp.float32)
    totals = jnp.zeros((heads_here, query_rows), jnp.float32)
    weighted = jnp.zeros((heads_here, query_rows, HEAD_DIM), jnp.float32)
    return (maxima, totals, weighted)


def merge_states(first, second):
    largest = jnp.maximum(first[0], second[0])
    first_factor = jnp.exp(first[0] - largest)
    second_factor = jnp.exp(second[0] - largest)
    totals = first[1] * first_factor + second[1] * second_factor
    weighted = first[2] * first_factor[..., None] + second[2] * second_factor[..., None]
    return (largest, totals, weighted)


def block_state(q_heads, seg_q, key_heads, value_heads, seg_k):
    score_scale = 1.0 / math.sqrt(HEAD_DIM)
    scores = (
        jnp.einsum("qhd,khd->hqk", q_heads, key_heads, preferred_element_type=jnp.float32)
        * score_scale
    )
    same_seg = seg_q[:, None] == seg_k[None, :]
    masked = jnp.where(same_seg[None], scores, NEG_FILL)
    maxima = jnp.max(masked, axis=2)
    weights = jnp.where(same_seg[None], jnp.exp(masked - maxima[..., None]), 0.0)
    totals = jnp.sum(weights, axis=2)
    weighted = jnp.einsum(
        "hqk,khd->hqd",
        weights.astype(jnp.bfloat16),
        value_heads,
        preferred_element_type=jnp.float32,
    )
    return (maxima, totals, weighted)


def absorb_keys(carry_state, q_heads, seg_q, key_rows, value_rows, seg_k):
    row_count = key_rows.shape[0]
    heads_here = q_heads.shape[1]
    block_rows = 512
    block_count = row_count // block_rows
    key_blocks = key_rows.reshape(block_count, block_rows, heads_here, HEAD_DIM)
    value_blocks = value_rows.reshape(block_count, block_rows, heads_here, HEAD_DIM)
    seg_blocks = seg_k.reshape(block_count, block_rows)

    def step_block(state_now, operands):
        key_block, value_block, seg_block = operands
        return (
            merge_states(state_now, block_state(q_heads, seg_q, key_block, value_block, seg_block)),
            None,
        )

    return lax.scan(step_block, carry_state, (key_blocks, value_blocks, seg_blocks))[0]


def body(hidden_in, seg_ids, positions, mod_table, w_qkv, q_gain, k_gain, w_out):
    tok_rows, feat_local = hidden_in.shape
    model_width = feat_local * lax.axis_size("tp")
    heads_width = w_qkv.shape[2]
    heads_here = heads_width // HEAD_DIM
    all_heads_width = heads_width * lax.axis_size("tp")
    x_float = hidden_in.astype(jnp.float32)
    row_sums, row_squares = lax.psum(
        (jnp.sum(x_float, axis=1), jnp.sum(x_float * x_float, axis=1)), "tp"
    )
    mean_value = row_sums / model_width
    variance = row_squares / model_width - mean_value * mean_value
    normed = (x_float - mean_value[:, None]) * lax.rsqrt(variance[:, None] + EPSILON)
    segment_count = mod_table.shape[0]
    table = mod_table.reshape(segment_count, 3 * feat_local)
    onehot = (seg_ids[:, None] == jnp.arange(segment_count, dtype=jnp.int32)[None, :]).astype(
        jnp.float32
    )
    modulation = jnp.dot(onehot, table, precision=lax.Precision.HIGHEST).reshape(
        tok_rows, 3, feat_local
    )
    modded = (normed * (1.0 + modulation[:, 1]) + modulation[:, 0]).astype(jnp.bfloat16)
    full_rows = lax.all_gather(modded, "tp", axis=1, tiled=True)
    portion = lax.all_gather(w_qkv, "seq", axis=0, tiled=True)
    flat = portion.reshape(portion.shape[0], 3 * heads_width)
    projected = jnp.dot(full_rows, flat, preferred_element_type=jnp.float32)
    query_f = projected[:, :heads_width]
    key_f = projected[:, heads_width : 2 * heads_width]
    value_f = projected[:, 2 * heads_width :]
    query_sq, key_sq = lax.psum(
        (jnp.sum(query_f * query_f, axis=1), jnp.sum(key_f * key_f, axis=1)), "tp"
    )
    query_n = query_f * lax.rsqrt(query_sq / all_heads_width + EPSILON)[:, None] * q_gain[None, :]
    key_n = key_f * lax.rsqrt(key_sq / all_heads_width + EPSILON)[:, None] * k_gain[None, :]
    cosine, sine = rope_tables(positions)
    q_heads = rotate_pairs(query_n.reshape(tok_rows, heads_here, HEAD_DIM), cosine, sine).astype(
        jnp.bfloat16
    )
    k_heads = rotate_pairs(key_n.reshape(tok_rows, heads_here, HEAD_DIM), cosine, sine).astype(
        jnp.bfloat16
    )
    k_cache = k_heads.reshape(tok_rows, heads_width)
    v_cache = value_f.astype(jnp.bfloat16)
    key_rows = lax.all_gather(k_cache, "seq", axis=0, tiled=True)
    value_rows = lax.all_gather(v_cache, "seq", axis=0, tiled=True)
    seg_k = lax.all_gather(seg_ids, "seq", axis=0, tiled=True)
    state_end = absorb_keys(
        empty_state(tok_rows, heads_here), q_heads, seg_ids, key_rows, value_rows, seg_k
    )
    attention = (state_end[2] / state_end[1][..., None]).transpose(1, 0, 2)
    attn_out = attention.reshape(tok_rows, heads_width).astype(jnp.bfloat16)
    terms = jnp.dot(
        attn_out,
        lax.all_gather(w_out, "seq", axis=1, tiled=True),
        preferred_element_type=jnp.float32,
    )
    mixed = lax.psum_scatter(
        terms.astype(jnp.bfloat16), "tp", scatter_dimension=1, tiled=True
    ).astype(jnp.float32)
    hidden_out = (x_float + modulation[:, 2] * mixed).astype(jnp.bfloat16)
    return (hidden_out, k_cache, v_cache)


MESH = pl.DeviceIdType.MESH
EXACT = lax.Precision.HIGHEST
FAR = -1e30
CHUNKS = 4
AHEAD = 2
PLACES = 64


def dot00(a, b):
    return lax.dot_general(
        a, b, (((0,), (0,)), ((), ())), precision=EXACT, preferred_element_type=jnp.float32
    )


def dot11(a, b, precision=None):
    return lax.dot_general(
        a, b, (((1,), (1,)), ((), ())), precision=precision, preferred_element_type=jnp.float32
    )


def fused(
    n_seq, n_tp, width, all_heads,
    hid, segs, positions, modt, freq, w_any, q_gain, k_gain, w_out_any,
    out, k_out, v_out,
    w, w_out, mod8, meta_all, st1, gathered, full, part, relay, parts_in, parts_last,
    st2, st3, qkv, cosine, sine, q_ext, k_ext, v_all, attn, terms, pair_in, summed, moved,
    arrived, joint, joined, part_v, relay_v, v_in, v_last, lookup, keys_t, gate,
    w_sem, j_r, pv_s, pv_r, lv_s, lv_r, meta_s, meta_r, st1_s, st1_r, z_s, z_r, f_s, f_r, swap_s, swap_r, p_s, p_r,
    last_s, last_r, st2_s, st2_r, st3_s, st3_r, k_s, k_r, v_s, v_r, a_s, a_r, pair_s, pair_r,
    mv_s, mv_r, ar_s, ar_r,
):
    s = lax.axis_index("seq")
    t = lax.axis_index("tp")
    z = t // 2
    c = t % 2
    rows, feats = hid.shape
    n_z = n_tp // 2
    chunks = CHUNKS
    cr = rows // chunks
    many = n_seq * cr
    sibling = z * 2 + 1 - c
    x_next = (s // 2) * 2 + 1 - s % 2
    y_next = (1 - s // 2) * 2 + s % 2
    corner = (1 - s // 2) * 2 + 1 - s % 2

    def copy(src, dst, send, recv, to_s, to_t):
        return pltpu.make_async_remote_copy(
            src_ref=src, dst_ref=dst, send_sem=send, recv_sem=recv,
            device_id=(to_s, to_t), device_id_type=MESH,
        )

    def chunk(i):
        return pl.ds(pl.multiple_of(i * cr, cr), cr)

    def lanes_of(h):
        return pl.ds(pl.multiple_of(h * 128, 128), 128)

    plane = [(s + d) % n_seq for d in range(1, n_seq)]
    column = [(t + d) % n_tp for d in range(1, n_tp)]
    line = [(z + jnp.where(z < n_z // 2, d, n_z - d)) % n_z for d in range(1, n_z)]

    def apart(p):
        return (p + z == n_z - 1) & (p * z == 0)

    def between(p):
        return ((z == n_z - 2) & (p == 0)) | ((z == 1) & (p == n_z - 1))

    barrier = pltpu.get_barrier_semaphore()
    for p in plane:
        pl.semaphore_signal(barrier, inc=1, device_id=(p, t), device_id_type=MESH)
    for p in column:
        pl.semaphore_signal(barrier, inc=1, device_id=(s, p), device_id_type=MESH)
    load_w = pltpu.make_async_copy(w_any, w, w_sem.at[0])
    load_w_out = pltpu.make_async_copy(w_out_any, w_out, w_sem.at[1])
    load_w.start()
    load_w_out.start()

    x = hid[...].astype(jnp.float32)
    row8 = lax.broadcasted_iota(jnp.int32, (8, rows), 0)
    ones_b = jnp.ones((8, feats), jnp.bfloat16)
    ones_f = jnp.ones((8, feats), jnp.float32)
    st1[t] = jnp.where(row8 == 0, dot11(ones_b, hid[...]), dot11(ones_f, x * x, EXACT))
    meta_all[s] = jnp.zeros((8, rows), jnp.float32)
    meta_all[s, 0:3] = positions[...].astype(jnp.float32)
    meta_all[s, 3:4] = segs[...].astype(jnp.float32)
    pl.semaphore_wait(barrier, n_seq - 1 + n_tp - 1)
    for p in column:
        copy(st1.at[t], st1.at[t], st1_s.at[p], st1_r.at[t], s, p).start()
    for p in plane:
        copy(meta_all.at[s], meta_all.at[s], meta_s.at[p], meta_r.at[s], p, t).start()

    row32 = lax.broadcasted_iota(jnp.int32, (32, rows), 0)
    onehot = ((segs[...] == row32 % 8) & (row32 < 24)).astype(jnp.float32).astype(jnp.bfloat16)
    mod8[...] = jnp.zeros(mod8.shape, jnp.float32)
    mod8[:, : modt.shape[1]] = modt[...]

    def modulation(n):
        whole = mod8[n]
        high = whole.astype(jnp.bfloat16).astype(jnp.float32)
        middle = (whole - high).astype(jnp.bfloat16).astype(jnp.float32)
        low = whole - high - middle
        parts = jnp.concatenate([high, middle, low, jnp.zeros_like(low)], axis=0)
        return lax.dot_general(
            onehot, parts.astype(jnp.bfloat16), (((0,), (0,)), ((), ())),
            preferred_element_type=jnp.float32,
        )

    shift = modulation(0)
    scale = modulation(1)
    gate[...] = modulation(2)

    for p in column:
        copy(st1.at[p], st1.at[p], st1_s.at[p], st1_r.at[p], s, p).wait_recv()
    totals = jnp.sum(st1[...], axis=0)
    mean_row = totals[0:1] / width
    scale_row = lax.rsqrt(totals[1:2] / width - mean_row * mean_row + EPSILON)
    both = jnp.where(row8 == 0, mean_row, jnp.where(row8 == 1, scale_row, 0.0))
    pick = lax.broadcasted_iota(jnp.int32, (8, 128), 0)
    mean_col = dot00(both, (pick == 0).astype(jnp.float32))[:, 0:1]
    scale_col = dot00(both, (pick == 1).astype(jnp.float32))[:, 0:1]
    normed = (x - mean_col) * scale_col
    gathered[z] = (normed * (1.0 + scale) + shift).astype(jnp.bfloat16)

    def own_block(i, p):
        mine = gathered.at[z, chunk(i)]
        return copy(mine, mine, z_s.at[i, p], z_r.at[i, z], s, p * 2 + c)

    def block_on(i, p):
        theirs = gathered.at[p, chunk(i)]
        return copy(theirs, theirs, z_s.at[i, z], z_r.at[i, p], s, (n_z - 1 - p) * 2 + c)

    def along_z(i):
        for p in line:
            @pl.when(jnp.logical_not(apart(p)))
            def _():
                own_block(i, p).start()

    for i in range(AHEAD):
        along_z(i)
    for p in plane:
        copy(meta_all.at[p], meta_all.at[p], meta_s.at[p], meta_r.at[p], p, t).wait_recv()
    lane = lax.broadcasted_iota(jnp.int32, (rows, 128), 1)
    even = lane % 2 == 0

    def pass_on(i, p):
        @pl.when(p == s)
        def _():
            full[c, s, chunk(i)] = gathered[p, chunk(i)]

        @pl.when(p != s)
        def _():
            copy(
                gathered.at[p, chunk(i)], full.at[c, s, chunk(i)], f_s.at[i, p], f_r.at[i, s], p, t
            ).start()

    def from_line(i):
        pass_on(i, z)
        for p in line:
            theirs = gathered.at[p, chunk(i)]
            copy(theirs, theirs, z_s.at[i, p], z_r.at[i, p], s, p * 2 + c).wait_recv()

            @pl.when(between(p))
            def _():
                block_on(i, p).start()

            pass_on(i, p)

    def swap(i, half):
        block = full.at[half, :, chunk(i)]
        return copy(block, block, swap_s.at[i], swap_r.at[i], s, sibling)

    def from_plane(i):
        for p in plane:
            theirs = full.at[c, p, chunk(i)]
            copy(theirs, theirs, f_s.at[i, p], f_r.at[i, p], p, t).wait_recv()
        swap(i, c).start()

    place_col = lax.broadcasted_iota(jnp.int32, (PLACES, 128), 0).astype(jnp.float32)
    angle = place_col * (freq[0:1, :] + freq[1:2, :] + freq[2:3, :])
    even_col = lax.broadcasted_iota(jnp.int32, (PLACES, 128), 1) % 2 == 0
    cos_all = jnp.cos(angle)
    sin_all = jnp.where(even_col, -1.0, 1.0) * jnp.sin(angle)
    for a in range(3):
        on_axis = freq[a : a + 1, :] > 0.0
        lookup[a * PLACES : (a + 1) * PLACES, :128] = jnp.where(on_axis, cos_all, 0.0)
        lookup[a * PLACES : (a + 1) * PLACES, 128:] = jnp.where(on_axis, sin_all, 0.0)

    def tables(j):
        block = meta_all[j]
        place = lax.broadcasted_iota(jnp.int32, (PLACES, rows), 0).astype(jnp.float32)
        where = [(block[a : a + 1] == place).astype(jnp.float32) for a in range(3)]
        found = dot00(jnp.concatenate(where, axis=0), lookup[...])
        cosine[:, j] = found[:, :128].reshape(chunks, cr, 128)
        sine[:, j] = found[:, 128:].reshape(chunks, cr, 128)
        seg = dot00(block, (pick == 3).astype(jnp.float32))
        same = seg == lane.astype(jnp.float32)
        q_mask = same.astype(jnp.float32).astype(jnp.bfloat16)
        k_mask = jnp.where(same | (lane >= 8), 0.0, FAR).astype(jnp.bfloat16)
        q_ext[:, j, :, 128:] = q_mask.reshape(chunks, cr, 128)
        k_ext[:, j, :, 128:] = k_mask.reshape(chunks, cr, 128)

    def first_of(i):
        return jnp.where(i % 2 == 0, x_next, y_next)

    def second_of(i):
        return jnp.where(i % 2 == 0, y_next, x_next)

    qk_bufs = (part, parts_in, relay, parts_last, p_s, p_r, last_s, last_r)
    v_bufs = (part_v, v_in, relay_v, v_last, pv_s, pv_r, lv_s, lv_r)

    def to_first(bufs, i, n, h):
        own, got, _, _, send, recv, _, _ = bufs
        return copy(own.at[i, h], got.at[i, n], send.at[i, n], recv.at[i, n], first_of(i), t)

    def to_second(bufs, i):
        _, _, passed, got, _, _, send, recv = bufs
        return copy(passed.at[i], got.at[i], send.at[i], recv.at[i], second_of(i), t)

    def project(bufs, fields, i):
        left = full[0, :, chunk(i)].reshape(many, feats)
        right = full[1, :, chunk(i)].reshape(many, feats)
        for at, n in enumerate(fields):
            acc = jnp.dot(left, w[n, :feats], preferred_element_type=jnp.float32)
            acc += jnp.dot(right, w[n, feats:], preferred_element_type=jnp.float32)
            for h in range(n_seq):
                bufs[0][i, h, :, at * 128 : (at + 1) * 128] = acc[
                    :, h * 128 : (h + 1) * 128
                ].astype(jnp.bfloat16)
        to_first(bufs, i, 1, corner).start()
        to_first(bufs, i, 0, first_of(i)).start()

    def project_qk(i):
        swap(i, 1 - c).wait_recv()
        project(qk_bufs, (0, 1), i)

    def project_v(i):
        project(v_bufs, (2,), i)

    def relay_on(bufs, i):
        own, got, passed = bufs[:3]
        to_first(bufs, i, 1, corner).wait_recv()
        passed[i] = (
            own[i, second_of(i)].astype(jnp.float32) + got[i, 1].astype(jnp.float32)
        ).astype(jnp.bfloat16)
        to_second(bufs, i).start()

    def summed_head(bufs, i):
        own, got, _, last = bufs[:4]
        to_first(bufs, i, 0, corner).wait_recv()
        to_second(bufs, i).wait_recv()
        total = own[i, s].astype(jnp.float32) + got[i, 0].astype(jnp.float32)
        return total + last[i].astype(jnp.float32)

    row_of = lax.broadcasted_iota(jnp.int32, (8, 256), 0)
    half_of = lax.broadcasted_iota(jnp.int32, (8, 256), 1) // 128
    st2[s] = jnp.zeros((8, rows), jnp.float32)

    def collect(i):
        total = summed_head(qk_bufs, i)
        qkv[i] = total
        st2[s] = st2[s] + dot11((row_of == 2 * i + half_of).astype(jnp.float32), total * total, EXACT)

    def collect_v(i, carry):
        v_all[i] = summed_head(v_bufs, i).astype(jnp.bfloat16).reshape(n_seq, cr, 128)
        return carry

    load_w.wait()
    load_w_out.wait()

    def during(step, at, work, first=0):
        @pl.when((step >= at + first) & (step < at + chunks))
        def _():
            work(step - at)

    def project_step(step, carry):
        during(step, 2, project_qk)
        during(step, 3, functools.partial(relay_on, qk_bufs))
        during(step, 1, from_plane)
        during(step, 4, project_v)
        during(step, 4, collect)
        during(step, 0, tables)
        during(step, 0, from_line)
        during(step, -AHEAD, along_z, AHEAD)
        return carry

    lax.fori_loop(0, chunks + 4, project_step, 0)

    for p in plane:
        copy(st2.at[s], st2.at[s], st2_s.at[p], st2_r.at[s], p, t).start()

    def relay_v_on(i, carry):
        relay_on(v_bufs, i)
        return carry

    lax.fori_loop(0, chunks, relay_v_on, 0)

    gains = (q_gain[pl.ds(s, 1), :], k_gain[pl.ds(s, 1), :])

    def rotate(i, carry):
        cos_i = cosine[i].reshape(many, 128)
        sin_i = sine[i].reshape(many, 128)
        for n in range(2):
            cols = slice(n * 128, (n + 1) * 128)
            field = qkv[i, :, cols] * gains[n]
            swapped = jnp.where(even, pltpu.roll(field, 127, 1), pltpu.roll(field, 1, 1))
            qkv[i, :, cols] = field * cos_i + swapped * sin_i
        return carry

    for p in plane:
        copy(st2.at[p], st2.at[p], st2_s.at[p], st2_r.at[p], p, t).wait_recv()
    st3[t] = jnp.sum(st2[...], axis=0)
    for p in column:
        copy(st3.at[t], st3.at[t], st3_s.at[p], st3_r.at[t], s, p).start()

    def send_v(p):
        return copy(v_all.at[:, p], v_out.at[:, :, lanes_of(s)], v_s.at[p], v_r.at[s], p, t)

    def send_k(p):
        mine = k_ext.at[:, p, :, pl.ds(0, 128)]
        return copy(mine, k_out.at[:, :, lanes_of(s)], k_s.at[p], k_r.at[s], p, t)

    lax.fori_loop(0, chunks, rotate, 0)
    for p in column:
        copy(st3.at[p], st3.at[p], st3_s.at[p], st3_r.at[p], s, p).wait_recv()
    norm_rows = lax.rsqrt(jnp.sum(st3[...], axis=0) / all_heads + EPSILON)

    lane_row = lax.broadcasted_iota(jnp.int32, (8, 128), 1)
    norm_cols = dot00(norm_rows, (pick == lane_row).astype(jnp.float32))
    for i in range(chunks):
        q_i = (qkv[i, :, :128] * norm_cols[:, 2 * i : 2 * i + 1]).astype(jnp.bfloat16)
        k_i = (qkv[i, :, 128:256] * norm_cols[:, 2 * i + 1 : 2 * i + 2]).astype(jnp.bfloat16)
        q_ext[i, :, :, :128] = q_i.reshape(n_seq, cr, 128)
        k_ext[i, :, :, :128] = k_i.reshape(n_seq, cr, 128)
        keys_t[:, i * many : (i + 1) * many] = k_ext[i].reshape(many, 256).T
    lax.fori_loop(0, chunks, collect_v, 0)
    for p in plane:
        send_v(p).start()
    v_out[:, :, lanes_of(s)] = v_all[:, s]

    score_scale = 1.0 / math.sqrt(HEAD_DIM)

    def attend(i):
        values = v_all[...].reshape(n_seq * rows, 128)
        scores = jnp.dot(
            q_ext[i].reshape(many, 256), keys_t[...], preferred_element_type=jnp.float32
        )
        top = jnp.max(scores, axis=1, keepdims=True)
        weights = jnp.exp((scores - top) * score_scale)
        denominator = jnp.sum(weights, axis=1, keepdims=True)
        mixed = jnp.dot(weights.astype(jnp.bfloat16), values, preferred_element_type=jnp.float32)
        done = (mixed / denominator).astype(jnp.bfloat16)
        attn[i, :, :, lanes_of(s)] = done.reshape(n_seq, cr, 128)
        for p in plane:
            mine = attn.at[i, :, :, lanes_of(s)]
            copy(mine, mine, a_s.at[i, p], a_r.at[i, s], p, t).start()

    def pair(i):
        return copy(
            terms.at[i, 1 - c], pair_in.at[i], pair_s.at[i], pair_r.at[i], s, sibling
        )

    def out_project(i):
        for p in plane:
            theirs = attn.at[i, :, :, lanes_of(p)]
            copy(theirs, theirs, a_s.at[i, p], a_r.at[i, p], p, t).wait_recv()
        for n in range(2):
            cols = slice(n * feats, (n + 1) * feats)
            product = jnp.dot(
                attn[i].reshape(many, n_seq * 128), w_out[:, cols],
                preferred_element_type=jnp.float32,
            )
            terms[i, n] = product.astype(jnp.bfloat16).reshape(n_seq, cr, feats)
        pair(i).start()

    def pair_sum(i):
        pair(i).wait_recv()
        summed[i] = (terms[i, c].astype(jnp.float32) + pair_in[i].astype(jnp.float32)).astype(
            jnp.bfloat16
        )
        moved[s, i] = summed[i, s]
        for p in plane:
            copy(summed.at[i, p], moved.at[s, i], mv_s.at[i, p], mv_r.at[i, s], p, t).start()

    def to_line(i, p):
        return copy(
            moved.at[p, i], arrived.at[z, i], ar_s.at[i, p], ar_r.at[i, z], s, p * 2 + c
        )

    def to_joint(i, p):
        via = jnp.where(z == 0, 1, n_z - 2)
        return copy(moved.at[p, i], joint.at[i], ar_s.at[i, p], j_r.at[i], s, via * 2 + c)

    def deliver(i, p):
        @pl.when(p == z)
        def _():
            arrived[z, i] = moved[p, i]

        @pl.when(apart(p))
        def _():
            to_joint(i, p).start()
            arrived[p, i] = jnp.zeros((cr, feats), jnp.bfloat16)

        @pl.when((p != z) & jnp.logical_not(apart(p)) & jnp.logical_not(between(p)))
        def _():
            to_line(i, p).start()

    def join(i):
        @pl.when((z > 0) & (z < n_z - 1))
        def _():
            p = jnp.where(z == 1, n_z - 1, 0)
            to_joint(i, p).wait_recv()
            joined[i] = (
                moved[p, i].astype(jnp.float32) + joint[i].astype(jnp.float32)
            ).astype(jnp.bfloat16)
            copy(
                joined.at[i], arrived.at[z, i], ar_s.at[i, p], ar_r.at[i, z], s, p * 2 + c
            ).start()

    def deliver_all(i):
        deliver(i, s)
        for p in plane:
            theirs = moved.at[p, i]
            copy(theirs, theirs, mv_s.at[i, p], mv_r.at[i, p], p, t).wait_recv()
            deliver(i, p)

    def attend_step(step, carry):
        during(step, 4, join)
        during(step, 3, deliver_all)
        during(step, 2, pair_sum)

        @pl.when(step == chunks + 1)
        def _():
            for p in plane:
                send_k(p).start()

        during(step, 0, attend)
        during(step, 1, out_project)
        return carry

    lax.fori_loop(0, chunks + 4, attend_step, 0)
    k_out[:, :, lanes_of(s)] = k_ext[:, s, :, :128]

    def finish(i, carry):
        for p in line:
            theirs = arrived.at[p, i]

            @pl.when(jnp.logical_not(apart(p)))
            def _():
                copy(theirs, theirs, ar_s.at[i, p], ar_r.at[i, p], s, p * 2 + c).wait_recv()

        mixed = arrived[0, i].astype(jnp.float32)
        for p in range(1, n_z):
            mixed += arrived[p, i].astype(jnp.float32)
        base = hid[chunk(i), :].astype(jnp.float32)
        out[chunk(i), :] = (base + gate[chunk(i), :] * mixed).astype(jnp.bfloat16)
        return carry

    lax.fori_loop(0, chunks, finish, 0)

    for p in plane:
        copy(
            k_ext.at[:, p, :, pl.ds(0, 128)], k_out.at[:, :, lanes_of(p)], k_s.at[p], k_r.at[p], p, t
        ).wait()
        copy(v_all.at[:, p], v_out.at[:, :, lanes_of(p)], v_s.at[p], v_r.at[p], p, t).wait()
        copy(meta_all.at[s], meta_all.at[s], meta_s.at[p], meta_r.at[s], p, t).wait_send()
        copy(st2.at[s], st2.at[s], st2_s.at[p], st2_r.at[s], p, t).wait_send()
    for p in column:
        copy(st1.at[t], st1.at[t], st1_s.at[p], st1_r.at[t], s, p).wait_send()
        copy(st3.at[t], st3.at[t], st3_s.at[p], st3_r.at[t], s, p).wait_send()

    def drain(i, carry):
        swap(i, c).wait_send()
        pair(i).wait_send()
        for bufs in (qk_bufs, v_bufs):
            to_first(bufs, i, 0, first_of(i)).wait_send()
            to_first(bufs, i, 1, corner).wait_send()
            to_second(bufs, i).wait_send()
        for p in line:
            @pl.when(jnp.logical_not(apart(p)))
            def _():
                own_block(i, p).wait_send()

            @pl.when(between(p))
            def _():
                block_on(i, p).wait_send()

            to_line(i, p).wait_send()
        for p in plane:
            copy(
                gathered.at[p, chunk(i)], full.at[c, s, chunk(i)], f_s.at[i, p], f_r.at[i, s], p, t
            ).wait_send()
            mine = attn.at[i, :, :, lanes_of(s)]
            copy(mine, mine, a_s.at[i, p], a_r.at[i, s], p, t).wait_send()
            copy(summed.at[i, p], moved.at[s, i], mv_s.at[i, p], mv_r.at[i, s], p, t).wait_send()
        return carry

    lax.fori_loop(0, chunks, drain, 0)


def hand_over(*refs):
    for i in range(3):
        refs[3 + i][...] = refs[i][...]


def frequencies():
    part_width = HEAD_DIM // 6
    widths = (HEAD_DIM - 4 * part_width, 2 * part_width, 2 * part_width)
    table = np.zeros((8, HEAD_DIM), np.float32)
    at = 0
    for axis_number, wide in enumerate(widths):
        exponent = np.arange(0, wide, 2, dtype=np.float32) / np.float32(wide)
        frequency = (1.0 / np.float32(10000.0) ** exponent).astype(np.float32)
        table[axis_number, at : at + wide] = np.repeat(frequency, 2)
        at += wide
    return table


def fused_body(hidden_in, seg_ids, positions, mod_table, w_qkv, q_gain, k_gain, w_out):
    n_seq = lax.axis_size("seq")
    n_tp = lax.axis_size("tp")
    rows, feats = hidden_in.shape
    depth, _, heads_width = w_qkv.shape
    bf16, f32 = jnp.bfloat16, jnp.float32
    n_z = n_tp // 2
    chunks = CHUNKS
    cr = rows // chunks
    many = n_seq * cr
    dma = pltpu.SemaphoreType.DMA
    scratch = [
        pltpu.VMEM((3, depth, heads_width), bf16),
        pltpu.VMEM(w_out.shape, bf16),
        pltpu.VMEM((3, 8, feats), f32),
        pltpu.VMEM((n_seq, 8, rows), f32),
        pltpu.VMEM((n_tp, 8, rows), f32),
        pltpu.VMEM((n_z, rows, feats), bf16),
        pltpu.VMEM((2, n_seq, rows, feats), bf16),
        pltpu.VMEM((chunks, n_seq, many, 256), bf16),
        pltpu.VMEM((chunks, many, 256), bf16),
        pltpu.VMEM((chunks, 2, many, 256), bf16),
        pltpu.VMEM((chunks, many, 256), bf16),
        pltpu.VMEM((n_seq, 8, rows), f32),
        pltpu.VMEM((n_tp, 8, rows), f32),
        pltpu.VMEM((chunks, many, 256), f32),
        pltpu.VMEM((chunks, n_seq, cr, 128), f32),
        pltpu.VMEM((chunks, n_seq, cr, 128), f32),
        pltpu.VMEM((chunks, n_seq, cr, 256), bf16),
        pltpu.VMEM((chunks, n_seq, cr, 256), bf16),
        pltpu.VMEM((chunks, n_seq, cr, 128), bf16),
        pltpu.VMEM((chunks, n_seq, cr, heads_width), bf16),
        pltpu.VMEM((chunks, 2, n_seq, cr, feats), bf16),
        pltpu.VMEM((chunks, n_seq, cr, feats), bf16),
        pltpu.VMEM((chunks, n_seq, cr, feats), bf16),
        pltpu.VMEM((n_seq, chunks, cr, feats), bf16),
        pltpu.VMEM((n_z, chunks, cr, feats), bf16),
        pltpu.VMEM((chunks, cr, feats), bf16),
        pltpu.VMEM((chunks, cr, feats), bf16),
        pltpu.VMEM((chunks, n_seq, many, 128), bf16),
        pltpu.VMEM((chunks, many, 128), bf16),
        pltpu.VMEM((chunks, 2, many, 128), bf16),
        pltpu.VMEM((chunks, many, 128), bf16),
        pltpu.VMEM((3 * PLACES, 256), f32),
        pltpu.VMEM((256, chunks * many), bf16),
        pltpu.VMEM((rows, feats), f32),
        dma((2,)),
        dma((chunks,)),
        dma((chunks, 2)),
        dma((chunks, 2)),
        dma((chunks,)),
        dma((chunks,)),
    ]
    wide = (chunks, n_seq)
    shapes = [
        (n_seq,), (n_tp,), (chunks, n_z), wide, (chunks,), (chunks, 2), (chunks,),
        (n_seq,), (n_tp,), (n_seq,), (n_seq,), wide, (chunks,), wide, (chunks, n_z),
    ]
    for shape in shapes:
        scratch += [dma(shape), dma(shape)]
    vmem = pl.BlockSpec(memory_space=pltpu.VMEM)
    whole = pl.BlockSpec(memory_space=pl.ANY)
    results = pl.pallas_call(
        functools.partial(fused, n_seq, n_tp, feats * n_tp, heads_width * n_tp),
        out_shape=(
            jax.ShapeDtypeStruct((rows, feats), bf16),
            jax.ShapeDtypeStruct((chunks, cr, heads_width), bf16),
            jax.ShapeDtypeStruct((chunks, cr, heads_width), bf16),
        ),
        in_specs=[vmem, vmem, vmem, vmem, vmem, whole, vmem, vmem, whole],
        out_specs=(vmem, vmem, vmem),
        scratch_shapes=scratch,
        compiler_params=pltpu.CompilerParams(
            collective_id=0, has_side_effects=True, vmem_limit_bytes=58 * 1024 * 1024
        ),
        cost_estimate=pl.CostEstimate(
            flops=6_000_000_000, bytes_accessed=8_000_000, transcendentals=1_200_000
        ),
    )(
        hidden_in, seg_ids.reshape(1, rows), positions, mod_table.transpose(1, 0, 2),
        jnp.asarray(frequencies()), w_qkv.transpose(1, 0, 2),
        q_gain.reshape(n_seq, HEAD_DIM), k_gain.reshape(n_seq, HEAD_DIM), w_out,
    )
    hidden, k_cache, v_cache = pl.pallas_call(
        hand_over,
        out_shape=tuple(jax.ShapeDtypeStruct(r.shape, r.dtype) for r in results),
        in_specs=[vmem] * 3,
        out_specs=(vmem,) * 3,
        cost_estimate=pl.CostEstimate(flops=0, bytes_accessed=1_700_000, transcendentals=0),
    )(*results)
    return (
        hidden,
        k_cache.reshape(rows, heads_width),
        v_cache.reshape(rows, heads_width),
    )


def pick_body(*operands):
    hidden_in, seg_ids, positions, mod_table, w_qkv = operands[:5]
    n_seq, n_tp = lax.axis_size("seq"), lax.axis_size("tp")
    fits = (
        n_tp == 2 * n_seq
        and n_seq == 4
        and w_qkv.shape[2] == n_seq * HEAD_DIM
        and w_qkv.shape[0] == 2 * hidden_in.shape[1]
        and hidden_in.shape[0] == 256
        and mod_table.shape[0] <= 8
    )
    return (fused_body if fits else body)(*operands)


def solution(mesh):
    in_specs = (
        P("seq", "tp"),
        P("seq"),
        P(None, "seq"),
        P(None, None, "tp"),
        P("seq", None, "tp"),
        P("tp"),
        P("tp"),
        P("tp", "seq"),
    )
    out_specs = (P("seq", "tp"), P("seq", "tp"), P("seq", "tp"))
    return jax.shard_map(pick_body, mesh=mesh, in_specs=in_specs, out_specs=out_specs, check_vma=False)
```

```python
import functools
import math

import jax
import jax.numpy as jnp
import numpy as np
from jax import lax
from jax.experimental import pallas as pl
from jax.experimental.pallas import tpu as pltpu
from jax.sharding import PartitionSpec as P

HEAD_DIM = 128


EPSILON = 1e-06
NEG_FILL = -1e30


def rope_tables(positions):
    part_width = HEAD_DIM // 6
    widths = (HEAD_DIM - 4 * part_width, 2 * part_width, 2 * part_width)
    angle_list = []
    for axis_number in range(3):
        exponent = jnp.arange(0, widths[axis_number], 2, dtype=jnp.float32) / widths[axis_number]
        frequency = 1.0 / 10000.0**exponent
        angle_list.append(positions[axis_number].astype(jnp.float32)[:, None] * frequency[None, :])
    angle_all = jnp.concatenate(angle_list, axis=1)
    return (jnp.cos(angle_all), jnp.sin(angle_all))


def rotate_pairs(field, cosine, sine):
    even_part = field[..., 0::2]
    odd_part = field[..., 1::2]
    cos_wide = cosine[:, None, :]
    sin_wide = sine[:, None, :]
    new_even = even_part * cos_wide - odd_part * sin_wide
    new_odd = even_part * sin_wide + odd_part * cos_wide
    return jnp.stack([new_even, new_odd], axis=-1).reshape(field.shape)


def empty_state(query_rows, heads_here):
    maxima = jnp.full((heads_here, query_rows), NEG_FILL, jnp.float32)
    totals = jnp.zeros((heads_here, query_rows), jnp.float32)
    weighted = jnp.zeros((heads_here, query_rows, HEAD_DIM), jnp.float32)
    return (maxima, totals, weighted)


def merge_states(first, second):
    largest = jnp.maximum(first[0], second[0])
    first_factor = jnp.exp(first[0] - largest)
    second_factor = jnp.exp(second[0] - largest)
    totals = first[1] * first_factor + second[1] * second_factor
    weighted = first[2] * first_factor[..., None] + second[2] * second_factor[..., None]
    return (largest, totals, weighted)


def block_state(q_heads, seg_q, key_heads, value_heads, seg_k):
    score_scale = 1.0 / math.sqrt(HEAD_DIM)
    scores = (
        jnp.einsum("qhd,khd->hqk", q_heads, key_heads, preferred_element_type=jnp.float32)
        * score_scale
    )
    same_seg = seg_q[:, None] == seg_k[None, :]
    masked = jnp.where(same_seg[None], scores, NEG_FILL)
    maxima = jnp.max(masked, axis=2)
    weights = jnp.where(same_seg[None], jnp.exp(masked - maxima[..., None]), 0.0)
    totals = jnp.sum(weights, axis=2)
    weighted = jnp.einsum(
        "hqk,khd->hqd",
        weights.astype(jnp.bfloat16),
        value_heads,
        preferred_element_type=jnp.float32,
    )
    return (maxima, totals, weighted)


def absorb_keys(carry_state, q_heads, seg_q, key_rows, value_rows, seg_k):
    row_count = key_rows.shape[0]
    heads_here = q_heads.shape[1]
    block_rows = 512
    block_count = row_count // block_rows
    key_blocks = key_rows.reshape(block_count, block_rows, heads_here, HEAD_DIM)
    value_blocks = value_rows.reshape(block_count, block_rows, heads_here, HEAD_DIM)
    seg_blocks = seg_k.reshape(block_count, block_rows)

    def step_block(state_now, operands):
        key_block, value_block, seg_block = operands
        return (
            merge_states(state_now, block_state(q_heads, seg_q, key_block, value_block, seg_block)),
            None,
        )

    return lax.scan(step_block, carry_state, (key_blocks, value_blocks, seg_blocks))[0]


def body(hidden_in, seg_ids, positions, mod_table, w_qkv, q_gain, k_gain, w_out):
    tok_rows, feat_local = hidden_in.shape
    model_width = feat_local * lax.axis_size("tp")
    heads_width = w_qkv.shape[2]
    heads_here = heads_width // HEAD_DIM
    all_heads_width = heads_width * lax.axis_size("tp")
    x_float = hidden_in.astype(jnp.float32)
    row_sums, row_squares = lax.psum(
        (jnp.sum(x_float, axis=1), jnp.sum(x_float * x_float, axis=1)), "tp"
    )
    mean_value = row_sums / model_width
    variance = row_squares / model_width - mean_value * mean_value
    normed = (x_float - mean_value[:, None]) * lax.rsqrt(variance[:, None] + EPSILON)
    segment_count = mod_table.shape[0]
    table = mod_table.reshape(segment_count, 3 * feat_local)
    onehot = (seg_ids[:, None] == jnp.arange(segment_count, dtype=jnp.int32)[None, :]).astype(
        jnp.float32
    )
    modulation = jnp.dot(onehot, table, precision=lax.Precision.HIGHEST).reshape(
        tok_rows, 3, feat_local
    )
    modded = (normed * (1.0 + modulation[:, 1]) + modulation[:, 0]).astype(jnp.bfloat16)
    full_rows = lax.all_gather(modded, "tp", axis=1, tiled=True)
    portion = lax.all_gather(w_qkv, "seq", axis=0, tiled=True)
    flat = portion.reshape(portion.shape[0], 3 * heads_width)
    projected = jnp.dot(full_rows, flat, preferred_element_type=jnp.float32)
    query_f = projected[:, :heads_width]
    key_f = projected[:, heads_width : 2 * heads_width]
    value_f = projected[:, 2 * heads_width :]
    query_sq, key_sq = lax.psum(
        (jnp.sum(query_f * query_f, axis=1), jnp.sum(key_f * key_f, axis=1)), "tp"
    )
    query_n = query_f * lax.rsqrt(query_sq / all_heads_width + EPSILON)[:, None] * q_gain[None, :]
    key_n = key_f * lax.rsqrt(key_sq / all_heads_width + EPSILON)[:, None] * k_gain[None, :]
    cosine, sine = rope_tables(positions)
    q_heads = rotate_pairs(query_n.reshape(tok_rows, heads_here, HEAD_DIM), cosine, sine).astype(
        jnp.bfloat16
    )
    k_heads = rotate_pairs(key_n.reshape(tok_rows, heads_here, HEAD_DIM), cosine, sine).astype(
        jnp.bfloat16
    )
    k_cache = k_heads.reshape(tok_rows, heads_width)
    v_cache = value_f.astype(jnp.bfloat16)
    key_rows = lax.all_gather(k_cache, "seq", axis=0, tiled=True)
    value_rows = lax.all_gather(v_cache, "seq", axis=0, tiled=True)
    seg_k = lax.all_gather(seg_ids, "seq", axis=0, tiled=True)
    state_end = absorb_keys(
        empty_state(tok_rows, heads_here), q_heads, seg_ids, key_rows, value_rows, seg_k
    )
    attention = (state_end[2] / state_end[1][..., None]).transpose(1, 0, 2)
    attn_out = attention.reshape(tok_rows, heads_width).astype(jnp.bfloat16)
    terms = jnp.dot(
        attn_out,
        lax.all_gather(w_out, "seq", axis=1, tiled=True),
        preferred_element_type=jnp.float32,
    )
    mixed = lax.psum_scatter(
        terms.astype(jnp.bfloat16), "tp", scatter_dimension=1, tiled=True
    ).astype(jnp.float32)
    hidden_out = (x_float + modulation[:, 2] * mixed).astype(jnp.bfloat16)
    return (hidden_out, k_cache, v_cache)


MESH = pl.DeviceIdType.MESH
EXACT = lax.Precision.HIGHEST
FAR = -1e30
CHUNKS = 4
AHEAD = 2
PLACES = 64


def dot00(a, b):
    return lax.dot_general(
        a, b, (((0,), (0,)), ((), ())), precision=EXACT, preferred_element_type=jnp.float32
    )


def dot11(a, b, precision=None):
    return lax.dot_general(
        a, b, (((1,), (1,)), ((), ())), precision=precision, preferred_element_type=jnp.float32
    )


def fused(
    n_seq, n_tp, width, all_heads,
    hid, segs, positions, modt, freq, w_any, q_gain, k_gain, w_out_any,
    out, k_out, v_out,
    w, w_out, mod8, meta_all, st1, gathered, full, part, relay, parts_in, parts_last,
    st2, st3, qkv, cosine, sine, q_ext, k_ext, v_all, attn, terms, pair_in, summed, moved,
    arrived, joint, joined, part_v, relay_v, v_in, v_last, lookup, keys_t, gate,
    w_sem, j_r, pv_s, pv_r, lv_s, lv_r, meta_s, meta_r, st1_s, st1_r, z_s, z_r, f_s, f_r, swap_s, swap_r, p_s, p_r,
    last_s, last_r, st2_s, st2_r, st3_s, st3_r, k_s, k_r, v_s, v_r, a_s, a_r, pair_s, pair_r,
    mv_s, mv_r, ar_s, ar_r,
):
    s = lax.axis_index("seq")
    t = lax.axis_index("tp")
    z = t // 2
    c = t % 2
    rows, feats = hid.shape
    n_z = n_tp // 2
    chunks = CHUNKS
    cr = rows // chunks
    many = n_seq * cr
    sibling = z * 2 + 1 - c
    x_next = (s // 2) * 2 + 1 - s % 2
    y_next = (1 - s // 2) * 2 + s % 2
    corner = (1 - s // 2) * 2 + 1 - s % 2

    def copy(src, dst, send, recv, to_s, to_t):
        return pltpu.make_async_remote_copy(
            src_ref=src, dst_ref=dst, send_sem=send, recv_sem=recv,
            device_id=(to_s, to_t), device_id_type=MESH,
        )

    def chunk(i):
        return pl.ds(pl.multiple_of(i * cr, cr), cr)

    def lanes_of(h):
        return pl.ds(pl.multiple_of(h * 128, 128), 128)

    plane = [(s + d) % n_seq for d in range(1, n_seq)]
    column = [(t + d) % n_tp for d in range(1, n_tp)]
    line = [(z + jnp.where(z < n_z // 2, d, n_z - d)) % n_z for d in range(1, n_z)]

    def apart(p):
        return (p + z == n_z - 1) & (p * z == 0)

    def between(p):
        return ((z == n_z - 2) & (p == 0)) | ((z == 1) & (p == n_z - 1))

    barrier = pltpu.get_barrier_semaphore()
    for p in plane:
        pl.semaphore_signal(barrier, inc=1, device_id=(p, t), device_id_type=MESH)
    for p in column:
        pl.semaphore_signal(barrier, inc=1, device_id=(s, p), device_id_type=MESH)
    load_w = pltpu.make_async_copy(w_any, w, w_sem.at[0])
    load_w_out = pltpu.make_async_copy(w_out_any, w_out, w_sem.at[1])
    load_w.start()
    load_w_out.start()

    x = hid[...].astype(jnp.float32)
    row8 = lax.broadcasted_iota(jnp.int32, (8, rows), 0)
    ones_b = jnp.ones((8, feats), jnp.bfloat16)
    ones_f = jnp.ones((8, feats), jnp.float32)
    st1[t] = jnp.where(row8 == 0, dot11(ones_b, hid[...]), dot11(ones_f, x * x, EXACT))
    meta_all[s] = jnp.zeros((8, rows), jnp.float32)
    meta_all[s, 0:3] = positions[...].astype(jnp.float32)
    meta_all[s, 3:4] = segs[...].astype(jnp.float32)
    pl.semaphore_wait(barrier, n_seq - 1 + n_tp - 1)
    for p in column:
        copy(st1.at[t], st1.at[t], st1_s.at[p], st1_r.at[t], s, p).start()
    for p in plane:
        copy(meta_all.at[s], meta_all.at[s], meta_s.at[p], meta_r.at[s], p, t).start()

    row32 = lax.broadcasted_iota(jnp.int32, (32, rows), 0)
    onehot = ((segs[...] == row32 % 8) & (row32 < 24)).astype(jnp.float32).astype(jnp.bfloat16)
    mod8[...] = jnp.zeros(mod8.shape, jnp.float32)
    mod8[:, : modt.shape[1]] = modt[...]

    def modulation(n):
        whole = mod8[n]
        high = whole.astype(jnp.bfloat16).astype(jnp.float32)
        middle = (whole - high).astype(jnp.bfloat16).astype(jnp.float32)
        low = whole - high - middle
        parts = jnp.concatenate([high, middle, low, jnp.zeros_like(low)], axis=0)
        return lax.dot_general(
            onehot, parts.astype(jnp.bfloat16), (((0,), (0,)), ((), ())),
            preferred_element_type=jnp.float32,
        )

    shift = modulation(0)
    scale = modulation(1)
    gate[...] = modulation(2)

    for p in column:
        copy(st1.at[p], st1.at[p], st1_s.at[p], st1_r.at[p], s, p).wait_recv()
    totals = jnp.sum(st1[...], axis=0)
    mean_row = totals[0:1] / width
    scale_row = lax.rsqrt(totals[1:2] / width - mean_row * mean_row + EPSILON)
    both = jnp.where(row8 == 0, mean_row, jnp.where(row8 == 1, scale_row, 0.0))
    pick = lax.broadcasted_iota(jnp.int32, (8, 128), 0)
    mean_col = dot00(both, (pick == 0).astype(jnp.float32))[:, 0:1]
    scale_col = dot00(both, (pick == 1).astype(jnp.float32))[:, 0:1]
    normed = (x - mean_col) * scale_col
    gathered[z] = (normed * (1.0 + scale) + shift).astype(jnp.bfloat16)

    def own_block(i, p):
        mine = gathered.at[z, chunk(i)]
        return copy(mine, mine, z_s.at[i, p], z_r.at[i, z], s, p * 2 + c)

    def block_on(i, p):
        theirs = gathered.at[p, chunk(i)]
        return copy(theirs, theirs, z_s.at[i, z], z_r.at[i, p], s, (n_z - 1 - p) * 2 + c)

    def along_z(i):
        for p in line:
            @pl.when(jnp.logical_not(apart(p)))
            def _():
                own_block(i, p).start()

    for i in range(AHEAD):
        along_z(i)
    for p in plane:
        copy(meta_all.at[p], meta_all.at[p], meta_s.at[p], meta_r.at[p], p, t).wait_recv()
    lane = lax.broadcasted_iota(jnp.int32, (rows, 128), 1)
    even = lane % 2 == 0

    def pass_on(i, p):
        @pl.when(p == s)
        def _():
            full[c, s, chunk(i)] = gathered[p, chunk(i)]

        @pl.when(p != s)
        def _():
            copy(
                gathered.at[p, chunk(i)], full.at[c, s, chunk(i)], f_s.at[i, p], f_r.at[i, s], p, t
            ).start()

    def from_line(i):
        pass_on(i, z)
        for p in line:
            theirs = gathered.at[p, chunk(i)]
            copy(theirs, theirs, z_s.at[i, p], z_r.at[i, p], s, p * 2 + c).wait_recv()

            @pl.when(between(p))
            def _():
                block_on(i, p).start()

            pass_on(i, p)

    def swap(i, half):
        block = full.at[half, :, chunk(i)]
        return copy(block, block, swap_s.at[i], swap_r.at[i], s, sibling)

    def from_plane(i):
        for p in plane:
            theirs = full.at[c, p, chunk(i)]
            copy(theirs, theirs, f_s.at[i, p], f_r.at[i, p], p, t).wait_recv()
        swap(i, c).start()

    place_col = lax.broadcasted_iota(jnp.int32, (PLACES, 128), 0).astype(jnp.float32)
    angle = place_col * (freq[0:1, :] + freq[1:2, :] + freq[2:3, :])
    even_col = lax.broadcasted_iota(jnp.int32, (PLACES, 128), 1) % 2 == 0
    cos_all = jnp.cos(angle)
    sin_all = jnp.where(even_col, -1.0, 1.0) * jnp.sin(angle)
    for a in range(3):
        on_axis = freq[a : a + 1, :] > 0.0
        lookup[a * PLACES : (a + 1) * PLACES, :128] = jnp.where(on_axis, cos_all, 0.0)
        lookup[a * PLACES : (a + 1) * PLACES, 128:] = jnp.where(on_axis, sin_all, 0.0)

    def tables(j):
        block = meta_all[j]
        place = lax.broadcasted_iota(jnp.int32, (PLACES, rows), 0).astype(jnp.float32)
        where = [(block[a : a + 1] == place).astype(jnp.float32) for a in range(3)]
        found = dot00(jnp.concatenate(where, axis=0), lookup[...])
        cosine[:, j] = found[:, :128].reshape(chunks, cr, 128)
        sine[:, j] = found[:, 128:].reshape(chunks, cr, 128)
        seg = dot00(block, (pick == 3).astype(jnp.float32))
        same = seg == lane.astype(jnp.float32)
        q_mask = same.astype(jnp.float32).astype(jnp.bfloat16)
        k_mask = jnp.where(same | (lane >= 8), 0.0, FAR).astype(jnp.bfloat16)
        q_ext[:, j, :, 128:] = q_mask.reshape(chunks, cr, 128)
        k_ext[:, j, :, 128:] = k_mask.reshape(chunks, cr, 128)

    def first_of(i):
        return jnp.where(i % 2 == 0, x_next, y_next)

    def second_of(i):
        return jnp.where(i % 2 == 0, y_next, x_next)

    qk_bufs = (part, parts_in, relay, parts_last, p_s, p_r, last_s, last_r)
    v_bufs = (part_v, v_in, relay_v, v_last, pv_s, pv_r, lv_s, lv_r)

    def to_first(bufs, i, n, h):
        own, got, _, _, send, recv, _, _ = bufs
        return copy(own.at[i, h], got.at[i, n], send.at[i, n], recv.at[i, n], first_of(i), t)

    def to_second(bufs, i):
        _, _, passed, got, _, _, send, recv = bufs
        return copy(passed.at[i], got.at[i], send.at[i], recv.at[i], second_of(i), t)

    def project(bufs, fields, i):
        left = full[0, :, chunk(i)].reshape(many, feats)
        right = full[1, :, chunk(i)].reshape(many, feats)
        for at, n in enumerate(fields):
            acc = jnp.dot(left, w[n, :feats], preferred_element_type=jnp.float32)
            acc += jnp.dot(right, w[n, feats:], preferred_element_type=jnp.float32)
            for h in range(n_seq):
                bufs[0][i, h, :, at * 128 : (at + 1) * 128] = acc[
                    :, h * 128 : (h + 1) * 128
                ].astype(jnp.bfloat16)
        to_first(bufs, i, 1, corner).start()
        to_first(bufs, i, 0, first_of(i)).start()

    def project_qk(i):
        swap(i, 1 - c).wait_recv()
        project(qk_bufs, (0, 1), i)

    def project_v(i):
        project(v_bufs, (2,), i)

    def relay_on(bufs, i):
        own, got, passed = bufs[:3]
        to_first(bufs, i, 1, corner).wait_recv()
        passed[i] = (
            own[i, second_of(i)].astype(jnp.float32) + got[i, 1].astype(jnp.float32)
        ).astype(jnp.bfloat16)
        to_second(bufs, i).start()

    def summed_head(bufs, i):
        own, got, _, last = bufs[:4]
        to_first(bufs, i, 0, corner).wait_recv()
        to_second(bufs, i).wait_recv()
        total = own[i, s].astype(jnp.float32) + got[i, 0].astype(jnp.float32)
        return total + last[i].astype(jnp.float32)

    row_of = lax.broadcasted_iota(jnp.int32, (8, 256), 0)
    half_of = lax.broadcasted_iota(jnp.int32, (8, 256), 1) // 128
    st2[s] = jnp.zeros((8, rows), jnp.float32)

    def collect(i):
        total = summed_head(qk_bufs, i)
        qkv[i] = total
        st2[s] = st2[s] + dot11((row_of == 2 * i + half_of).astype(jnp.float32), total * total, EXACT)

    def collect_v(i, carry):
        v_all[i] = summed_head(v_bufs, i).astype(jnp.bfloat16).reshape(n_seq, cr, 128)
        return carry

    load_w.wait()
    load_w_out.wait()

    def during(step, at, work, first=0):
        @pl.when((step >= at + first) & (step < at + chunks))
        def _():
            work(step - at)

    def project_step(step, carry):
        during(step, 2, project_qk)
        during(step, 3, functools.partial(relay_on, qk_bufs))
        during(step, 1, from_plane)
        during(step, 4, project_v)
        during(step, 4, collect)
        during(step, 0, tables)
        during(step, 0, from_line)
        during(step, -AHEAD, along_z, AHEAD)
        return carry

    lax.fori_loop(0, chunks + 4, project_step, 0)

    for p in plane:
        copy(st2.at[s], st2.at[s], st2_s.at[p], st2_r.at[s], p, t).start()

    def relay_v_on(i, carry):
        relay_on(v_bufs, i)
        return carry

    gains = (q_gain[pl.ds(s, 1), :], k_gain[pl.ds(s, 1), :])

    def rotate(i, carry):
        cos_i = cosine[i].reshape(many, 128)
        sin_i = sine[i].reshape(many, 128)
        for n in range(2):
            cols = slice(n * 128, (n + 1) * 128)
            field = qkv[i, :, cols] * gains[n]
            swapped = jnp.where(even, pltpu.roll(field, 127, 1), pltpu.roll(field, 1, 1))
            qkv[i, :, cols] = field * cos_i + swapped * sin_i
        return carry

    lax.fori_loop(0, chunks, rotate, 0)
    lax.fori_loop(0, chunks - 1, relay_v_on, 0)
    for p in plane:
        copy(st2.at[p], st2.at[p], st2_s.at[p], st2_r.at[p], p, t).wait_recv()
    st3[t] = jnp.sum(st2[...], axis=0)
    for p in column:
        copy(st3.at[t], st3.at[t], st3_s.at[p], st3_r.at[t], s, p).start()

    def send_v(p):
        return copy(v_all.at[:, p], v_out.at[:, :, lanes_of(s)], v_s.at[p], v_r.at[s], p, t)

    def send_k(p):
        mine = k_ext.at[:, p, :, pl.ds(0, 128)]
        return copy(mine, k_out.at[:, :, lanes_of(s)], k_s.at[p], k_r.at[s], p, t)

    relay_v_on(chunks - 1, 0)
    for p in column:
        copy(st3.at[p], st3.at[p], st3_s.at[p], st3_r.at[p], s, p).wait_recv()
    norm_rows = lax.rsqrt(jnp.sum(st3[...], axis=0) / all_heads + EPSILON)

    lane_row = lax.broadcasted_iota(jnp.int32, (8, 128), 1)
    norm_cols = dot00(norm_rows, (pick == lane_row).astype(jnp.float32))
    for i in range(chunks):
        q_i = (qkv[i, :, :128] * norm_cols[:, 2 * i : 2 * i + 1]).astype(jnp.bfloat16)
        k_i = (qkv[i, :, 128:256] * norm_cols[:, 2 * i + 1 : 2 * i + 2]).astype(jnp.bfloat16)
        q_ext[i, :, :, :128] = q_i.reshape(n_seq, cr, 128)
        k_ext[i, :, :, :128] = k_i.reshape(n_seq, cr, 128)
        keys_t[:, i * many : (i + 1) * many] = k_ext[i].reshape(many, 256).T
    lax.fori_loop(0, chunks, collect_v, 0)
    for p in plane:
        send_v(p).start()
    v_out[:, :, lanes_of(s)] = v_all[:, s]

    score_scale = math.log2(math.e) / math.sqrt(HEAD_DIM)

    def attend(i):
        values = v_all[...].reshape(n_seq * rows, 128)
        scores = jnp.dot(
            q_ext[i].reshape(many, 256), keys_t[...], preferred_element_type=jnp.float32
        )
        top = jnp.max(scores, axis=1, keepdims=True)
        weights = jnp.exp2((scores - top) * score_scale)
        denominator = jnp.sum(weights, axis=1, keepdims=True)
        mixed = jnp.dot(weights.astype(jnp.bfloat16), values, preferred_element_type=jnp.float32)
        done = (mixed / denominator).astype(jnp.bfloat16)
        attn[i, :, :, lanes_of(s)] = done.reshape(n_seq, cr, 128)
        for p in plane:
            mine = attn.at[i, :, :, lanes_of(s)]
            copy(mine, mine, a_s.at[i, p], a_r.at[i, s], p, t).start()

    def pair(i):
        return copy(
            terms.at[i, 1 - c], pair_in.at[i], pair_s.at[i], pair_r.at[i], s, sibling
        )

    def out_project(i):
        for p in plane:
            theirs = attn.at[i, :, :, lanes_of(p)]
            copy(theirs, theirs, a_s.at[i, p], a_r.at[i, p], p, t).wait_recv()
        for n in range(2):
            cols = slice(n * feats, (n + 1) * feats)
            product = jnp.dot(
                attn[i].reshape(many, n_seq * 128), w_out[:, cols],
                preferred_element_type=jnp.float32,
            )
            terms[i, n] = product.astype(jnp.bfloat16).reshape(n_seq, cr, feats)
        pair(i).start()

    def pair_sum(i):
        pair(i).wait_recv()
        summed[i] = (terms[i, c].astype(jnp.float32) + pair_in[i].astype(jnp.float32)).astype(
            jnp.bfloat16
        )
        moved[s, i] = summed[i, s]
        for p in plane:
            copy(summed.at[i, p], moved.at[s, i], mv_s.at[i, p], mv_r.at[i, s], p, t).start()

    def to_line(i, p):
        return copy(
            moved.at[p, i], arrived.at[z, i], ar_s.at[i, p], ar_r.at[i, z], s, p * 2 + c
        )

    def to_joint(i, p):
        via = jnp.where(z == 0, 1, n_z - 2)
        return copy(moved.at[p, i], joint.at[i], ar_s.at[i, p], j_r.at[i], s, via * 2 + c)

    def deliver(i, p):
        @pl.when(p == z)
        def _():
            arrived[z, i] = moved[p, i]

        @pl.when(apart(p))
        def _():
            to_joint(i, p).start()
            arrived[p, i] = jnp.zeros((cr, feats), jnp.bfloat16)

        @pl.when((p != z) & jnp.logical_not(apart(p)) & jnp.logical_not(between(p)))
        def _():
            to_line(i, p).start()

    def join(i):
        @pl.when((z > 0) & (z < n_z - 1))
        def _():
            p = jnp.where(z == 1, n_z - 1, 0)
            to_joint(i, p).wait_recv()
            joined[i] = (
                moved[p, i].astype(jnp.float32) + joint[i].astype(jnp.float32)
            ).astype(jnp.bfloat16)
            copy(
                joined.at[i], arrived.at[z, i], ar_s.at[i, p], ar_r.at[i, z], s, p * 2 + c
            ).start()

    def deliver_all(i):
        deliver(i, s)
        for p in plane:
            theirs = moved.at[p, i]
            copy(theirs, theirs, mv_s.at[i, p], mv_r.at[i, p], p, t).wait_recv()
            deliver(i, p)

    def attend_step(step, carry):
        during(step, 4, join)
        during(step, 3, deliver_all)
        during(step, 2, pair_sum)

        @pl.when(step == chunks + 1)
        def _():
            for p in plane:
                send_k(p).start()

        during(step, 0, attend)
        during(step, 1, out_project)
        return carry

    lax.fori_loop(0, chunks + 4, attend_step, 0)
    k_out[:, :, lanes_of(s)] = k_ext[:, s, :, :128]

    for p in plane:
        copy(
            k_ext.at[:, p, :, pl.ds(0, 128)], k_out.at[:, :, lanes_of(p)], k_s.at[p], k_r.at[p], p, t
        ).wait()
        copy(v_all.at[:, p], v_out.at[:, :, lanes_of(p)], v_s.at[p], v_r.at[p], p, t).wait()
        copy(meta_all.at[s], meta_all.at[s], meta_s.at[p], meta_r.at[s], p, t).wait_send()
        copy(st2.at[s], st2.at[s], st2_s.at[p], st2_r.at[s], p, t).wait_send()
    for p in column:
        copy(st1.at[t], st1.at[t], st1_s.at[p], st1_r.at[t], s, p).wait_send()
        copy(st3.at[t], st3.at[t], st3_s.at[p], st3_r.at[t], s, p).wait_send()

    def drain(i, carry):
        swap(i, c).wait_send()
        pair(i).wait_send()
        for bufs in (qk_bufs, v_bufs):
            to_first(bufs, i, 0, first_of(i)).wait_send()
            to_first(bufs, i, 1, corner).wait_send()
            to_second(bufs, i).wait_send()
        for p in line:
            @pl.when(jnp.logical_not(apart(p)))
            def _():
                own_block(i, p).wait_send()

            @pl.when(between(p))
            def _():
                block_on(i, p).wait_send()

        for p in plane:
            copy(
                gathered.at[p, chunk(i)], full.at[c, s, chunk(i)], f_s.at[i, p], f_r.at[i, s], p, t
            ).wait_send()
            mine = attn.at[i, :, :, lanes_of(s)]
            copy(mine, mine, a_s.at[i, p], a_r.at[i, s], p, t).wait_send()
            copy(summed.at[i, p], moved.at[s, i], mv_s.at[i, p], mv_r.at[i, s], p, t).wait_send()
        return carry

    lax.fori_loop(0, chunks, drain, 0)

    def finish(i, carry):
        for p in line:
            theirs = arrived.at[p, i]

            @pl.when(jnp.logical_not(apart(p)))
            def _():
                copy(theirs, theirs, ar_s.at[i, p], ar_r.at[i, p], s, p * 2 + c).wait_recv()

        mixed = arrived[0, i].astype(jnp.float32)
        for p in range(1, n_z):
            mixed += arrived[p, i].astype(jnp.float32)
        base = hid[chunk(i), :].astype(jnp.float32)
        out[chunk(i), :] = (base + gate[chunk(i), :] * mixed).astype(jnp.bfloat16)
        return carry

    lax.fori_loop(0, chunks, finish, 0)

    def drain_line(i, carry):
        for p in line:
            to_line(i, p).wait_send()
        return carry

    lax.fori_loop(0, chunks, drain_line, 0)


def hand_over(*refs):
    for i in range(3):
        refs[3 + i][...] = refs[i][...]


def frequencies():
    part_width = HEAD_DIM // 6
    widths = (HEAD_DIM - 4 * part_width, 2 * part_width, 2 * part_width)
    table = np.zeros((8, HEAD_DIM), np.float32)
    at = 0
    for axis_number, wide in enumerate(widths):
        exponent = np.arange(0, wide, 2, dtype=np.float32) / np.float32(wide)
        frequency = (1.0 / np.float32(10000.0) ** exponent).astype(np.float32)
        table[axis_number, at : at + wide] = np.repeat(frequency, 2)
        at += wide
    return table


def fused_body(hidden_in, seg_ids, positions, mod_table, w_qkv, q_gain, k_gain, w_out):
    n_seq = lax.axis_size("seq")
    n_tp = lax.axis_size("tp")
    rows, feats = hidden_in.shape
    depth, _, heads_width = w_qkv.shape
    bf16, f32 = jnp.bfloat16, jnp.float32
    n_z = n_tp // 2
    chunks = CHUNKS
    cr = rows // chunks
    many = n_seq * cr
    dma = pltpu.SemaphoreType.DMA
    scratch = [
        pltpu.VMEM((3, depth, heads_width), bf16),
        pltpu.VMEM(w_out.shape, bf16),
        pltpu.VMEM((3, 8, feats), f32),
        pltpu.VMEM((n_seq, 8, rows), f32),
        pltpu.VMEM((n_tp, 8, rows), f32),
        pltpu.VMEM((n_z, rows, feats), bf16),
        pltpu.VMEM((2, n_seq, rows, feats), bf16),
        pltpu.VMEM((chunks, n_seq, many, 256), bf16),
        pltpu.VMEM((chunks, many, 256), bf16),
        pltpu.VMEM((chunks, 2, many, 256), bf16),
        pltpu.VMEM((chunks, many, 256), bf16),
        pltpu.VMEM((n_seq, 8, rows), f32),
        pltpu.VMEM((n_tp, 8, rows), f32),
        pltpu.VMEM((chunks, many, 256), f32),
        pltpu.VMEM((chunks, n_seq, cr, 128), f32),
        pltpu.VMEM((chunks, n_seq, cr, 128), f32),
        pltpu.VMEM((chunks, n_seq, cr, 256), bf16),
        pltpu.VMEM((chunks, n_seq, cr, 256), bf16),
        pltpu.VMEM((chunks, n_seq, cr, 128), bf16),
        pltpu.VMEM((chunks, n_seq, cr, heads_width), bf16),
        pltpu.VMEM((chunks, 2, n_seq, cr, feats), bf16),
        pltpu.VMEM((chunks, n_seq, cr, feats), bf16),
        pltpu.VMEM((chunks, n_seq, cr, feats), bf16),
        pltpu.VMEM((n_seq, chunks, cr, feats), bf16),
        pltpu.VMEM((n_z, chunks, cr, feats), bf16),
        pltpu.VMEM((chunks, cr, feats), bf16),
        pltpu.VMEM((chunks, cr, feats), bf16),
        pltpu.VMEM((chunks, n_seq, many, 128), bf16),
        pltpu.VMEM((chunks, many, 128), bf16),
        pltpu.VMEM((chunks, 2, many, 128), bf16),
        pltpu.VMEM((chunks, many, 128), bf16),
        pltpu.VMEM((3 * PLACES, 256), f32),
        pltpu.VMEM((256, chunks * many), bf16),
        pltpu.VMEM((rows, feats), f32),
        dma((2,)),
        dma((chunks,)),
        dma((chunks, 2)),
        dma((chunks, 2)),
        dma((chunks,)),
        dma((chunks,)),
    ]
    wide = (chunks, n_seq)
    shapes = [
        (n_seq,), (n_tp,), (chunks, n_z), wide, (chunks,), (chunks, 2), (chunks,),
        (n_seq,), (n_tp,), (n_seq,), (n_seq,), wide, (chunks,), wide, (chunks, n_z),
    ]
    for shape in shapes:
        scratch += [dma(shape), dma(shape)]
    vmem = pl.BlockSpec(memory_space=pltpu.VMEM)
    whole = pl.BlockSpec(memory_space=pl.ANY)
    results = pl.pallas_call(
        functools.partial(fused, n_seq, n_tp, feats * n_tp, heads_width * n_tp),
        out_shape=(
            jax.ShapeDtypeStruct((rows, feats), bf16),
            jax.ShapeDtypeStruct((chunks, cr, heads_width), bf16),
            jax.ShapeDtypeStruct((chunks, cr, heads_width), bf16),
        ),
        in_specs=[vmem, vmem, vmem, vmem, vmem, whole, vmem, vmem, whole],
        out_specs=(vmem, vmem, vmem),
        scratch_shapes=scratch,
        compiler_params=pltpu.CompilerParams(
            collective_id=0, has_side_effects=True, vmem_limit_bytes=58 * 1024 * 1024
        ),
        cost_estimate=pl.CostEstimate(
            flops=6_000_000_000, bytes_accessed=8_000_000, transcendentals=1_200_000
        ),
    )(
        hidden_in, seg_ids.reshape(1, rows), positions, mod_table.transpose(1, 0, 2),
        jnp.asarray(frequencies()), w_qkv.transpose(1, 0, 2),
        q_gain.reshape(n_seq, HEAD_DIM), k_gain.reshape(n_seq, HEAD_DIM), w_out,
    )
    hidden, k_cache, v_cache = pl.pallas_call(
        hand_over,
        out_shape=tuple(jax.ShapeDtypeStruct(r.shape, r.dtype) for r in results),
        in_specs=[vmem] * 3,
        out_specs=(vmem,) * 3,
        cost_estimate=pl.CostEstimate(flops=0, bytes_accessed=1_700_000, transcendentals=0),
    )(*results)
    return (
        hidden,
        k_cache.reshape(rows, heads_width),
        v_cache.reshape(rows, heads_width),
    )


def pick_body(*operands):
    hidden_in, seg_ids, positions, mod_table, w_qkv = operands[:5]
    n_seq, n_tp = lax.axis_size("seq"), lax.axis_size("tp")
    fits = (
        n_tp == 2 * n_seq
        and n_seq == 4
        and w_qkv.shape[2] == n_seq * HEAD_DIM
        and w_qkv.shape[0] == 2 * hidden_in.shape[1]
        and hidden_in.shape[0] == 256
        and mod_table.shape[0] <= 8
    )
    return (fused_body if fits else body)(*operands)


def solution(mesh):
    in_specs = (
        P("seq", "tp"),
        P("seq"),
        P(None, "seq"),
        P(None, None, "tp"),
        P("seq", None, "tp"),
        P("tp"),
        P("tp"),
        P("tp", "seq"),
    )
    out_specs = (P("seq", "tp"), P("seq", "tp"), P("seq", "tp"))
    return jax.shard_map(pick_body, mesh=mesh, in_specs=in_specs, out_specs=out_specs, check_vma=False)
```

```python
import functools
import math

import jax
import jax.numpy as jnp
import numpy as np
from jax import lax
from jax.experimental import pallas as pl
from jax.experimental.pallas import tpu as pltpu
from jax.sharding import PartitionSpec as P

HEAD_DIM = 128


EPSILON = 1e-06
NEG_FILL = -1e30


def rope_tables(positions):
    part_width = HEAD_DIM // 6
    widths = (HEAD_DIM - 4 * part_width, 2 * part_width, 2 * part_width)
    angle_list = []
    for axis_number in range(3):
        exponent = jnp.arange(0, widths[axis_number], 2, dtype=jnp.float32) / widths[axis_number]
        frequency = 1.0 / 10000.0**exponent
        angle_list.append(positions[axis_number].astype(jnp.float32)[:, None] * frequency[None, :])
    angle_all = jnp.concatenate(angle_list, axis=1)
    return (jnp.cos(angle_all), jnp.sin(angle_all))


def rotate_pairs(field, cosine, sine):
    even_part = field[..., 0::2]
    odd_part = field[..., 1::2]
    cos_wide = cosine[:, None, :]
    sin_wide = sine[:, None, :]
    new_even = even_part * cos_wide - odd_part * sin_wide
    new_odd = even_part * sin_wide + odd_part * cos_wide
    return jnp.stack([new_even, new_odd], axis=-1).reshape(field.shape)


def empty_state(query_rows, heads_here):
    maxima = jnp.full((heads_here, query_rows), NEG_FILL, jnp.float32)
    totals = jnp.zeros((heads_here, query_rows), jnp.float32)
    weighted = jnp.zeros((heads_here, query_rows, HEAD_DIM), jnp.float32)
    return (maxima, totals, weighted)


def merge_states(first, second):
    largest = jnp.maximum(first[0], second[0])
    first_factor = jnp.exp(first[0] - largest)
    second_factor = jnp.exp(second[0] - largest)
    totals = first[1] * first_factor + second[1] * second_factor
    weighted = first[2] * first_factor[..., None] + second[2] * second_factor[..., None]
    return (largest, totals, weighted)


def block_state(q_heads, seg_q, key_heads, value_heads, seg_k):
    score_scale = 1.0 / math.sqrt(HEAD_DIM)
    scores = (
        jnp.einsum("qhd,khd->hqk", q_heads, key_heads, preferred_element_type=jnp.float32)
        * score_scale
    )
    same_seg = seg_q[:, None] == seg_k[None, :]
    masked = jnp.where(same_seg[None], scores, NEG_FILL)
    maxima = jnp.max(masked, axis=2)
    weights = jnp.where(same_seg[None], jnp.exp(masked - maxima[..., None]), 0.0)
    totals = jnp.sum(weights, axis=2)
    weighted = jnp.einsum(
        "hqk,khd->hqd",
        weights.astype(jnp.bfloat16),
        value_heads,
        preferred_element_type=jnp.float32,
    )
    return (maxima, totals, weighted)


def absorb_keys(carry_state, q_heads, seg_q, key_rows, value_rows, seg_k):
    row_count = key_rows.shape[0]
    heads_here = q_heads.shape[1]
    block_rows = 512
    block_count = row_count // block_rows
    key_blocks = key_rows.reshape(block_count, block_rows, heads_here, HEAD_DIM)
    value_blocks = value_rows.reshape(block_count, block_rows, heads_here, HEAD_DIM)
    seg_blocks = seg_k.reshape(block_count, block_rows)

    def step_block(state_now, operands):
        key_block, value_block, seg_block = operands
        return (
            merge_states(state_now, block_state(q_heads, seg_q, key_block, value_block, seg_block)),
            None,
        )

    return lax.scan(step_block, carry_state, (key_blocks, value_blocks, seg_blocks))[0]


def body(hidden_in, seg_ids, positions, mod_table, w_qkv, q_gain, k_gain, w_out):
    tok_rows, feat_local = hidden_in.shape
    model_width = feat_local * lax.axis_size("tp")
    heads_width = w_qkv.shape[2]
    heads_here = heads_width // HEAD_DIM
    all_heads_width = heads_width * lax.axis_size("tp")
    x_float = hidden_in.astype(jnp.float32)
    row_sums, row_squares = lax.psum(
        (jnp.sum(x_float, axis=1), jnp.sum(x_float * x_float, axis=1)), "tp"
    )
    mean_value = row_sums / model_width
    variance = row_squares / model_width - mean_value * mean_value
    normed = (x_float - mean_value[:, None]) * lax.rsqrt(variance[:, None] + EPSILON)
    segment_count = mod_table.shape[0]
    table = mod_table.reshape(segment_count, 3 * feat_local)
    onehot = (seg_ids[:, None] == jnp.arange(segment_count, dtype=jnp.int32)[None, :]).astype(
        jnp.float32
    )
    modulation = jnp.dot(onehot, table, precision=lax.Precision.HIGHEST).reshape(
        tok_rows, 3, feat_local
    )
    modded = (normed * (1.0 + modulation[:, 1]) + modulation[:, 0]).astype(jnp.bfloat16)
    full_rows = lax.all_gather(modded, "tp", axis=1, tiled=True)
    portion = lax.all_gather(w_qkv, "seq", axis=0, tiled=True)
    flat = portion.reshape(portion.shape[0], 3 * heads_width)
    projected = jnp.dot(full_rows, flat, preferred_element_type=jnp.float32)
    query_f = projected[:, :heads_width]
    key_f = projected[:, heads_width : 2 * heads_width]
    value_f = projected[:, 2 * heads_width :]
    query_sq, key_sq = lax.psum(
        (jnp.sum(query_f * query_f, axis=1), jnp.sum(key_f * key_f, axis=1)), "tp"
    )
    query_n = query_f * lax.rsqrt(query_sq / all_heads_width + EPSILON)[:, None] * q_gain[None, :]
    key_n = key_f * lax.rsqrt(key_sq / all_heads_width + EPSILON)[:, None] * k_gain[None, :]
    cosine, sine = rope_tables(positions)
    q_heads = rotate_pairs(query_n.reshape(tok_rows, heads_here, HEAD_DIM), cosine, sine).astype(
        jnp.bfloat16
    )
    k_heads = rotate_pairs(key_n.reshape(tok_rows, heads_here, HEAD_DIM), cosine, sine).astype(
        jnp.bfloat16
    )
    k_cache = k_heads.reshape(tok_rows, heads_width)
    v_cache = value_f.astype(jnp.bfloat16)
    key_rows = lax.all_gather(k_cache, "seq", axis=0, tiled=True)
    value_rows = lax.all_gather(v_cache, "seq", axis=0, tiled=True)
    seg_k = lax.all_gather(seg_ids, "seq", axis=0, tiled=True)
    state_end = absorb_keys(
        empty_state(tok_rows, heads_here), q_heads, seg_ids, key_rows, value_rows, seg_k
    )
    attention = (state_end[2] / state_end[1][..., None]).transpose(1, 0, 2)
    attn_out = attention.reshape(tok_rows, heads_width).astype(jnp.bfloat16)
    terms = jnp.dot(
        attn_out,
        lax.all_gather(w_out, "seq", axis=1, tiled=True),
        preferred_element_type=jnp.float32,
    )
    mixed = lax.psum_scatter(
        terms.astype(jnp.bfloat16), "tp", scatter_dimension=1, tiled=True
    ).astype(jnp.float32)
    hidden_out = (x_float + modulation[:, 2] * mixed).astype(jnp.bfloat16)
    return (hidden_out, k_cache, v_cache)


MESH = pl.DeviceIdType.MESH
EXACT = lax.Precision.HIGHEST
FAR = -1e30
CHUNKS = 4
AHEAD = 2
PLACES = 64


def dot00(a, b):
    return lax.dot_general(
        a, b, (((0,), (0,)), ((), ())), precision=EXACT, preferred_element_type=jnp.float32
    )


def dot11(a, b, precision=None):
    return lax.dot_general(
        a, b, (((1,), (1,)), ((), ())), precision=precision, preferred_element_type=jnp.float32
    )


def fused(
    n_seq, n_tp, width, all_heads,
    hid, segs, positions, modt, freq, w_any, q_gain, k_gain, w_out_any,
    out, k_out, v_out,
    w, w_out, mod8, meta_all, st1, gathered, full, part, relay, parts_in, parts_last,
    st2, st3, qkv, cosine, sine, q_ext, k_ext, v_all, attn, terms, pair_in, summed, moved,
    arrived, joint, joined, part_v, relay_v, v_in, v_last, lookup, keys_t, gate,
    w_sem, j_r, pv_s, pv_r, lv_s, lv_r, meta_s, meta_r, st1_s, st1_r, z_s, z_r, f_s, f_r, swap_s, swap_r, p_s, p_r,
    last_s, last_r, st2_s, st2_r, st3_s, st3_r, k_s, k_r, v_s, v_r, a_s, a_r, pair_s, pair_r,
    mv_s, mv_r, ar_s, ar_r,
):
    s = lax.axis_index("seq")
    t = lax.axis_index("tp")
    z = t // 2
    c = t % 2
    rows, feats = hid.shape
    n_z = n_tp // 2
    chunks = CHUNKS
    cr = rows // chunks
    many = n_seq * cr
    sibling = z * 2 + 1 - c
    x_next = (s // 2) * 2 + 1 - s % 2
    y_next = (1 - s // 2) * 2 + s % 2
    corner = (1 - s // 2) * 2 + 1 - s % 2

    def copy(src, dst, send, recv, to_s, to_t):
        return pltpu.make_async_remote_copy(
            src_ref=src, dst_ref=dst, send_sem=send, recv_sem=recv,
            device_id=(to_s, to_t), device_id_type=MESH,
        )

    def chunk(i):
        return pl.ds(pl.multiple_of(i * cr, cr), cr)

    def lanes_of(h):
        return pl.ds(pl.multiple_of(h * 128, 128), 128)

    plane = [(s + d) % n_seq for d in range(1, n_seq)]
    column = [(t + d) % n_tp for d in range(1, n_tp)]
    line = [(z + jnp.where(z < n_z // 2, d, n_z - d)) % n_z for d in range(1, n_z)]

    def apart(p):
        return (p + z == n_z - 1) & (p * z == 0)

    def between(p):
        return ((z == n_z - 2) & (p == 0)) | ((z == 1) & (p == n_z - 1))

    barrier = pltpu.get_barrier_semaphore()
    for p in plane:
        pl.semaphore_signal(barrier, inc=1, device_id=(p, t), device_id_type=MESH)
    for p in column:
        pl.semaphore_signal(barrier, inc=1, device_id=(s, p), device_id_type=MESH)
    load_w = pltpu.make_async_copy(w_any, w, w_sem.at[0])
    load_w_out = pltpu.make_async_copy(w_out_any, w_out, w_sem.at[1])
    load_w.start()
    load_w_out.start()

    x = hid[...].astype(jnp.float32)
    row8 = lax.broadcasted_iota(jnp.int32, (8, rows), 0)
    ones_b = jnp.ones((8, feats), jnp.bfloat16)
    ones_f = jnp.ones((8, feats), jnp.float32)
    st1[t] = jnp.where(row8 == 0, dot11(ones_b, hid[...]), dot11(ones_f, x * x, EXACT))
    meta_all[s] = jnp.zeros((8, rows), jnp.float32)
    meta_all[s, 0:3] = positions[...].astype(jnp.float32)
    meta_all[s, 3:4] = segs[...].astype(jnp.float32)
    pl.semaphore_wait(barrier, n_seq - 1 + n_tp - 1)
    for p in column:
        copy(st1.at[t], st1.at[t], st1_s.at[p], st1_r.at[t], s, p).start()
    for p in plane:
        copy(meta_all.at[s], meta_all.at[s], meta_s.at[p], meta_r.at[s], p, t).start()

    row32 = lax.broadcasted_iota(jnp.int32, (32, rows), 0)
    onehot = ((segs[...] == row32 % 8) & (row32 < 24)).astype(jnp.float32).astype(jnp.bfloat16)
    mod8[...] = jnp.zeros(mod8.shape, jnp.float32)
    mod8[:, : modt.shape[1]] = modt[...]

    def modulation(n):
        whole = mod8[n]
        high = whole.astype(jnp.bfloat16).astype(jnp.float32)
        middle = (whole - high).astype(jnp.bfloat16).astype(jnp.float32)
        low = whole - high - middle
        parts = jnp.concatenate([high, middle, low, jnp.zeros_like(low)], axis=0)
        return lax.dot_general(
            onehot, parts.astype(jnp.bfloat16), (((0,), (0,)), ((), ())),
            preferred_element_type=jnp.float32,
        )

    shift = modulation(0)
    scale = modulation(1)
    gate[...] = modulation(2)

    for p in column:
        copy(st1.at[p], st1.at[p], st1_s.at[p], st1_r.at[p], s, p).wait_recv()
    totals = jnp.sum(st1[...], axis=0)
    mean_row = totals[0:1] / width
    scale_row = lax.rsqrt(totals[1:2] / width - mean_row * mean_row + EPSILON)
    both = jnp.where(row8 == 0, mean_row, jnp.where(row8 == 1, scale_row, 0.0))
    pick = lax.broadcasted_iota(jnp.int32, (8, 128), 0)
    mean_col = dot00(both, (pick == 0).astype(jnp.float32))[:, 0:1]
    scale_col = dot00(both, (pick == 1).astype(jnp.float32))[:, 0:1]
    normed = (x - mean_col) * scale_col
    gathered[z] = (normed * (1.0 + scale) + shift).astype(jnp.bfloat16)

    def own_block(i, p):
        mine = gathered.at[z, chunk(i)]
        return copy(mine, mine, z_s.at[i, p], z_r.at[i, z], s, p * 2 + c)

    def block_on(i, p):
        theirs = gathered.at[p, chunk(i)]
        return copy(theirs, theirs, z_s.at[i, z], z_r.at[i, p], s, (n_z - 1 - p) * 2 + c)

    def along_z(i):
        for p in line:
            @pl.when(jnp.logical_not(apart(p)))
            def _():
                own_block(i, p).start()

    for i in range(AHEAD):
        along_z(i)
    for p in plane:
        copy(meta_all.at[p], meta_all.at[p], meta_s.at[p], meta_r.at[p], p, t).wait_recv()
    lane = lax.broadcasted_iota(jnp.int32, (rows, 128), 1)
    even = lane % 2 == 0

    def pass_on(i, p):
        @pl.when(p == s)
        def _():
            full[c, s, chunk(i)] = gathered[p, chunk(i)]

        @pl.when(p != s)
        def _():
            copy(
                gathered.at[p, chunk(i)], full.at[c, s, chunk(i)], f_s.at[i, p], f_r.at[i, s], p, t
            ).start()

    def from_line(i):
        pass_on(i, z)
        for p in line:
            theirs = gathered.at[p, chunk(i)]
            copy(theirs, theirs, z_s.at[i, p], z_r.at[i, p], s, p * 2 + c).wait_recv()

            @pl.when(between(p))
            def _():
                block_on(i, p).start()

            pass_on(i, p)

    def swap(i, half):
        block = full.at[half, :, chunk(i)]
        return copy(block, block, swap_s.at[i], swap_r.at[i], s, sibling)

    def from_plane(i):
        for p in plane:
            theirs = full.at[c, p, chunk(i)]
            copy(theirs, theirs, f_s.at[i, p], f_r.at[i, p], p, t).wait_recv()
        swap(i, c).start()

    place_col = lax.broadcasted_iota(jnp.int32, (PLACES, 128), 0).astype(jnp.float32)
    angle = place_col * (freq[0:1, :] + freq[1:2, :] + freq[2:3, :])
    even_col = lax.broadcasted_iota(jnp.int32, (PLACES, 128), 1) % 2 == 0
    cos_all = jnp.cos(angle)
    sin_all = jnp.where(even_col, -1.0, 1.0) * jnp.sin(angle)
    for a in range(3):
        on_axis = freq[a : a + 1, :] > 0.0
        lookup[a * PLACES : (a + 1) * PLACES, :128] = jnp.where(on_axis, cos_all, 0.0)
        lookup[a * PLACES : (a + 1) * PLACES, 128:] = jnp.where(on_axis, sin_all, 0.0)

    def tables(j):
        block = meta_all[j]
        place = lax.broadcasted_iota(jnp.int32, (PLACES, rows), 0).astype(jnp.float32)
        where = [(block[a : a + 1] == place).astype(jnp.float32) for a in range(3)]
        found = dot00(jnp.concatenate(where, axis=0), lookup[...])
        cosine[:, j] = found[:, :128].reshape(chunks, cr, 128)
        sine[:, j] = found[:, 128:].reshape(chunks, cr, 128)
        seg = dot00(block, (pick == 3).astype(jnp.float32))
        same = seg == lane.astype(jnp.float32)
        q_mask = same.astype(jnp.float32).astype(jnp.bfloat16)
        k_mask = jnp.where(same | (lane >= 8), 0.0, FAR).astype(jnp.bfloat16)
        q_ext[:, j, :, 128:] = q_mask.reshape(chunks, cr, 128)
        k_ext[:, j, :, 128:] = k_mask.reshape(chunks, cr, 128)

    def first_of(i):
        return jnp.where(i % 2 == 0, x_next, y_next)

    def second_of(i):
        return jnp.where(i % 2 == 0, y_next, x_next)

    qk_bufs = (part, parts_in, relay, parts_last, p_s, p_r, last_s, last_r)
    v_bufs = (part_v, v_in, relay_v, v_last, pv_s, pv_r, lv_s, lv_r)

    def to_first(bufs, i, n, h):
        own, got, _, _, send, recv, _, _ = bufs
        return copy(own.at[i, h], got.at[i, n], send.at[i, n], recv.at[i, n], first_of(i), t)

    def to_second(bufs, i):
        _, _, passed, got, _, _, send, recv = bufs
        return copy(passed.at[i], got.at[i], send.at[i], recv.at[i], second_of(i), t)

    def project(bufs, fields, i):
        left = full[0, :, chunk(i)].reshape(many, feats)
        right = full[1, :, chunk(i)].reshape(many, feats)
        for at, n in enumerate(fields):
            acc = jnp.dot(left, w[n, :feats], preferred_element_type=jnp.float32)
            acc += jnp.dot(right, w[n, feats:], preferred_element_type=jnp.float32)
            for h in range(n_seq):
                bufs[0][i, h, :, at * 128 : (at + 1) * 128] = acc[
                    :, h * 128 : (h + 1) * 128
                ].astype(jnp.bfloat16)
        to_first(bufs, i, 1, corner).start()
        to_first(bufs, i, 0, first_of(i)).start()

    def project_qk(i):
        swap(i, 1 - c).wait_recv()
        project(qk_bufs, (0, 1), i)

    def project_v(i):
        project(v_bufs, (2,), i)

    def relay_on(bufs, i):
        own, got, passed = bufs[:3]
        to_first(bufs, i, 1, corner).wait_recv()
        passed[i] = (
            own[i, second_of(i)].astype(jnp.float32) + got[i, 1].astype(jnp.float32)
        ).astype(jnp.bfloat16)
        to_second(bufs, i).start()

    def summed_head(bufs, i):
        own, got, _, last = bufs[:4]
        to_first(bufs, i, 0, corner).wait_recv()
        to_second(bufs, i).wait_recv()
        total = own[i, s].astype(jnp.float32) + got[i, 0].astype(jnp.float32)
        return total + last[i].astype(jnp.float32)

    row_of = lax.broadcasted_iota(jnp.int32, (8, 256), 0)
    half_of = lax.broadcasted_iota(jnp.int32, (8, 256), 1) // 128
    st2[s] = jnp.zeros((8, rows), jnp.float32)

    def collect(i):
        total = summed_head(qk_bufs, i)
        qkv[i] = total
        st2[s] = st2[s] + dot11((row_of == 2 * i + half_of).astype(jnp.float32), total * total, EXACT)

    def collect_v(i, carry):
        v_all[i] = summed_head(v_bufs, i).astype(jnp.bfloat16).reshape(n_seq, cr, 128)
        return carry

    load_w.wait()
    load_w_out.wait()

    def during(step, at, work, first=0):
        @pl.when((step >= at + first) & (step < at + chunks))
        def _():
            work(step - at)

    def project_step(step, carry):
        during(step, 2, project_qk)
        during(step, 3, functools.partial(relay_on, qk_bufs))
        during(step, 1, from_plane)
        for i in range(chunks):
            @pl.when(step == chunks + 2 + 2 * i // chunks)
            def _():
                project_v(i)

        during(step, 4, collect)
        during(step, 0, tables)
        during(step, 0, from_line)
        during(step, -AHEAD, along_z, AHEAD)
        return carry

    lax.fori_loop(0, chunks + 4, project_step, 0)

    for p in plane:
        copy(st2.at[s], st2.at[s], st2_s.at[p], st2_r.at[s], p, t).start()

    def relay_v_on(i, carry):
        relay_on(v_bufs, i)
        return carry

    gains = (q_gain[pl.ds(s, 1), :], k_gain[pl.ds(s, 1), :])

    def rotate(i, carry):
        cos_i = cosine[i].reshape(many, 128)
        sin_i = sine[i].reshape(many, 128)
        for n in range(2):
            cols = slice(n * 128, (n + 1) * 128)
            field = qkv[i, :, cols] * gains[n]
            swapped = jnp.where(even, pltpu.roll(field, 127, 1), pltpu.roll(field, 1, 1))
            qkv[i, :, cols] = field * cos_i + swapped * sin_i
        return carry

    lax.fori_loop(0, chunks, rotate, 0)
    lax.fori_loop(0, chunks - 1, relay_v_on, 0)
    for p in plane:
        copy(st2.at[p], st2.at[p], st2_s.at[p], st2_r.at[p], p, t).wait_recv()
    st3[t] = jnp.sum(st2[...], axis=0)
    for p in column:
        copy(st3.at[t], st3.at[t], st3_s.at[p], st3_r.at[t], s, p).start()

    def send_v(p):
        return copy(v_all.at[:, p], v_out.at[:, :, lanes_of(s)], v_s.at[p], v_r.at[s], p, t)

    def send_k(p):
        mine = k_ext.at[:, p, :, pl.ds(0, 128)]
        return copy(mine, k_out.at[:, :, lanes_of(s)], k_s.at[p], k_r.at[s], p, t)

    relay_v_on(chunks - 1, 0)
    for p in column:
        copy(st3.at[p], st3.at[p], st3_s.at[p], st3_r.at[p], s, p).wait_recv()
    norm_rows = lax.rsqrt(jnp.sum(st3[...], axis=0) / all_heads + EPSILON)

    lane_row = lax.broadcasted_iota(jnp.int32, (8, 128), 1)
    norm_cols = dot00(norm_rows, (pick == lane_row).astype(jnp.float32))
    for i in range(chunks):
        q_i = (qkv[i, :, :128] * norm_cols[:, 2 * i : 2 * i + 1]).astype(jnp.bfloat16)
        k_i = (qkv[i, :, 128:256] * norm_cols[:, 2 * i + 1 : 2 * i + 2]).astype(jnp.bfloat16)
        q_ext[i, :, :, :128] = q_i.reshape(n_seq, cr, 128)
        k_ext[i, :, :, :128] = k_i.reshape(n_seq, cr, 128)
        keys_t[:, i * many : (i + 1) * many] = k_ext[i].reshape(many, 256).T
    lax.fori_loop(0, chunks, collect_v, 0)
    for p in plane:
        send_v(p).start()
    v_out[:, :, lanes_of(s)] = v_all[:, s]

    score_scale = math.log2(math.e) / math.sqrt(HEAD_DIM)

    def attend(i):
        values = v_all[...].reshape(n_seq * rows, 128)
        scores = jnp.dot(
            q_ext[i].reshape(many, 256), keys_t[...], preferred_element_type=jnp.float32
        )
        top = jnp.max(scores, axis=1, keepdims=True)
        weights = jnp.exp2((scores - top) * score_scale)
        denominator = jnp.sum(weights, axis=1, keepdims=True)
        mixed = jnp.dot(weights.astype(jnp.bfloat16), values, preferred_element_type=jnp.float32)
        done = (mixed / denominator).astype(jnp.bfloat16)
        attn[i, :, :, lanes_of(s)] = done.reshape(n_seq, cr, 128)
        for p in plane:
            mine = attn.at[i, :, :, lanes_of(s)]
            copy(mine, mine, a_s.at[i, p], a_r.at[i, s], p, t).start()

    def pair(i):
        return copy(
            terms.at[i, 1 - c], pair_in.at[i], pair_s.at[i], pair_r.at[i], s, sibling
        )

    def out_project(i):
        for p in plane:
            theirs = attn.at[i, :, :, lanes_of(p)]
            copy(theirs, theirs, a_s.at[i, p], a_r.at[i, p], p, t).wait_recv()
        for n in range(2):
            cols = slice(n * feats, (n + 1) * feats)
            product = jnp.dot(
                attn[i].reshape(many, n_seq * 128), w_out[:, cols],
                preferred_element_type=jnp.float32,
            )
            terms[i, n] = product.astype(jnp.bfloat16).reshape(n_seq, cr, feats)
        pair(i).start()

    def pair_sum(i):
        pair(i).wait_recv()
        summed[i] = (terms[i, c].astype(jnp.float32) + pair_in[i].astype(jnp.float32)).astype(
            jnp.bfloat16
        )
        moved[s, i] = summed[i, s]
        for p in plane:
            copy(summed.at[i, p], moved.at[s, i], mv_s.at[i, p], mv_r.at[i, s], p, t).start()

    def to_line(i, p):
        return copy(
            moved.at[p, i], arrived.at[z, i], ar_s.at[i, p], ar_r.at[i, z], s, p * 2 + c
        )

    def to_joint(i, p):
        via = jnp.where(z == 0, 1, n_z - 2)
        return copy(moved.at[p, i], joint.at[i], ar_s.at[i, p], j_r.at[i], s, via * 2 + c)

    def deliver(i, p):
        @pl.when(p == z)
        def _():
            arrived[z, i] = moved[p, i]

        @pl.when(apart(p))
        def _():
            to_joint(i, p).start()
            arrived[p, i] = jnp.zeros((cr, feats), jnp.bfloat16)

        @pl.when((p != z) & jnp.logical_not(apart(p)) & jnp.logical_not(between(p)))
        def _():
            to_line(i, p).start()

    def join(i):
        @pl.when((z > 0) & (z < n_z - 1))
        def _():
            p = jnp.where(z == 1, n_z - 1, 0)
            to_joint(i, p).wait_recv()
            joined[i] = (
                moved[p, i].astype(jnp.float32) + joint[i].astype(jnp.float32)
            ).astype(jnp.bfloat16)
            copy(
                joined.at[i], arrived.at[z, i], ar_s.at[i, p], ar_r.at[i, z], s, p * 2 + c
            ).start()

    def deliver_all(i):
        deliver(i, s)
        for p in plane:
            theirs = moved.at[p, i]
            copy(theirs, theirs, mv_s.at[i, p], mv_r.at[i, p], p, t).wait_recv()
            deliver(i, p)

    def attend_step(step, carry):
        during(step, 4, join)
        during(step, 3, deliver_all)
        during(step, 0, attend)
        during(step, 2, pair_sum)

        @pl.when(step == chunks + 1)
        def _():
            for p in plane:
                send_k(p).start()

        during(step, 1, out_project)
        return carry

    lax.fori_loop(0, chunks + 4, attend_step, 0)
    k_out[:, :, lanes_of(s)] = k_ext[:, s, :, :128]

    for p in plane:
        copy(
            k_ext.at[:, p, :, pl.ds(0, 128)], k_out.at[:, :, lanes_of(p)], k_s.at[p], k_r.at[p], p, t
        ).wait()
        copy(v_all.at[:, p], v_out.at[:, :, lanes_of(p)], v_s.at[p], v_r.at[p], p, t).wait()
        copy(meta_all.at[s], meta_all.at[s], meta_s.at[p], meta_r.at[s], p, t).wait_send()
        copy(st2.at[s], st2.at[s], st2_s.at[p], st2_r.at[s], p, t).wait_send()
    for p in column:
        copy(st1.at[t], st1.at[t], st1_s.at[p], st1_r.at[t], s, p).wait_send()
        copy(st3.at[t], st3.at[t], st3_s.at[p], st3_r.at[t], s, p).wait_send()

    def drain(i, carry):
        swap(i, c).wait_send()
        pair(i).wait_send()
        for bufs in (qk_bufs, v_bufs):
            to_first(bufs, i, 0, first_of(i)).wait_send()
            to_first(bufs, i, 1, corner).wait_send()
            to_second(bufs, i).wait_send()
        for p in line:
            @pl.when(jnp.logical_not(apart(p)))
            def _():
                own_block(i, p).wait_send()

            @pl.when(between(p))
            def _():
                block_on(i, p).wait_send()

        for p in plane:
            copy(
                gathered.at[p, chunk(i)], full.at[c, s, chunk(i)], f_s.at[i, p], f_r.at[i, s], p, t
            ).wait_send()
            mine = attn.at[i, :, :, lanes_of(s)]
            copy(mine, mine, a_s.at[i, p], a_r.at[i, s], p, t).wait_send()
            copy(summed.at[i, p], moved.at[s, i], mv_s.at[i, p], mv_r.at[i, s], p, t).wait_send()
        return carry

    lax.fori_loop(0, chunks, drain, 0)

    def finish(i, carry):
        for p in line:
            theirs = arrived.at[p, i]

            @pl.when(jnp.logical_not(apart(p)))
            def _():
                copy(theirs, theirs, ar_s.at[i, p], ar_r.at[i, p], s, p * 2 + c).wait_recv()

        mixed = arrived[0, i].astype(jnp.float32)
        for p in range(1, n_z):
            mixed += arrived[p, i].astype(jnp.float32)
        base = hid[chunk(i), :].astype(jnp.float32)
        out[chunk(i), :] = (base + gate[chunk(i), :] * mixed).astype(jnp.bfloat16)
        return carry

    lax.fori_loop(0, chunks, finish, 0)

    def drain_line(i, carry):
        for p in line:
            to_line(i, p).wait_send()
        return carry

    lax.fori_loop(0, chunks, drain_line, 0)


def hand_over(*refs):
    for i in range(3):
        refs[3 + i][...] = refs[i][...]


def frequencies():
    part_width = HEAD_DIM // 6
    widths = (HEAD_DIM - 4 * part_width, 2 * part_width, 2 * part_width)
    table = np.zeros((8, HEAD_DIM), np.float32)
    at = 0
    for axis_number, wide in enumerate(widths):
        exponent = np.arange(0, wide, 2, dtype=np.float32) / np.float32(wide)
        frequency = (1.0 / np.float32(10000.0) ** exponent).astype(np.float32)
        table[axis_number, at : at + wide] = np.repeat(frequency, 2)
        at += wide
    return table


def fused_body(hidden_in, seg_ids, positions, mod_table, w_qkv, q_gain, k_gain, w_out):
    n_seq = lax.axis_size("seq")
    n_tp = lax.axis_size("tp")
    rows, feats = hidden_in.shape
    depth, _, heads_width = w_qkv.shape
    bf16, f32 = jnp.bfloat16, jnp.float32
    n_z = n_tp // 2
    chunks = CHUNKS
    cr = rows // chunks
    many = n_seq * cr
    dma = pltpu.SemaphoreType.DMA
    scratch = [
        pltpu.VMEM((3, depth, heads_width), bf16),
        pltpu.VMEM(w_out.shape, bf16),
        pltpu.VMEM((3, 8, feats), f32),
        pltpu.VMEM((n_seq, 8, rows), f32),
        pltpu.VMEM((n_tp, 8, rows), f32),
        pltpu.VMEM((n_z, rows, feats), bf16),
        pltpu.VMEM((2, n_seq, rows, feats), bf16),
        pltpu.VMEM((chunks, n_seq, many, 256), bf16),
        pltpu.VMEM((chunks, many, 256), bf16),
        pltpu.VMEM((chunks, 2, many, 256), bf16),
        pltpu.VMEM((chunks, many, 256), bf16),
        pltpu.VMEM((n_seq, 8, rows), f32),
        pltpu.VMEM((n_tp, 8, rows), f32),
        pltpu.VMEM((chunks, many, 256), f32),
        pltpu.VMEM((chunks, n_seq, cr, 128), f32),
        pltpu.VMEM((chunks, n_seq, cr, 128), f32),
        pltpu.VMEM((chunks, n_seq, cr, 256), bf16),
        pltpu.VMEM((chunks, n_seq, cr, 256), bf16),
        pltpu.VMEM((chunks, n_seq, cr, 128), bf16),
        pltpu.VMEM((chunks, n_seq, cr, heads_width), bf16),
        pltpu.VMEM((chunks, 2, n_seq, cr, feats), bf16),
        pltpu.VMEM((chunks, n_seq, cr, feats), bf16),
        pltpu.VMEM((chunks, n_seq, cr, feats), bf16),
        pltpu.VMEM((n_seq, chunks, cr, feats), bf16),
        pltpu.VMEM((n_z, chunks, cr, feats), bf16),
        pltpu.VMEM((chunks, cr, feats), bf16),
        pltpu.VMEM((chunks, cr, feats), bf16),
        pltpu.VMEM((chunks, n_seq, many, 128), bf16),
        pltpu.VMEM((chunks, many, 128), bf16),
        pltpu.VMEM((chunks, 2, many, 128), bf16),
        pltpu.VMEM((chunks, many, 128), bf16),
        pltpu.VMEM((3 * PLACES, 256), f32),
        pltpu.VMEM((256, chunks * many), bf16),
        pltpu.VMEM((rows, feats), f32),
        dma((2,)),
        dma((chunks,)),
        dma((chunks, 2)),
        dma((chunks, 2)),
        dma((chunks,)),
        dma((chunks,)),
    ]
    wide = (chunks, n_seq)
    shapes = [
        (n_seq,), (n_tp,), (chunks, n_z), wide, (chunks,), (chunks, 2), (chunks,),
        (n_seq,), (n_tp,), (n_seq,), (n_seq,), wide, (chunks,), wide, (chunks, n_z),
    ]
    for shape in shapes:
        scratch += [dma(shape), dma(shape)]
    vmem = pl.BlockSpec(memory_space=pltpu.VMEM)
    whole = pl.BlockSpec(memory_space=pl.ANY)
    results = pl.pallas_call(
        functools.partial(fused, n_seq, n_tp, feats * n_tp, heads_width * n_tp),
        out_shape=(
            jax.ShapeDtypeStruct((rows, feats), bf16),
            jax.ShapeDtypeStruct((chunks, cr, heads_width), bf16),
            jax.ShapeDtypeStruct((chunks, cr, heads_width), bf16),
        ),
        in_specs=[vmem, vmem, vmem, vmem, vmem, whole, vmem, vmem, whole],
        out_specs=(vmem, vmem, vmem),
        scratch_shapes=scratch,
        compiler_params=pltpu.CompilerParams(
            collective_id=0, has_side_effects=True, vmem_limit_bytes=58 * 1024 * 1024
        ),
        cost_estimate=pl.CostEstimate(
            flops=6_000_000_000, bytes_accessed=8_000_000, transcendentals=1_200_000
        ),
    )(
        hidden_in, seg_ids.reshape(1, rows), positions, mod_table.transpose(1, 0, 2),
        jnp.asarray(frequencies()), w_qkv.transpose(1, 0, 2),
        q_gain.reshape(n_seq, HEAD_DIM), k_gain.reshape(n_seq, HEAD_DIM), w_out,
    )
    hidden, k_cache, v_cache = pl.pallas_call(
        hand_over,
        out_shape=tuple(jax.ShapeDtypeStruct(r.shape, r.dtype) for r in results),
        in_specs=[vmem] * 3,
        out_specs=(vmem,) * 3,
        cost_estimate=pl.CostEstimate(flops=0, bytes_accessed=1_700_000, transcendentals=0),
    )(*results)
    return (
        hidden,
        k_cache.reshape(rows, heads_width),
        v_cache.reshape(rows, heads_width),
    )


def pick_body(*operands):
    hidden_in, seg_ids, positions, mod_table, w_qkv = operands[:5]
    n_seq, n_tp = lax.axis_size("seq"), lax.axis_size("tp")
    fits = (
        n_tp == 2 * n_seq
        and n_seq == 4
        and w_qkv.shape[2] == n_seq * HEAD_DIM
        and w_qkv.shape[0] == 2 * hidden_in.shape[1]
        and hidden_in.shape[0] == 256
        and mod_table.shape[0] <= 8
    )
    return (fused_body if fits else body)(*operands)


def solution(mesh):
    in_specs = (
        P("seq", "tp"),
        P("seq"),
        P(None, "seq"),
        P(None, None, "tp"),
        P("seq", None, "tp"),
        P("tp"),
        P("tp"),
        P("tp", "seq"),
    )
    out_specs = (P("seq", "tp"), P("seq", "tp"), P("seq", "tp"))
    return jax.shard_map(pick_body, mesh=mesh, in_specs=in_specs, out_specs=out_specs, check_vma=False)
```
